128 devices in a mesh: lon: 16 (over y_hi, x, core), ch: 8 (over y_lo, z).
Axes of the slice: x: 4, y: 4 (y_hi: 2, y_lo: 2; y = y_hi * 2 + y_lo), z: 4, core: 2. Of those that a mesh axis runs over, the one named last changes fastest.
Arguments:
- latents: bfloat16 [96, 2, 1024, 640], P(None, None, 'lon', 'ch'), may hold values from -11 to 11
- next_latents: bfloat16 [96, 2, 1024, 640], P('ch', None, 'lon'), may hold values from -18 to 18
- timesteps: int32 [2], replicated, may hold values from 400 to 900
- resume_steps: int32 [2], replicated, may hold values from 40 to 100
- conv_weights: bfloat16 [2, 3, 3, 640, 640], replicated, may hold values from -0.078125 to 0.078125
- conv_bias: float32 [2, 640], replicated, may hold values from -1.5 to 1.5
- norm_gain: float32 [2, 640], replicated, may hold values from 0.1 to 1.9
- norm_shift: float32 [2, 640], replicated, may hold values from -1.5 to 1.5
- time_w1: float32 [320, 1280], replicated, may hold values from -0.3125 to 0.3125
- time_w2: float32 [1280, 640], replicated, may hold values from -0.15625 to 0.15625
Outputs:
- predicted_noise: bfloat16 [96, 2, 1024, 640], P('ch', None, 'lon')
- logprob: float32 [2], replicated
The draws below stay inside these ranges and needn't reach their ends.
All inputs are finite; a program needn't handle non-finite values.
Results may differ from the reference program's by a relative error of at most 0.0044.
Values may be sent and summed in bfloat16 or wider, within the bound.
No kernel may reach another device: no remote copies, remote signals or barrier semaphores. Data moves between devices by JAX's collectives and lax.ppermute only.
A program may use at most 576 MiB of HBM per device.

```python
import math
import jax
import jax.numpy as jnp
from jax import lax

C = 640
GROUPS = 32
TEMB = 320
TIME_HIDDEN = 1280
SAMPLES = 2
LAT = 96
LON = 1024


def draw_latents(key, part):
    key = jax.random.fold_in(key, 7)
    key_base, key_rough = jax.random.split(key, 2)
    shape = (LAT, SAMPLES, LON, C)
    column = jnp.arange(LON, dtype=jnp.float32) / LON
    col_scale = (0.6 * 3.0 ** column)[None, None, :, None]
    rough = jnp.exp(jax.random.uniform(key_rough, (LAT, SAMPLES, LON, 1), jnp.float32, -0.35, 0.35))
    base = jax.random.truncated_normal(key_base, -4.0, 4.0, shape, jnp.float32)
    return (base * col_scale * rough).astype(jnp.bfloat16)


def draw_next_latents(key, part):
    key = jax.random.fold_in(key, 11)
    key_base, key_rough, key_sample = jax.random.split(key, 3)
    shape = (LAT, SAMPLES, LON, C)
    column = jnp.arange(LON, dtype=jnp.float32) / LON
    col_scale = (0.6 * 3.0 ** column)[None, None, :, None]
    sample_scale = jnp.exp(jax.random.uniform(key_sample, (SAMPLES,), jnp.float32, -1.2, 0.47))[None, :, None, None]
    rough = jnp.exp(jax.random.uniform(key_rough, (LAT, SAMPLES, LON, 1), jnp.float32, -0.4, 0.4))
    base = jax.random.truncated_normal(key_base, -4.0, 4.0, shape, jnp.float32)
    return (base * col_scale * sample_scale * rough).astype(jnp.bfloat16)


def scatter_about(own_key, extent, deviation, limit, kind=jnp.bfloat16):
    return jnp.clip(deviation * jax.random.normal(own_key, extent, jnp.float32), -limit, limit).astype(kind)


def setup_inputs(seed: int = 0) -> dict:
    arg_keys = jax.random.split(jax.random.key(seed), 11)
    latents = draw_latents(jax.random.fold_in(arg_keys[10], 71), 0)
    next_latents = draw_next_latents(jax.random.fold_in(arg_keys[10], 71), 0)
    timesteps = jax.random.randint(arg_keys[2], (SAMPLES,), 400, 901).astype(jnp.int32)
    resume_steps = jax.random.randint(arg_keys[3], (SAMPLES,), 40, 101).astype(jnp.int32)
    conv_weights = scatter_about(arg_keys[4], (2, 3, 3, C, C), (9 * C) ** -0.5, 0.078125)
    conv_bias = scatter_about(arg_keys[5], (2, C), 0.3, 1.5, jnp.float32)
    norm_gain = jnp.clip(1.0 + 0.18 * jax.random.normal(arg_keys[6], (2, C), jnp.float32), 0.1, 1.9)
    norm_shift = scatter_about(arg_keys[7], (2, C), 0.3, 1.5, jnp.float32)
    time_w1 = scatter_about(arg_keys[8], (TEMB, TIME_HIDDEN), TEMB ** -0.5, 0.3125, jnp.float32)
    time_w2 = scatter_about(arg_keys[9], (TIME_HIDDEN, C), TIME_HIDDEN ** -0.5, 0.15625, jnp.float32)
    return dict(latents=latents, next_latents=next_latents, timesteps=timesteps, resume_steps=resume_steps, conv_weights=conv_weights, conv_bias=conv_bias, norm_gain=norm_gain, norm_shift=norm_shift, time_w1=time_w1, time_w2=time_w2)


def time_embed(timesteps, time_w1, time_w2):
    half = time_w1.shape[0] // 2
    freqs = jnp.exp(-math.log(10000.0) * jnp.arange(half, dtype=jnp.float32) / half)
    angles = timesteps.astype(jnp.float32)[:, None] * freqs[None, :]
    features = jnp.concatenate([jnp.cos(angles), jnp.sin(angles)], axis=1)
    hidden = jax.nn.silu(jnp.dot(features, time_w1, precision=lax.Precision.HIGHEST))
    return jnp.dot(hidden, time_w2, precision=lax.Precision.HIGHEST)

def group_sums(values, groups):
    rows, samples, cols, chans = values.shape
    grouped = values.reshape(rows, samples, cols, groups, chans // groups)
    return (lax.optimization_barrier(jnp.sum(grouped, axis=(0, 2, 4))), lax.optimization_barrier(jnp.sum(grouped * grouped, axis=(0, 2, 4))))

def normalize(values, sums, squares, total, gain, shift):
    groups = sums.shape[1]
    width = values.shape[3] // groups
    center = sums / total
    spread = squares / total - center * center
    factor = lax.rsqrt(spread + 1e-05)
    center = jnp.repeat(center, width, axis=1)[None, :, None, :]
    factor = jnp.repeat(factor, width, axis=1)[None, :, None, :]
    normed = (values - center) * factor * gain + shift
    return jax.nn.silu(normed).astype(jnp.bfloat16)

def convolve(padded, kernel):
    height = padded.shape[0] - 2
    across = padded.shape[2] - 2
    total = jnp.zeros((height, padded.shape[1], across, kernel.shape[3]), jnp.float32)
    for tap_row in range(3):
        for tap_col in range(3):
            piece = padded[tap_row:tap_row + height, :, tap_col:tap_col + across, :]
            total = total + lax.dot_general(piece, kernel[tap_row, tap_col], (((3,), (0,)), ((), ())), preferred_element_type=jnp.float32)
    return total

def plan(steps):
    frac = steps.astype(jnp.float32) / 1000.0
    return jnp.cos((frac + 0.008) / 1.008 * (math.pi / 2.0)) ** 2

def step_terms(current, noise, following, timesteps, resume_steps):
    alpha = plan(timesteps)
    prior = plan(timesteps - resume_steps)
    variance = (1.0 - prior) / (1.0 - alpha) * (1.0 - alpha / prior)
    keep = (1.0 - prior) * jnp.sqrt(alpha / (prior * (1.0 - alpha)))
    shape_b = lambda v: v[None, :, None, None]
    clean = (current - shape_b(jnp.sqrt(1.0 - alpha)) * noise) / shape_b(jnp.sqrt(alpha))
    center = shape_b(jnp.sqrt(prior)) * clean + shape_b(keep) * noise
    diff = following - center
    return (lax.optimization_barrier(jnp.sum(-(diff * diff) / (2.0 * shape_b(variance)), axis=(0, 2, 3))), variance)

def wrap_pad(field):
    field = jnp.concatenate([field[:, :, -1:, :], field, field[:, :, :1, :]], axis=2)
    return jnp.pad(field, ((1, 1), (0, 0), (0, 0), (0, 0)))

def reference(latents, next_latents, timesteps, resume_steps, conv_weights, conv_bias, norm_gain, norm_shift, time_w1, time_w2):
    temb = time_embed(timesteps, time_w1, time_w2)
    current = latents.astype(jnp.float32)
    total = LAT * LON * (C // GROUPS)
    sums, squares = group_sums(current, GROUPS)
    first_input = normalize(current, sums, squares, total, norm_gain[0], norm_shift[0])
    hidden = convolve(wrap_pad(first_input), conv_weights[0]) + conv_bias[0] + temb[None, :, None, :]
    sums, squares = group_sums(hidden, GROUPS)
    second_input = normalize(hidden, sums, squares, total, norm_gain[1], norm_shift[1])
    predicted_noise = (convolve(wrap_pad(second_input), conv_weights[1]) + conv_bias[1] + current).astype(jnp.bfloat16)
    terms, variance = step_terms(current, predicted_noise.astype(jnp.float32), next_latents.astype(jnp.float32), timesteps, resume_steps)
    logprob = terms / (LAT * LON * C) - 0.5 * jnp.log(variance) - 0.5 * math.log(2.0 * math.pi)
    return (predicted_noise, logprob)
```

```python
import math

import jax
import jax.numpy as jnp
from jax import lax
from jax.sharding import PartitionSpec as P

GROUPS = 32
LAT = 96


def with_halo(array, sides, width, wrap):
    for axis, dim in sides:
        size, length = (lax.axis_size(axis), array.shape[dim])
        up = [(i, (i + 1) % size) for i in range(size if wrap else size - 1)]
        down = [(j, i) for i, j in up]
        last = lax.slice_in_dim(array, length - width, length, axis=dim)
        first = lax.slice_in_dim(array, 0, width, axis=dim)
        before = lax.ppermute(last, axis, up)
        after = lax.ppermute(first, axis, down)
        array = jnp.concatenate([before, array, after], axis=dim)
    return array


def time_embed(timesteps, time_w1, time_w2):
    half = time_w1.shape[0] // 2
    freqs = jnp.exp(-math.log(10000.0) * jnp.arange(half, dtype=jnp.float32) / half)
    angles = timesteps.astype(jnp.float32)[:, None] * freqs[None, :]
    features = jnp.concatenate([jnp.cos(angles), jnp.sin(angles)], axis=1)
    hidden = jax.nn.silu(jnp.dot(features, time_w1, precision=lax.Precision.HIGHEST))
    return jnp.dot(hidden, time_w2, precision=lax.Precision.HIGHEST)


def group_sums(values, groups):
    rows, samples, cols, chans = values.shape
    grouped = values.reshape(rows, samples, cols, groups, chans // groups)
    return (jnp.sum(grouped, axis=(0, 2, 4)), jnp.sum(grouped * grouped, axis=(0, 2, 4)))


def normalize(values, sums, squares, total, gain, shift):
    groups = sums.shape[1]
    width = values.shape[3] // groups
    center = sums / total
    spread = squares / total - center * center
    factor = lax.rsqrt(spread + 1e-05)
    center = jnp.repeat(center, width, axis=1)[None, :, None, :]
    factor = jnp.repeat(factor, width, axis=1)[None, :, None, :]
    normed = (values - center) * factor * gain + shift
    return jax.nn.silu(normed).astype(jnp.bfloat16)


def convolve(padded, kernel):
    height = padded.shape[0] - 2
    across = padded.shape[2] - 2
    total = jnp.zeros((height, padded.shape[1], across, kernel.shape[3]), jnp.float32)
    for tap_row in range(3):
        for tap_col in range(3):
            piece = padded[tap_row : tap_row + height, :, tap_col : tap_col + across, :]
            total = total + lax.dot_general(
                piece,
                kernel[tap_row, tap_col],
                (((3,), (0,)), ((), ())),
                preferred_element_type=jnp.float32,
            )
    return total


def plan(steps):
    frac = steps.astype(jnp.float32) / 1000.0
    return jnp.cos((frac + 0.008) / 1.008 * (math.pi / 2.0)) ** 2


def step_terms(current, noise, following, timesteps, resume_steps):
    alpha = plan(timesteps)
    prior = plan(timesteps - resume_steps)
    variance = (1.0 - prior) / (1.0 - alpha) * (1.0 - alpha / prior)
    keep = (1.0 - prior) * jnp.sqrt(alpha / (prior * (1.0 - alpha)))
    shape_b = lambda v: v[None, :, None, None]
    clean = (current - shape_b(jnp.sqrt(1.0 - alpha)) * noise) / shape_b(jnp.sqrt(alpha))
    center = shape_b(jnp.sqrt(prior)) * clean + shape_b(keep) * noise
    diff = following - center
    return (jnp.sum(-(diff * diff) / (2.0 * shape_b(variance)), axis=(0, 2, 3)), variance)


def all_sum(parts):
    flat = jnp.concatenate([part.reshape(-1) for part in parts])
    count = lax.axis_size("lon") * lax.axis_size("ch")
    padded = jnp.pad(flat, (0, -flat.size % 128)).reshape(1, -1)
    sent = jnp.broadcast_to(padded[None], (count,) + padded.shape)
    got = lax.all_to_all(sent, ("lon", "ch"), split_axis=0, concat_axis=0, tiled=True)
    total = jnp.sum(got, axis=0).reshape(-1)
    out, at = ([], 0)
    for part in parts:
        out.append(total[at : at + part.size].reshape(part.shape))
        at += part.size
    return out


def extend(field, width):
    beside_all = with_halo(field, (("lon", 2),), width, True)
    return with_halo(beside_all, (("ch", 0),), width, False)


def body(
    latents,
    next_latents,
    timesteps,
    resume_steps,
    conv_weights,
    conv_bias,
    norm_gain,
    norm_shift,
    time_w1,
    time_w2,
):
    lon_count = lax.axis_size("lon")
    cols = latents.shape[2]
    chans = conv_weights.shape[3]
    groups = GROUPS
    group_width = chans // groups
    total = latents.shape[0] * cols * lon_count * group_width
    temb = time_embed(timesteps, time_w1, time_w2)
    row_latents = lax.all_to_all(latents, "ch", split_axis=0, concat_axis=3, tiled=True)
    current = row_latents.astype(jnp.float32)
    sums, squares = all_sum(group_sums(current, groups))
    first_input = normalize(current, sums, squares, total, norm_gain[0], norm_shift[0])
    hidden = (
        convolve(extend(first_input, 1), conv_weights[0]) + conv_bias[0] + temb[None, :, None, :]
    )
    sums, squares = all_sum(group_sums(hidden, groups))
    second_input = extend(normalize(hidden, sums, squares, total, norm_gain[1], norm_shift[1]), 1)
    predicted_noise = (convolve(second_input, conv_weights[1]) + conv_bias[1] + current).astype(
        jnp.bfloat16
    )
    terms, variance = step_terms(
        current,
        predicted_noise.astype(jnp.float32),
        next_latents.astype(jnp.float32),
        timesteps,
        resume_steps,
    )
    (terms,) = all_sum([terms])
    logprob = (
        terms / (LAT * cols * lon_count * chans)
        - 0.5 * jnp.log(variance)
        - 0.5 * math.log(2.0 * math.pi)
    )
    return (predicted_noise, logprob)


def solution(mesh):
    return jax.shard_map(
        body,
        mesh=mesh,
        in_specs=(
            P(None, None, "lon", "ch"),
            P("ch", None, "lon", None),
            P(),
            P(),
            P(),
            P(),
            P(),
            P(),
            P(),
            P(),
        ),
        out_specs=(P("ch", None, "lon", None), P()),
        check_vma=False,
    )
```

```python
import functools
import math

import jax
import jax.numpy as jnp
from jax import lax
from jax.experimental import pallas as pl
from jax.experimental.pallas import tpu as pltpu
from jax.sharding import PartitionSpec as P

GROUPS = 32
C = 640
LAT = 96
ROWS = 12
COLS = 64
SRC = 8
PART = C // SRC
WIDTH = C // GROUPS
TAPS = 9
F32 = jnp.float32
BF16 = jnp.bfloat16
VMEM = pl.BlockSpec(memory_space=pltpu.VMEM)
SMEM = pl.BlockSpec(memory_space=pltpu.SMEM)
ANY = pl.BlockSpec(memory_space=pl.ANY)
LIMIT = 56 * 2**20


def place(q, s):
    return 2 * q + 3 + 16 * s


def roll(x, by):
    by %= 128
    return x if by == 0 else pltpu.roll(x, by, 1)


def flip(x):
    n = x.shape[1]
    row = lax.broadcasted_iota(jnp.int32, (n, n), 0)
    col = lax.broadcasted_iota(jnp.int32, (n, n), 1)
    eye = jnp.where(row == col, 1.0, 0.0).astype(BF16)
    return lax.dot_general(eye, x, (((1,), (1,)), ((), ())), preferred_element_type=F32)


def lanes(rows):
    return lax.broadcasted_iota(jnp.int32, (rows, 128), 1)


def members(rows, first, base):
    chan = lax.broadcasted_iota(jnp.int32, (rows, 128), 0) + first
    low = (lanes(rows) - base) * WIDTH
    return (chan >= low) & (chan < low + WIDTH)


def silu(x):
    return 0.5 * x * (1.0 + jnp.tanh(0.5 * x))


def pack_kernel(
    part_ref, main_ref, above_ref, below_ref, left_ref, right_ref,
    pay0_ref, pay1_ref, sums_ref, halo, grid, total, square,
):
    d = pl.program_id(0)

    @pl.when(d == 0)
    def _():
        total[...] = jnp.zeros_like(total)
        square[...] = jnp.zeros_like(square)
        halo[...] = jnp.zeros_like(halo)
        grid[...] = jnp.zeros_like(grid)
        for s in range(2):
            halo[0, s, 8 : 8 + LAT, :] = left_ref[s].astype(F32)
            halo[1, s, 8 : 8 + LAT, :] = right_ref[s].astype(F32)

    start = 7 + d * ROWS
    for s in range(2):
        out = pay0_ref if s == 0 else pay1_ref
        for q in range(6):
            tile = flip(jnp.concatenate([main_ref[q, s], main_ref[q + 6, s]], axis=0))
            total[s] += tile
            square[s] += tile * tile
            out[0, q * PART : (q + 1) * PART, :] = tile.astype(BF16)
        edge = flip(jnp.concatenate([above_ref[0, s], below_ref[0, s]], axis=0))
        out[0, 6 * PART : 7 * PART, :] = edge.astype(BF16)
        at = place(-1, s)
        grid[pl.ds(at, 8, stride=2), :] = halo[0, s, pl.ds(start, 8), :]
        grid[pl.ds(at + 64, 8, stride=2), :] = halo[0, s, pl.ds(start + 6, 8), :]
        grid[pl.ds(at + 63, 8, stride=2), :] = halo[1, s, pl.ds(start, 8), :]
        grid[pl.ds(at - 1, 8, stride=2), :] = halo[1, s, pl.ds(start + 6, 8), :]
    pay0_ref[0, 7 * PART : 8 * PART, :] = flip(grid[...].astype(BF16)).astype(BF16)

    @pl.when(d == SRC - 1)
    def _():
        row = jnp.zeros((1, 128), F32)
        for s in range(2):
            for k, acc in ((0, total), (1, square)):
                column = jnp.sum(acc[s], axis=1, keepdims=True)
                own = members(PART, part_ref[0] * PART, 64 * k + 32 * s)
                row += jnp.sum(jnp.where(own, column, 0.0), axis=0, keepdims=True)
        sums_ref[...] = jnp.broadcast_to(row, sums_ref.shape)


def pack(part, latents, left, right):
    block = (ROWS, 2, COLS, PART)
    edge = (1, 2, COLS, PART)
    return pl.pallas_call(
        pack_kernel,
        grid=(SRC,),
        in_specs=[
            SMEM,
            pl.BlockSpec(block, lambda d: (d, 0, 0, 0)),
            pl.BlockSpec(edge, lambda d: (jnp.maximum(d * ROWS - 1, 0), 0, 0, 0)),
            pl.BlockSpec(edge, lambda d: (jnp.minimum(d * ROWS + ROWS, LAT - 1), 0, 0, 0)),
            pl.BlockSpec((2, LAT, PART), lambda d: (0, 0, 0)),
            pl.BlockSpec((2, LAT, PART), lambda d: (0, 0, 0)),
        ],
        out_specs=[
            pl.BlockSpec((1, 8 * PART, 128), lambda d: (d, 0, 0)),
            pl.BlockSpec((1, 7 * PART, 128), lambda d: (d, 0, 0)),
            pl.BlockSpec((128, 128), lambda d: (0, 0)),
        ],
        out_shape=[
            jax.ShapeDtypeStruct((SRC, 8 * PART, 128), BF16),
            jax.ShapeDtypeStruct((SRC, 7 * PART, 128), BF16),
            jax.ShapeDtypeStruct((128, 128), F32),
        ],
        scratch_shapes=[
            pltpu.VMEM((2, 2, LAT + 24, PART), F32),
            pltpu.VMEM((128, PART), F32),
            pltpu.VMEM((2, PART, 128), F32),
            pltpu.VMEM((2, PART, 128), F32),
        ],
        compiler_params=pltpu.CompilerParams(vmem_limit_bytes=LIMIT),
        name="pack_latents",
    )(part, latents, latents, latents, left, right)


def weight_kernel(w_ref, o_ref):
    for at in range(0, C, 128):
        o_ref[0, at : at + 128, :] = flip(w_ref[0, 0, :, at : at + 128]).astype(BF16)


def turn_weights(weights):
    taps = weights.reshape(2, TAPS, C, C)
    return pl.pallas_call(
        weight_kernel,
        grid=(2, TAPS),
        in_specs=[pl.BlockSpec((1, 1, C, C), lambda j, t: (j, t, 0, 0))],
        out_specs=pl.BlockSpec((1, C, C), lambda j, t: (j, 0, t)),
        out_shape=jax.ShapeDtypeStruct((2, C, TAPS * C), BF16),
        compiler_params=pltpu.CompilerParams(vmem_limit_bytes=LIMIT),
        name="turn_weights",
    )(taps)


def affine(sums_ref, par_ref, s, j, scale, offset):
    count = float(LAT * 1024 * WIDTH)
    row = jnp.sum(sums_ref[...], axis=0, keepdims=True)

    def of_channel(base):
        picked = jnp.where(members(C, 0, base), row, 0.0)
        return jnp.sum(picked, axis=1, keepdims=True) / count

    mean = of_channel(32 * s)
    spread = of_channel(64 + 32 * s) - mean * mean
    factor = lax.rsqrt(spread + 1e-05) * par_ref[:, 2 * j : 2 * j + 1]
    rest = par_ref[:, 2 * j + 1 : 2 * j + 2] - mean * factor
    scale[...] = jnp.broadcast_to(factor, scale.shape)
    offset[...] = jnp.broadcast_to(rest, offset.shape)


def spread_taps(xs, at, rows, tiles, edge, beside, s, part):
    lane = lanes(rows)
    low = lane < 64
    first = (lane == 0) | (lane == 64)
    last = (lane == 63) | (lane == 127)
    for q in range(-1, 7):
        if q == -1:
            tile = jnp.where(low, edge, roll(tiles[5], 64))
        elif q == 6:
            tile = jnp.where(low, roll(tiles[0], 64), edge)
        else:
            tile = tiles[q]
        side = roll(beside, -place(q, s))
        taps = (jnp.where(first, side, roll(tile, 1)), tile, jnp.where(last, side, roll(tile, -1)))
        for k, tap in enumerate(taps):
            if q == -1:
                tap = jnp.where(low & (part == 0), 0.0, tap)
            elif q == 6:
                tap = jnp.where((~low) & (part == SRC - 1), 0.0, tap)
            xs[pl.ds(k * C + at, rows), 128 * (q + 1) : 128 * (q + 2)] = tap.astype(BF16)


def product(wv, xs, n):
    x = jnp.concatenate([xs[:, n + 128 * i : n + 128 * i + 256] for i in range(3)], axis=0)
    return jnp.dot(wv[...], x, preferred_element_type=F32)


def first_kernel(
    s, part_ref, sums_ref, par_ref, recv_ref, beside_ref, w_hbm, *rest,
):
    if s == 1:
        before = rest[:5]
        rest = rest[5:]
    hid_ref, out_sums, to_right, to_left, to_next, to_prev, xs, wv, scale, offset, sem = rest
    weights = pltpu.make_async_copy(w_hbm.at[0], wv, sem)
    weights.start()
    part = part_ref[0]
    affine(sums_ref, par_ref, s, 0, scale, offset)

    @pl.loop(0, SRC)
    def _(b):
        at = pl.multiple_of(b * PART, PART)
        a, o = scale[pl.ds(at, PART), :], offset[pl.ds(at, PART), :]

        def act(x):
            return silu(x.astype(F32) * a + o)

        tiles = [act(recv_ref[b, q * PART : (q + 1) * PART, :]) for q in range(7)]
        spread_taps(xs, at, PART, tiles[:6], tiles[6], act(beside_ref[b]), s, part)

    weights.wait()
    bias = par_ref[:, 5 + s : 6 + s]
    for n in range(0, 768, 256):
        hid_ref[:, n : n + 256] = product(wv, xs, n) + bias

    row = jnp.zeros((1, 128), F32) if s == 0 else before[0][0:1, :]
    for at in range(0, C, 128):
        block = hid_ref[at : at + 128, :]
        pieces = [block[:, 128 * q : 128 * (q + 1)] for q in range(6)]
        for k in range(2):
            column = jnp.sum(sum(p * p if k else p for p in pieces), axis=1, keepdims=True)
            own = members(128, at, 64 * k + 32 * s)
            row += jnp.sum(jnp.where(own, column, 0.0), axis=0, keepdims=True)
        lane = lanes(128)
        right = jnp.zeros((128, 128), F32) if s == 0 else before[1][at : at + 128, :].astype(F32)
        left = jnp.zeros((128, 128), F32) if s == 0 else before[2][at : at + 128, :].astype(F32)
        for q in range(-1, 7):
            p = place(q, s)
            if q == -1:
                moved, whole = roll(pieces[5], 64), ((lane == p + 64), (lane == p - 1))
            elif q == 6:
                moved, whole = roll(pieces[0], 64), ((lane == p), (lane == p + 63))
            else:
                moved = pieces[q]
                whole = ((lane == p) | (lane == p + 64)), ((lane == p + 63) | (lane == p - 1))
            right = jnp.where(whole[0], roll(moved, p - 63), right)
            left = jnp.where(whole[1], roll(moved, p + 63), left)
        to_right[at : at + 128, :] = right.astype(BF16)
        to_left[at : at + 128, :] = left.astype(BF16)
        if s == 0:
            after, ahead = roll(pieces[5], 64), pieces[0]
        else:
            low = lane < 64
            after = jnp.where(low, before[3][at : at + 128, :].astype(F32), pieces[5])
            ahead = jnp.where(low, before[4][at : at + 128, :].astype(F32), roll(pieces[0], 64))
        to_next[at : at + 128, :] = after.astype(BF16)
        to_prev[at : at + 128, :] = ahead.astype(BF16)
    out_sums[...] = jnp.broadcast_to(row, out_sums.shape)


def first_conv(s, part, sums, params, recv, beside, weights, before):
    tile = jax.ShapeDtypeStruct((C, 128), BF16)
    return pl.pallas_call(
        functools.partial(first_kernel, s),
        in_specs=[SMEM, VMEM, VMEM, VMEM, VMEM, ANY] + [VMEM] * len(before),
        out_specs=[VMEM] * 6,
        out_shape=[
            jax.ShapeDtypeStruct((C, 768), F32),
            jax.ShapeDtypeStruct((128, 128), F32),
            tile, tile, tile, tile,
        ],
        scratch_shapes=[
            pltpu.VMEM((3 * C, 1024), BF16),
            pltpu.VMEM((C, TAPS * C), BF16),
            pltpu.VMEM((C, 128), F32),
            pltpu.VMEM((C, 128), F32),
            pltpu.SemaphoreType.DMA,
        ],
        compiler_params=pltpu.CompilerParams(vmem_limit_bytes=LIMIT),
        cost_estimate=pl.CostEstimate(
            flops=2 * 768 * C * C * 9, bytes_accessed=12_000_000, transcendentals=0
        ),
        name=f"first_conv_{s}",
    )(part, sums, params, recv, beside, weights, *before)


def second_kernel(
    part_ref, coef_ref, sums_ref, par_ref, near_ref, up_ref, down_ref, prev_ref, next_ref,
    hid0, hid1, w_hbm, recv0, recv1, target_hbm,
    noise_ref, out_ref,
    xs, wv, lat0, lat1, target, scale, offset, sems,
):
    copies = [
        pltpu.make_async_copy(w_hbm.at[1], wv, sems.at[0]),
        pltpu.make_async_copy(recv0.at[:, 0 : 6 * PART, :], lat0, sems.at[1]),
        pltpu.make_async_copy(recv1.at[:, 0 : 6 * PART, :], lat1, sems.at[2]),
        pltpu.make_async_copy(target_hbm, target, sems.at[3]),
    ]
    for copy in copies:
        copy.start()
    part = part_ref[0]
    result = jnp.zeros((1, 128), F32)
    for s in range(2):
        hid = (hid0, hid1)[s]
        lat = (lat0, lat1)[s]
        affine(sums_ref, par_ref, s, 1, scale, offset)

        @pl.loop(0, SRC)
        def _(b):
            at = pl.multiple_of(b * PART, PART)
            rows = pl.ds(at, PART)
            a, o = scale[rows, :], offset[rows, :]
            lane = lanes(PART)
            low = lane < 64

            def act(x):
                return silu(x.astype(F32) * a + o)

            tiles = [act(hid[rows, 128 * q : 128 * (q + 1)]) for q in range(6)]
            above, below = prev_ref[rows, :].astype(F32), next_ref[rows, :].astype(F32)
            if s == 0:
                edge = jnp.where(low, above, roll(below, 64))
            else:
                edge = jnp.where(low, roll(above, 64), below)
            beside = near_ref[rows, :].astype(F32)
            p = place(-1, s)
            corner = roll(up_ref[rows, :].astype(F32), 52)
            beside = jnp.where((lane == p) | (lane == p + 63), corner, beside)
            p = place(6, s)
            corner = roll(down_ref[rows, :].astype(F32), 76)
            beside = jnp.where((lane == p + 64) | (lane == p - 1), corner, beside)
            spread_taps(xs, at, PART, tiles, act(edge), act(beside), s, part)

        if s == 0:
            copies[0].wait()
        bias = par_ref[:, 4:5]
        if s == 0:
            for copy in copies[1:]:
                copy.wait()
        acc = jnp.zeros((128, 128), F32)
        keep, gain = coef_ref[2 * s], coef_ref[2 * s + 1]
        for n in range(0, 768, 256):
            out = product(wv, xs, n) + bias
            for half in range(2):
                q = n // 128 + half
                mine = lat[:, q * PART : (q + 1) * PART, :].reshape(C, 128).astype(F32)
                noise = (out[:, 128 * half : 128 * (half + 1)] + mine).astype(BF16)
                center = keep * mine + gain * noise.astype(F32)
                want = jnp.concatenate([target[q, s], target[q + 6, s]], axis=0)
                for at in range(0, C, 128):
                    turned = flip(noise[at : at + 128, :]).astype(BF16)
                    noise_ref[q, s, :, at : at + 128] = turned[0:64]
                    noise_ref[q + 6, s, :, at : at + 128] = turned[64:128]
                    diff = flip(want[:, at : at + 128]) - center[at : at + 128, :]
                    acc += diff * diff
        value = jnp.sum(acc, axis=(0, 1), keepdims=True)
        result = jnp.where(lanes(1) == s, value, result)
    out_ref[...] = jnp.broadcast_to(result, out_ref.shape)


def second_conv(part, coef, sums, params, tiles, hidden, weights, recv, target):
    return pl.pallas_call(
        second_kernel,
        in_specs=[SMEM, SMEM] + [VMEM] * 9 + [ANY] * 4,
        out_specs=[VMEM] * 2,
        out_shape=[
            jax.ShapeDtypeStruct((ROWS, 2, COLS, C), BF16),
            jax.ShapeDtypeStruct((128, 128), F32),
        ],
        scratch_shapes=[
            pltpu.VMEM((3 * C, 1024), BF16),
            pltpu.VMEM((C, TAPS * C), BF16),
            pltpu.VMEM((SRC, 6 * PART, 128), BF16),
            pltpu.VMEM((SRC, 6 * PART, 128), BF16),
            pltpu.VMEM((ROWS, 2, COLS, C), BF16),
            pltpu.VMEM((C, 128), F32),
            pltpu.VMEM((C, 128), F32),
            pltpu.SemaphoreType.DMA((4,)),
        ],
        compiler_params=pltpu.CompilerParams(vmem_limit_bytes=LIMIT),
        cost_estimate=pl.CostEstimate(
            flops=4 * 768 * C * C * 9, bytes_accessed=20_000_000, transcendentals=0
        ),
        name="second_conv",
    )(part, coef, sums, params, *tiles, *hidden, weights, *recv, target)


def time_embed(timesteps, time_w1, time_w2):
    half = time_w1.shape[0] // 2
    freqs = jnp.exp(-math.log(10000.0) * jnp.arange(half, dtype=F32) / half)
    angles = timesteps.astype(F32)[:, None] * freqs[None, :]
    features = jnp.concatenate([jnp.cos(angles), jnp.sin(angles)], axis=1)
    hidden = jax.nn.silu(jnp.dot(features, time_w1, precision=lax.Precision.HIGHEST))
    return jnp.dot(hidden, time_w2, precision=lax.Precision.HIGHEST)


def plan(steps):
    frac = steps.astype(F32) / 1000.0
    return jnp.cos((frac + 0.008) / 1.008 * (math.pi / 2.0)) ** 2


def everywhere(rows):
    got = lax.all_to_all(rows.reshape(128, 1, 128), ("lon", "ch"), 0, 0, tiled=True)
    return got.reshape(128, 128)


def ring(axis, step, wrap):
    size = lax.axis_size(axis)
    return [(i, (i + step) % size) for i in range(size) if wrap or 0 <= i + step < size]


def swap(array, axis):
    return lax.all_to_all(array, axis, split_axis=0, concat_axis=0, tiled=True)


def body(
    latents, next_latents, timesteps, resume_steps, conv_weights, conv_bias,
    norm_gain, norm_shift, time_w1, time_w2,
):
    part = lax.axis_index("ch").astype(jnp.int32).reshape(1)
    last = latents[:, :, COLS - 1, :].transpose(1, 0, 2)
    first = latents[:, :, 0, :].transpose(1, 0, 2)
    left = lax.ppermute(last, "lon", ring("lon", 1, True))
    right = lax.ppermute(first, "lon", ring("lon", -1, True))
    pay0, pay1, sums = pack(part, latents, left, right)
    pay0, pay1, sums, conv_weights, time_w1 = lax.optimization_barrier(
        (pay0, pay1, sums, conv_weights, time_w1)
    )
    recv0 = swap(pay0, "ch")
    recv1 = swap(pay1, "ch")
    sums = everywhere(sums)
    turned = turn_weights(conv_weights)

    temb = time_embed(timesteps, time_w1, time_w2)
    columns = [
        norm_gain[0], norm_shift[0], norm_gain[1], norm_shift[1], conv_bias[1],
        conv_bias[0] + temb[0], conv_bias[0] + temb[1],
    ]
    params = jnp.pad(jnp.stack(columns, axis=1), ((0, 0), (0, 128 - len(columns))))

    alpha = plan(timesteps)
    prior = plan(timesteps - resume_steps)
    variance = (1.0 - prior) / (1.0 - alpha) * (1.0 - alpha / prior)
    keep = (1.0 - prior) * jnp.sqrt(alpha / (prior * (1.0 - alpha)))
    ratio = jnp.sqrt(prior) / jnp.sqrt(alpha)
    coef = jnp.stack([ratio, keep - ratio * jnp.sqrt(1.0 - alpha)], axis=1).reshape(4)

    beside = recv0[:, 7 * PART : 8 * PART, :]
    hid0, *before = first_conv(0, part, sums, params, recv0, beside, turned, ())
    hid1, sums, to_right, to_left, to_next, to_prev = first_conv(
        1, part, sums, params, recv1, beside, turned, before
    )
    from_left = lax.ppermute(to_right, "lon", ring("lon", 1, True))
    from_right = lax.ppermute(to_left, "lon", ring("lon", -1, True))
    from_prev = lax.ppermute(to_next, "ch", ring("ch", 1, False))
    from_next = lax.ppermute(to_prev, "ch", ring("ch", -1, False))
    near = from_left + from_right
    up = lax.ppermute(near, "ch", ring("ch", 1, False))
    down = lax.ppermute(near, "ch", ring("ch", -1, False))
    sums = everywhere(sums)
    noise, terms = second_conv(
        part, coef, sums, params, (near, up, down, from_prev, from_next),
        (hid0, hid1), turned, (recv0, recv1), next_latents,
    )
    squares = jnp.sum(everywhere(terms), axis=0)[:2]
    logprob = (
        -squares / (2.0 * variance) / float(LAT * 1024 * C)
        - 0.5 * jnp.log(variance)
        - 0.5 * math.log(2.0 * math.pi)
    )
    return (noise, logprob)


def solution(mesh):
    return jax.shard_map(
        body,
        mesh=mesh,
        in_specs=(
            P(None, None, "lon", "ch"),
            P("ch", None, "lon", None),
            P(), P(), P(), P(), P(), P(), P(), P(),
        ),
        out_specs=(P("ch", None, "lon", None), P()),
        check_vma=False,
    )
```

```python
import functools
import math

import jax
import jax.numpy as jnp
import numpy as np
from jax import lax
from jax.experimental import pallas as pl
from jax.experimental.pallas import tpu as pltpu
from jax.sharding import PartitionSpec as P

GROUPS = 32
C = 640
LAT = 96
ROWS = 12
COLS = 64
SRC = 8
PART = C // SRC
WIDTH = C // GROUPS
TAPS = 9
F32 = jnp.float32
BF16 = jnp.bfloat16
VMEM = pl.BlockSpec(memory_space=pltpu.VMEM)
SMEM = pl.BlockSpec(memory_space=pltpu.SMEM)
ANY = pl.BlockSpec(memory_space=pl.ANY)
CHUNK = 16
LIMIT = 56 * 2**20


def roll(x, by):
    by %= 128
    return x if by == 0 else pltpu.roll(x, by, 1)


def flip(eye, x):
    return lax.dot_general(eye, x, (((1,), (1,)), ((), ())), preferred_element_type=F32)


def side_lanes(of_left, of_right):
    out = np.zeros((128, 1024), np.float32)
    for q in range(-1, 7):
        at = 128 * (q + 1)
        out[of_left(q), at] = 1
        out[of_left(q + 6), at + 64] = 1
        out[of_right(q), at + 63] = 1
        out[of_right(q + 6), at + 127] = 1
    return out.astype(BF16)


def halo_lane(s, side, row):
    return 32 * s + 16 * side + row + 1


def halo_taps():
    out = np.zeros((256, TAPS * 128), np.float32)
    for i in range(3):
        for k in range(3):
            for s in range(2):
                for side in range(2):
                    for row in range(-1, 13):
                        source = 128 * s + 16 * (3 * side + k) + row + i - 1 + 2
                        out[source, 128 * (3 * i + k) + halo_lane(s, side, row)] = 1
    return out.astype(BF16)


def lanes(rows):
    return lax.broadcasted_iota(jnp.int32, (rows, 128), 1)


def members(rows, first, base):
    chan = lax.broadcasted_iota(jnp.int32, (rows, 128), 0) + first
    low = (lanes(rows) - base) * WIDTH
    return (chan >= low) & (chan < low + WIDTH)


def silu(x):
    return 0.5 * x * (1.0 + jnp.tanh(0.5 * x))


def pack_kernel(s, part_ref, main_ref, left_ref, right_ref, *rest):
    if s == 1:
        prev_ref, *rest = rest
    pay_ref, sums_ref, taken, turned = rest
    e = pl.program_id(0)
    x = main_ref[0].astype(F32)

    @pl.when(e == 0)
    def _():
        taken[...] = jnp.zeros_like(taken)
        turned[...] = jnp.zeros_like(turned)
        sums_ref[...] = jnp.zeros_like(sums_ref) if s == 0 else prev_ref[...]

    row = sums_ref[...]
    for k in range(2):
        column = jnp.sum(jnp.sum(x * x if k else x, axis=0), axis=1, keepdims=True)
        own = members(CHUNK, part_ref[0] * PART + e * CHUNK, 64 * k + 32 * s)
        row += jnp.sum(jnp.where(own, column, 0.0), axis=0, keepdims=True)
    sums_ref[...] = row

    taken[:, 0:LAT] = x.reshape(COLS * CHUNK, LAT)
    for j in range(CHUNK):
        plain = taken[pl.ds(j, COLS, stride=CHUNK), :]
        both = jnp.concatenate([plain, roll(plain, -6)], axis=0).T
        turned[pl.ds(CHUNK + j, LAT, stride=CHUNK), :] = both[0:LAT, :]

    lane = lanes(CHUNK)
    low = lane < 64
    pad = jnp.zeros((CHUNK, 128 - LAT), F32)
    near = [left_ref[0, 0], left_ref[0, 1], main_ref[0, 0], main_ref[0, COLS - 1],
            right_ref[0, 0], right_ref[0, 1]]
    near = [jnp.concatenate([col.astype(F32), pad], axis=1) for col in near]

    def tile(r):
        return turned[CHUNK * (r + 1) : CHUNK * (r + 2), :]

    for d in range(SRC):
        for q in range(6):
            pay_ref[d, q] = tile(d * ROWS + q).astype(BF16)
        edge = jnp.where(low, tile(d * ROWS - 1), tile(d * ROWS + 6))
        pay_ref[d, 6] = edge.astype(BF16)
        halo = jnp.zeros((CHUNK, 128), F32)
        for kind in range(6):
            own = (lane >= 16 * kind) & (lane < 16 * kind + 16)
            halo = jnp.where(own, roll(near[kind], 16 * kind + 2 - d * ROWS), halo)
        pay_ref[d, 7] = halo.astype(BF16)


def pack(s, part, latents, left, right, before):
    line = pl.BlockSpec((1, 128), lambda e: (0, 0))
    return pl.pallas_call(
        functools.partial(pack_kernel, s),
        grid=(PART // CHUNK,),
        in_specs=[
            SMEM,
            pl.BlockSpec((1, COLS, CHUNK, LAT), lambda e: (s, 0, e, 0)),
            pl.BlockSpec((1, 2, CHUNK, LAT), lambda e: (s, 0, e, 0)),
            pl.BlockSpec((1, 2, CHUNK, LAT), lambda e: (s, 0, e, 0)),
        ]
        + [line] * len(before),
        out_specs=[pl.BlockSpec((SRC, 8, CHUNK, 128), lambda e: (0, 0, e, 0)), line],
        out_shape=[
            jax.ShapeDtypeStruct((SRC, 8, PART, 128), BF16),
            jax.ShapeDtypeStruct((1, 128), F32),
        ],
        scratch_shapes=[
            pltpu.VMEM((COLS * CHUNK, 128), F32),
            pltpu.VMEM(((LAT + 8) * CHUNK, 128), F32),
        ],
        compiler_params=pltpu.CompilerParams(vmem_limit_bytes=LIMIT),
        name=f"pack_latents_{s}",
    )(part, latents, left, right, *before)


def weight_kernel(w_ref, eye_ref, o_ref):
    for at in range(0, C, 256):
        n = min(256, C - at)
        turned = flip(eye_ref[0:n, 0:n], w_ref[0, 0, :, at : at + n])
        o_ref[at : at + n, :] = turned.astype(BF16)


def turn_weights(j, weights, eye):
    taps = weights.reshape(2, TAPS, C, C)
    return pl.pallas_call(
        weight_kernel,
        grid=(TAPS,),
        in_specs=[
            pl.BlockSpec((1, 1, C, C), lambda t: (j, t, 0, 0)),
            pl.BlockSpec((256, 256), lambda t: (0, 0)),
        ],
        out_specs=pl.BlockSpec((C, C), lambda t: (0, t)),
        out_shape=jax.ShapeDtypeStruct((C, TAPS * C), BF16),
        compiler_params=pltpu.CompilerParams(vmem_limit_bytes=LIMIT),
        cost_estimate=pl.CostEstimate(
            flops=TAPS * 2 * C * C * 256, bytes_accessed=15_000_000, transcendentals=0
        ),
        name=f"turn_weights_{j}",
    )(taps, eye)


def affine(sums_ref, par_ref, s, j, scale, offset):
    count = float(LAT * 1024 * WIDTH)
    row = jnp.sum(sums_ref[...], axis=0, keepdims=True)

    def of_channel(base):
        picked = jnp.where(members(C, 0, base), row, 0.0)
        return jnp.sum(picked, axis=1, keepdims=True) / count

    mean = of_channel(32 * s)
    spread = of_channel(64 + 32 * s) - mean * mean
    factor = lax.rsqrt(spread + 1e-05) * par_ref[:, 2 * j : 2 * j + 1]
    rest = par_ref[:, 2 * j + 1 : 2 * j + 2] - mean * factor
    scale[...] = jnp.broadcast_to(factor, scale.shape)
    offset[...] = jnp.broadcast_to(rest, offset.shape)


def spread_taps(xs, at, rows, tiles, edge, sides, part):
    lane = lanes(rows)
    low = lane < 64
    first = (lane == 0) | (lane == 64)
    last = (lane == 63) | (lane == 127)
    for q in range(-1, 7):
        if q == -1:
            tile = jnp.where(low, edge, roll(tiles[5], 64))
        elif q == 6:
            tile = jnp.where(low, roll(tiles[0], 64), edge)
        else:
            tile = tiles[q]
        side = sides[pl.ds(at, rows), 128 * (q + 1) : 128 * (q + 2)]
        taps = (jnp.where(first, side, roll(tile, 1)), tile, jnp.where(last, side, roll(tile, -1)))
        for k, tap in enumerate(taps):
            if q == -1:
                tap = jnp.where(low & (part == 0), 0.0, tap)
            elif q == 6:
                tap = jnp.where((~low) & (part == SRC - 1), 0.0, tap)
            xs[pl.ds(k * C + at, rows), 128 * (q + 1) : 128 * (q + 2)] = tap.astype(BF16)


def product(wv, xs, n):
    x = jnp.concatenate([xs[:, n + 128 * i : n + 128 * i + 256] for i in range(3)], axis=0)
    return jnp.dot(wv[...], x, preferred_element_type=F32)


def first_kernel(
    s, part_ref, sums_ref, par_ref, pick_ref, recv_hbm, w_hbm, *rest,
):
    if s == 1:
        taps_ref, recv_other, before_sums, before_next, before_prev, *rest = rest
        hid_hbm, out_sums, to_next, to_prev, out_halo, *rest = rest
        xs, wv, scale, offset, recv, hid, sides, sems, other, xh = rest
    else:
        hid_hbm, out_sums, to_next, to_prev, *rest = rest
        xs, wv, scale, offset, recv, hid, sides, sems = rest
    fetch = pltpu.make_async_copy(recv_hbm, recv, sems.at[0])
    fetch.start()
    if s == 1:
        fetch_other = pltpu.make_async_copy(recv_other.at[:, 7], other, sems.at[2])
        fetch_other.start()
    weights = pltpu.make_async_copy(w_hbm, wv, sems.at[1])
    weights.start()
    part = part_ref[0]

    def act(x, a, o):
        return silu(x.astype(F32) * a + o)

    def halo_act(x):
        r = (lanes(C) & 15) - 2
        outside = ((part == 0) & (r < 0)) | ((part == SRC - 1) & (r >= ROWS))
        return jnp.where(outside, 0.0, act(x, scale[...], offset[...])).astype(BF16)

    if s == 1:
        affine(sums_ref, par_ref, 0, 0, scale, offset)
        fetch_other.wait()
        halo_other = halo_act(other[...].reshape(C, 128))
    affine(sums_ref, par_ref, s, 0, scale, offset)
    fetch.wait()
    halo = halo_act(recv[:, 7].reshape(C, 128))
    sides[...] = jnp.dot(halo, pick_ref[...], preferred_element_type=F32)
    if s == 1:
        both = jnp.concatenate([halo_other, halo], axis=1)
        for t in range(TAPS):
            picked = jnp.dot(both, taps_ref[:, 128 * t : 128 * t + 128], preferred_element_type=F32)
            xh[C * t : C * (t + 1), :] = picked.astype(BF16)

    @pl.loop(0, SRC)
    def _(b):
        at = pl.multiple_of(b * PART, PART)
        a, o = scale[pl.ds(at, PART), :], offset[pl.ds(at, PART), :]
        tiles = [act(recv[b, q], a, o) for q in range(7)]
        spread_taps(xs, at, PART, tiles[:6], tiles[6], sides, part)

    weights.wait()
    bias = par_ref[:, 5 + s : 6 + s]
    stores = []
    for c in range(3):
        n = 256 * c
        hid[:, n : n + 256] = product(wv, xs, n) + bias
        store = pltpu.make_async_copy(
            hid.at[:, n : n + 256], hid_hbm.at[:, n : n + 256], sems.at[3 + c]
        )
        store.start()
        stores.append(store)
    if s == 1:
        halo = jnp.dot(wv[...], xh[...], preferred_element_type=F32)
        bias = jnp.where(lanes(C) < 32, par_ref[:, 5:6], par_ref[:, 6:7])
        out_halo[...] = (halo + bias).astype(BF16)

    row = jnp.zeros((1, 128), F32) if s == 0 else before_sums[0:1, :]
    for at in range(0, C, 128):
        pieces = [hid[at : at + 128, 128 * q : 128 * (q + 1)] for q in range(6)]
        for k in range(2):
            column = jnp.sum(sum(p * p if k else p for p in pieces), axis=1, keepdims=True)
            own = members(128, at, 64 * k + 32 * s)
            row += jnp.sum(jnp.where(own, column, 0.0), axis=0, keepdims=True)
        if s == 0:
            after, ahead = roll(pieces[5], 64), pieces[0]
        else:
            low = lanes(128) < 64
            after = jnp.where(low, before_next[at : at + 128, :].astype(F32), pieces[5])
            ahead = jnp.where(low, before_prev[at : at + 128, :].astype(F32), roll(pieces[0], 64))
        to_next[at : at + 128, :] = after.astype(BF16)
        to_prev[at : at + 128, :] = ahead.astype(BF16)
    out_sums[...] = jnp.broadcast_to(row, out_sums.shape)
    for store in stores:
        store.wait()


def first_conv(s, part, sums, params, pick, recv, weights, before):
    tile = jax.ShapeDtypeStruct((C, 128), BF16)
    more = [VMEM, ANY, VMEM, VMEM, VMEM] if s == 1 else []
    return pl.pallas_call(
        functools.partial(first_kernel, s),
        in_specs=[SMEM, VMEM, VMEM, VMEM, ANY, ANY] + more,
        out_specs=[ANY] + [VMEM] * (3 + s),
        out_shape=[
            jax.ShapeDtypeStruct((C, 768), F32),
            jax.ShapeDtypeStruct((128, 128), F32),
        ]
        + [tile] * (2 + s),
        scratch_shapes=[
            pltpu.VMEM((3 * C, 1024), BF16),
            pltpu.VMEM((C, TAPS * C), BF16),
            pltpu.VMEM((C, 128), F32),
            pltpu.VMEM((C, 128), F32),
            pltpu.VMEM((SRC, 8, PART, 128), BF16),
            pltpu.VMEM((C, 768), F32),
            pltpu.VMEM((C, 1024), F32),
            pltpu.SemaphoreType.DMA((6,)),
        ]
        + [pltpu.VMEM((SRC, PART, 128), BF16), pltpu.VMEM((TAPS * C, 128), BF16)][: 2 * s],
        compiler_params=pltpu.CompilerParams(vmem_limit_bytes=LIMIT),
        cost_estimate=pl.CostEstimate(
            flops=2 * 768 * C * C * 9, bytes_accessed=12_000_000, transcendentals=0
        ),
        name=f"first_conv_{s}",
    )(part, sums, params, pick, recv, weights, *before)


def second_kernel(
    part_ref, coef_ref, sums_ref, par_ref, pick_ref, eye_ref, near_ref, prev_ref, next_ref,
    hid0, hid1, w_hbm, recv0, recv1, target_hbm,
    noise_hbm, out_ref,
    xs, wv, hid, lat, target, noise_out, sides, scale, offset, sems,
):
    copies = [
        pltpu.make_async_copy(hid0, hid.at[0], sems.at[0]),
        pltpu.make_async_copy(w_hbm, wv, sems.at[1]),
        pltpu.make_async_copy(hid1, hid.at[1], sems.at[2]),
        pltpu.make_async_copy(recv0.at[:, 0:6], lat.at[0], sems.at[3]),
        pltpu.make_async_copy(recv1.at[:, 0:6], lat.at[1], sems.at[4]),
        pltpu.make_async_copy(target_hbm, target, sems.at[5]),
    ]
    for copy in copies:
        copy.start()
    part = part_ref[0]
    result = jnp.zeros((1, 128), F32)
    stores = []
    for s in range(2):
        affine(sums_ref, par_ref, s, 1, scale, offset)
        halo = silu(near_ref[...].astype(F32) * scale[...] + offset[...]).astype(BF16)
        sides[...] = jnp.dot(halo, pick_ref[s], preferred_element_type=F32)
        copies[2 * s].wait()

        @pl.loop(0, SRC)
        def _(b):
            at = pl.multiple_of(b * PART, PART)
            rows = pl.ds(at, PART)
            a, o = scale[rows, :], offset[rows, :]
            low = lanes(PART) < 64

            def act(x):
                return silu(x * a + o)

            tiles = [act(hid[s, rows, 128 * q : 128 * (q + 1)]) for q in range(6)]
            above, below = prev_ref[rows, :].astype(F32), next_ref[rows, :].astype(F32)
            if s == 0:
                edge = jnp.where(low, above, roll(below, 64))
            else:
                edge = jnp.where(low, roll(above, 64), below)
            spread_taps(xs, at, PART, tiles, act(edge), sides, part)

        if s == 0:
            copies[1].wait()
            for copy in copies[3:]:
                copy.wait()
        bias = par_ref[:, 4:5]
        acc = jnp.zeros((8, C), F32)
        keep, gain = coef_ref[2 * s], coef_ref[2 * s + 1]
        for n in range(0, 768, 256):
            q = n // 128
            mine = jnp.concatenate([lat[s, :, q + h].reshape(C, 128) for h in range(2)], axis=1)
            noise = (product(wv, xs, n) + bias + mine.astype(F32)).astype(BF16)
            plain = flip(eye_ref[...], noise)
            center = keep * flip(eye_ref[...], mine) + gain * plain
            for h in range(4):
                r = q + h // 2 + 6 * (h % 2)
                noise_out[s, r] = plain[64 * h : 64 * h + 64].astype(BF16)
                diff = target[r, s].astype(F32) - center[64 * h : 64 * h + 64]
                acc += jnp.sum((diff * diff).reshape(8, 8, C), axis=0)
        store = pltpu.make_async_copy(noise_out.at[s], noise_hbm.at[:, s], sems.at[6 + s])
        store.start()
        stores.append(store)
        value = jnp.sum(acc, axis=(0, 1), keepdims=True)
        result = jnp.where(lanes(1) == s, value, result)
    out_ref[...] = jnp.broadcast_to(result, out_ref.shape)
    for store in stores:
        store.wait()


def second_conv(part, coef, sums, params, pick, eye, tiles, hidden, weights, recv, target):
    return pl.pallas_call(
        second_kernel,
        in_specs=[SMEM, SMEM] + [VMEM] * 7 + [ANY] * 6,
        out_specs=[ANY, VMEM],
        out_shape=[
            jax.ShapeDtypeStruct((ROWS, 2, COLS, C), BF16),
            jax.ShapeDtypeStruct((128, 128), F32),
        ],
        scratch_shapes=[
            pltpu.VMEM((3 * C, 1024), BF16),
            pltpu.VMEM((C, TAPS * C), BF16),
            pltpu.VMEM((2, C, 768), F32),
            pltpu.VMEM((2, SRC, 6, PART, 128), BF16),
            pltpu.VMEM((ROWS, 2, COLS, C), BF16),
            pltpu.VMEM((2, ROWS, COLS, C), BF16),
            pltpu.VMEM((C, 1024), F32),
            pltpu.VMEM((C, 128), F32),
            pltpu.VMEM((C, 128), F32),
            pltpu.SemaphoreType.DMA((8,)),
        ],
        compiler_params=pltpu.CompilerParams(vmem_limit_bytes=LIMIT),
        cost_estimate=pl.CostEstimate(
            flops=4 * 768 * C * C * 9, bytes_accessed=20_000_000, transcendentals=0
        ),
        name="second_conv",
    )(part, coef, sums, params, pick, eye, *tiles, *hidden, weights, *recv, target)


def time_embed(timesteps, time_w1, time_w2):
    half = time_w1.shape[0] // 2
    freqs = jnp.exp(-math.log(10000.0) * jnp.arange(half, dtype=F32) / half)
    angles = timesteps.astype(F32)[:, None] * freqs[None, :]
    features = jnp.concatenate([jnp.cos(angles), jnp.sin(angles)], axis=1)
    hidden = jax.nn.silu(jnp.dot(features, time_w1, precision=lax.Precision.HIGHEST))
    return jnp.dot(hidden, time_w2, precision=lax.Precision.HIGHEST)


def plan(steps):
    frac = steps.astype(F32) / 1000.0
    return jnp.cos((frac + 0.008) / 1.008 * (math.pi / 2.0)) ** 2


def everywhere(rows):
    got = lax.all_to_all(rows.reshape(128, 1, 128), ("lon", "ch"), 0, 0, tiled=True)
    return got.reshape(128, 128)


def ring(axis, step, wrap):
    size = lax.axis_size(axis)
    return [(i, (i + step) % size) for i in range(size) if wrap or 0 <= i + step < size]


def swap(array, axis):
    return lax.all_to_all(array, axis, split_axis=0, concat_axis=0, tiled=True)


def after(value, *others):
    return lax.optimization_barrier((value,) + others)[0]


def butterfly(x):
    for axis in ("lon", "ch"):
        step = 1
        while step < lax.axis_size(axis):
            pairs = [(i, i ^ step) for i in range(lax.axis_size(axis))]
            x = x + lax.ppermute(x, axis, pairs)
            step *= 2
    return x


def body(
    latents, next_latents, timesteps, resume_steps, conv_weights, conv_bias,
    norm_gain, norm_shift, time_w1, time_w2,
):
    part = lax.axis_index("ch").astype(jnp.int32).reshape(1)
    eye = jnp.asarray(np.eye(256, dtype=np.float32).astype(BF16))
    first_pick = jnp.asarray(side_lanes(lambda r: 16 + r + 2, lambda r: 64 + r + 2))
    second_pick = jnp.asarray(
        np.stack(
            [
                side_lanes(lambda r: halo_lane(s, 0, r), lambda r: halo_lane(s, 1, r))
                for s in range(2)
            ]
        )
    )
    tap_pick = jnp.asarray(halo_taps())

    cells = latents.transpose(1, 2, 3, 0)
    left = lax.ppermute(cells[:, COLS - 2 :], "lon", ring("lon", 1, True))
    right = lax.ppermute(cells[:, :2], "lon", ring("lon", -1, True))
    pay0, sums = pack(0, part, cells, left, right, ())
    pay1, sums = pack(1, part, cells, left, right, (sums,))
    recv0 = swap(pay0, "ch")
    sums = butterfly(sums)
    recv1 = swap(after(pay1, recv0), "ch")
    conv_weights = after(conv_weights, pay1)
    turned = [turn_weights(j, conv_weights, eye) for j in range(2)]
    time_w1 = after(time_w1, pay1)

    temb = time_embed(timesteps, time_w1, time_w2)
    columns = [
        norm_gain[0], norm_shift[0], norm_gain[1], norm_shift[1], conv_bias[1],
        conv_bias[0] + temb[0], conv_bias[0] + temb[1],
    ]
    params = jnp.pad(jnp.stack(columns, axis=1), ((0, 0), (0, 128 - len(columns))))

    alpha = plan(timesteps)
    prior = plan(timesteps - resume_steps)
    variance = (1.0 - prior) / (1.0 - alpha) * (1.0 - alpha / prior)
    keep = (1.0 - prior) * jnp.sqrt(alpha / (prior * (1.0 - alpha)))
    ratio = jnp.sqrt(prior) / jnp.sqrt(alpha)
    coef = jnp.stack([ratio, keep - ratio * jnp.sqrt(1.0 - alpha)], axis=1).reshape(4)

    hid0, *before = first_conv(0, part, sums, params, first_pick, recv0, turned[0], ())
    hid1, sums, to_next, to_prev, near = first_conv(
        1, part, sums, params, first_pick, recv1, turned[0], (tap_pick, recv0, *before)
    )
    from_prev = lax.ppermute(to_next, "ch", ring("ch", 1, False))
    from_next = lax.ppermute(to_prev, "ch", ring("ch", -1, False))
    sums = everywhere(sums)
    noise, terms = second_conv(
        part, coef, sums, params, second_pick, eye, (near, from_prev, from_next),
        (hid0, hid1), turned[1], (recv0, recv1), next_latents,
    )
    squares = jnp.sum(everywhere(terms), axis=0)[:2]
    logprob = (
        -squares / (2.0 * variance) / float(LAT * 1024 * C)
        - 0.5 * jnp.log(variance)
        - 0.5 * math.log(2.0 * math.pi)
    )
    return (noise, logprob)


def solution(mesh):
    return jax.shard_map(
        body,
        mesh=mesh,
        in_specs=(
            P(None, None, "lon", "ch"),
            P("ch", None, "lon", None),
            P(), P(), P(), P(), P(), P(), P(), P(),
        ),
        out_specs=(P("ch", None, "lon", None), P()),
        check_vma=False,
    )
```

```python
import functools
import math

import jax
import jax.numpy as jnp
import numpy as np
from jax import lax
from jax.experimental import pallas as pl
from jax.experimental.pallas import tpu as pltpu
from jax.sharding import PartitionSpec as P

GROUPS = 32
C = 640
LAT = 96
ROWS = 12
COLS = 64
SRC = 8
PART = C // SRC
WIDTH = C // GROUPS
TAPS = 9
F32 = jnp.float32
BF16 = jnp.bfloat16
VMEM = pl.BlockSpec(memory_space=pltpu.VMEM)
SMEM = pl.BlockSpec(memory_space=pltpu.SMEM)
ANY = pl.BlockSpec(memory_space=pl.ANY)
CHUNK = 16
LIMIT = 32 * 2**20


def roll(x, by):
    by %= 128
    return x if by == 0 else pltpu.roll(x, by, 1)


def side_lanes(of_left, of_right):
    out = np.zeros((128, 1024), np.float32)
    for q in range(-1, 7):
        at = 128 * (q + 1)
        out[of_left(q), at] = 1
        out[of_left(q + 6), at + 64] = 1
        out[of_right(q), at + 63] = 1
        out[of_right(q + 6), at + 127] = 1
    return out.astype(BF16)


def halo_lane(s, side, row):
    return 32 * s + 16 * side + row + 1


def halo_taps():
    out = np.zeros((256, TAPS * 128), np.float32)
    for i in range(3):
        for k in range(3):
            for s in range(2):
                for side in range(2):
                    for row in range(-1, 13):
                        source = 128 * s + 16 * (3 * side + k) + row + i - 1 + 2
                        out[source, 128 * (3 * i + k) + halo_lane(s, side, row)] = 1
    return out.astype(BF16)


def lanes(rows):
    return lax.broadcasted_iota(jnp.int32, (rows, 128), 1)


def members(rows, first, base):
    chan = lax.broadcasted_iota(jnp.int32, (rows, 128), 0) + first
    low = (lanes(rows) - base) * WIDTH
    return (chan >= low) & (chan < low + WIDTH)


def silu(x):
    return 0.5 * x * (1.0 + jnp.tanh(0.5 * x))


def pack_kernel(s, part_ref, main_ref, *rest):
    if s == 1:
        prev_ref, *rest = rest
    pay_ref, sums_ref, taken, turned = rest
    e = pl.program_id(0)
    x = main_ref[0].astype(F32)

    @pl.when(e == 0)
    def _():
        taken[...] = jnp.zeros_like(taken)
        turned[...] = jnp.zeros_like(turned)
        sums_ref[...] = jnp.zeros_like(sums_ref) if s == 0 else prev_ref[...]

    row = sums_ref[...]
    for k in range(2):
        column = jnp.sum(jnp.sum(x * x if k else x, axis=0), axis=1, keepdims=True)
        own = members(CHUNK, part_ref[0] * PART + e * CHUNK, 64 * k + 32 * s)
        row += jnp.sum(jnp.where(own, column, 0.0), axis=0, keepdims=True)
    sums_ref[...] = row

    taken[:, 0:LAT] = x.reshape(COLS * CHUNK, LAT)
    for j in range(CHUNK):
        plain = taken[pl.ds(j, COLS, stride=CHUNK), :]
        both = jnp.concatenate([plain, roll(plain, -6)], axis=0).T
        turned[pl.ds(CHUNK + j, LAT, stride=CHUNK), :] = both[0:LAT, :]

    low = lanes(CHUNK) < 64

    def tile(r):
        return turned[CHUNK * (r + 1) : CHUNK * (r + 2), :]

    for d in range(SRC):
        for q in range(6):
            pay_ref[d, q] = tile(d * ROWS + q).astype(BF16)
        edge = jnp.where(low, tile(d * ROWS - 1), tile(d * ROWS + 6))
        pay_ref[d, 6] = edge.astype(BF16)


def pack(s, part, latents, before):
    line = pl.BlockSpec((1, 128), lambda e: (0, 0))
    return pl.pallas_call(
        functools.partial(pack_kernel, s),
        grid=(PART // CHUNK,),
        in_specs=[SMEM, pl.BlockSpec((1, COLS, CHUNK, LAT), lambda e: (s, 0, e, 0))]
        + [line] * len(before),
        out_specs=[pl.BlockSpec((SRC, 7, CHUNK, 128), lambda e: (0, 0, e, 0)), line],
        out_shape=[
            jax.ShapeDtypeStruct((SRC, 8, PART, 128), BF16),
            jax.ShapeDtypeStruct((1, 128), F32),
        ],
        scratch_shapes=[
            pltpu.VMEM((COLS * CHUNK, 128), F32),
            pltpu.VMEM(((LAT + 8) * CHUNK, 128), F32),
        ],
        compiler_params=pltpu.CompilerParams(vmem_limit_bytes=LIMIT),
        name=f"pack_latents_{s}",
    )(part, latents, *before)


def halo_kernel(left_ref, first_ref, last_ref, right_ref, _, pay_ref):
    lane = lanes(PART)
    pad = jnp.zeros((PART, 128 - LAT), F32)
    near = [left_ref[0, 0], left_ref[0, 1], first_ref[0, 0], last_ref[0, 0],
            right_ref[0, 0], right_ref[0, 1]]
    near = [jnp.concatenate([col.astype(F32), pad], axis=1) for col in near]
    for d in range(SRC):
        halo = jnp.zeros((PART, 128), F32)
        for kind in range(6):
            own = (lane >= 16 * kind) & (lane < 16 * kind + 16)
            halo = jnp.where(own, roll(near[kind], 16 * kind + 2 - d * ROWS), halo)
        pay_ref[d, 0] = halo.astype(BF16)


def pack_halo(s, latents, left, right, pay):
    pair = (1, 2, PART, LAT)
    one = (1, 1, PART, LAT)
    return pl.pallas_call(
        halo_kernel,
        grid=(1,),
        in_specs=[
            pl.BlockSpec(pair, lambda e: (s, 0, 0, 0)),
            pl.BlockSpec(one, lambda e: (s, 0, 0, 0)),
            pl.BlockSpec(one, lambda e: (s, COLS - 1, 0, 0)),
            pl.BlockSpec(pair, lambda e: (s, 0, 0, 0)),
            ANY,
        ],
        out_specs=pl.BlockSpec((SRC, 1, PART, 128), lambda e: (0, 7, 0, 0)),
        out_shape=jax.ShapeDtypeStruct((SRC, 8, PART, 128), BF16),
        input_output_aliases={4: 0},
        compiler_params=pltpu.CompilerParams(vmem_limit_bytes=LIMIT),
        name=f"pack_halo_{s}",
    )(left, latents, latents, right, pay)


def weight_kernel(w_ref, o_ref):
    at = pl.multiple_of(pl.program_id(0) * C, 128)
    o_ref[:, pl.ds(at, C)] = w_ref[0, 0].T


def turn_weights(j, weights):
    taps = weights.reshape(2, TAPS, C, C)
    return pl.pallas_call(
        weight_kernel,
        grid=(TAPS,),
        in_specs=[pl.BlockSpec((1, 1, C, C), lambda t: (j, t, 0, 0))],
        out_specs=VMEM,
        out_shape=pltpu.VMEM((C, TAPS * C), BF16),
        compiler_params=pltpu.CompilerParams(vmem_limit_bytes=LIMIT),
        cost_estimate=pl.CostEstimate(
            flops=TAPS * 2 * C * C * 256, bytes_accessed=15_000_000, transcendentals=0
        ),
        name=f"turn_weights_{j}",
    )(taps)


def target_kernel(upper_ref, lower_ref, o_ref):
    o_ref[0, 0] = jnp.concatenate([upper_ref[0, 0], lower_ref[0, 0]], axis=0).T


def turn_target(target):
    block = (1, 1, COLS, C)
    return pl.pallas_call(
        target_kernel,
        grid=(2, 6),
        in_specs=[
            pl.BlockSpec(block, lambda s, q: (q, s, 0, 0)),
            pl.BlockSpec(block, lambda s, q: (q + 6, s, 0, 0)),
        ],
        out_specs=pl.BlockSpec((1, 1, C, 128), lambda s, q: (s, q, 0, 0)),
        out_shape=jax.ShapeDtypeStruct((2, 6, C, 128), BF16),
        compiler_params=pltpu.CompilerParams(vmem_limit_bytes=LIMIT),
        name="turn_target",
    )(target, target)


def in_vmem(x):
    return pltpu.with_memory_space_constraint(x, pltpu.VMEM)


def affine(sums_ref, par_ref, s, j, scale, offset):
    count = float(LAT * 1024 * WIDTH)
    row = jnp.sum(sums_ref[...], axis=0, keepdims=True)

    def of_channel(base):
        picked = jnp.where(members(C, 0, base), row, 0.0)
        return jnp.sum(picked, axis=1, keepdims=True) / count

    mean = of_channel(32 * s)
    spread = of_channel(64 + 32 * s) - mean * mean
    factor = lax.rsqrt(spread + 1e-05) * par_ref[:, 2 * j : 2 * j + 1]
    rest = par_ref[:, 2 * j + 1 : 2 * j + 2] - mean * factor
    scale[...] = jnp.broadcast_to(factor, scale.shape)
    offset[...] = jnp.broadcast_to(rest, offset.shape)


def spread_taps(xs, at, rows, tiles, edge, sides, part):
    lane = lanes(rows)
    low = lane < 64
    first = (lane == 0) | (lane == 64)
    last = (lane == 63) | (lane == 127)
    for q in range(-1, 7):
        if q == -1:
            tile = jnp.where(low, edge, roll(tiles[5], 64))
        elif q == 6:
            tile = jnp.where(low, roll(tiles[0], 64), edge)
        else:
            tile = tiles[q]
        side = sides[pl.ds(at, rows), 128 * (q + 1) : 128 * (q + 2)]
        taps = (jnp.where(first, side, roll(tile, 1)), tile, jnp.where(last, side, roll(tile, -1)))
        for k, tap in enumerate(taps):
            if q == -1:
                tap = jnp.where(low & (part == 0), 0.0, tap)
            elif q == 6:
                tap = jnp.where((~low) & (part == SRC - 1), 0.0, tap)
            xs[pl.ds(k * C + at, rows), 128 * (q + 1) : 128 * (q + 2)] = tap.astype(BF16)


def product(wv, xs, n):
    x = jnp.concatenate([xs[:, n + 128 * i : n + 128 * i + 256] for i in range(3)], axis=0)
    return jnp.dot(wv[...], x, preferred_element_type=F32)


def first_kernel(
    s, part_ref, sums_ref, par_ref, pick_ref, recv_hbm, wv, *rest,
):
    if s == 1:
        taps_ref, recv_other, before_sums, before_next, before_prev, *rest = rest
        hid, out_sums, to_next, to_prev, out_halo, *rest = rest
        xs, scale, offset, recv, sides, sems, other, xh = rest
    else:
        hid, out_sums, to_next, to_prev, *rest = rest
        xs, scale, offset, recv, sides, sems = rest
    fetch = pltpu.make_async_copy(recv_hbm, recv, sems.at[0])
    fetch.start()
    if s == 1:
        fetch_other = pltpu.make_async_copy(recv_other.at[:, 7], other, sems.at[1])
        fetch_other.start()
    part = part_ref[0]

    def act(x, a, o):
        return silu(x.astype(F32) * a + o)

    def halo_act(x):
        r = (lanes(C) & 15) - 2
        outside = ((part == 0) & (r < 0)) | ((part == SRC - 1) & (r >= ROWS))
        return jnp.where(outside, 0.0, act(x, scale[...], offset[...])).astype(BF16)

    if s == 1:
        affine(sums_ref, par_ref, 0, 0, scale, offset)
        fetch_other.wait()
        halo_other = halo_act(other[...].reshape(C, 128))
    affine(sums_ref, par_ref, s, 0, scale, offset)
    fetch.wait()
    halo = halo_act(recv[:, 7].reshape(C, 128))
    sides[...] = jnp.dot(halo, pick_ref[...], preferred_element_type=F32)
    if s == 1:
        both = jnp.concatenate([halo_other, halo], axis=1)
        for t in range(TAPS):
            picked = jnp.dot(both, taps_ref[:, 128 * t : 128 * t + 128], preferred_element_type=F32)
            xh[C * t : C * (t + 1), :] = picked.astype(BF16)

    @pl.loop(0, SRC)
    def _(b):
        at = pl.multiple_of(b * PART, PART)
        a, o = scale[pl.ds(at, PART), :], offset[pl.ds(at, PART), :]
        tiles = [act(recv[b, q], a, o) for q in range(7)]
        spread_taps(xs, at, PART, tiles[:6], tiles[6], sides, part)

    bias = par_ref[:, 5 + s : 6 + s]
    for n in range(0, 768, 256):
        hid[:, n : n + 256] = product(wv, xs, n) + bias
    if s == 1:
        halo = jnp.dot(wv[...], xh[...], preferred_element_type=F32)
        bias = jnp.where(lanes(C) < 32, par_ref[:, 5:6], par_ref[:, 6:7])
        out_halo[...] = (halo + bias).astype(BF16)

    row = jnp.zeros((1, 128), F32) if s == 0 else before_sums[0:1, :]
    for at in range(0, C, 128):
        pieces = [hid[at : at + 128, 128 * q : 128 * (q + 1)] for q in range(6)]
        for k in range(2):
            column = jnp.sum(sum(p * p if k else p for p in pieces), axis=1, keepdims=True)
            own = members(128, at, 64 * k + 32 * s)
            row += jnp.sum(jnp.where(own, column, 0.0), axis=0, keepdims=True)
        if s == 0:
            after, ahead = roll(pieces[5], 64), pieces[0]
        else:
            low = lanes(128) < 64
            after = jnp.where(low, before_next[at : at + 128, :].astype(F32), pieces[5])
            ahead = jnp.where(low, before_prev[at : at + 128, :].astype(F32), roll(pieces[0], 64))
        to_next[at : at + 128, :] = after.astype(BF16)
        to_prev[at : at + 128, :] = ahead.astype(BF16)
    out_sums[...] = jnp.broadcast_to(row, out_sums.shape)


def first_conv(s, part, sums, params, pick, recv, weights, before):
    tile = jax.ShapeDtypeStruct((C, 128), BF16)
    more = [VMEM, ANY, VMEM, VMEM, VMEM] if s == 1 else []
    return pl.pallas_call(
        functools.partial(first_kernel, s),
        in_specs=[SMEM, VMEM, VMEM, VMEM, ANY, VMEM] + more,
        out_specs=[VMEM] * (4 + s),
        out_shape=[
            pltpu.VMEM((C, 768), F32),
            jax.ShapeDtypeStruct((128, 128), F32),
        ]
        + [tile] * (2 + s),
        scratch_shapes=[
            pltpu.VMEM((3 * C, 1024), BF16),
            pltpu.VMEM((C, 128), F32),
            pltpu.VMEM((C, 128), F32),
            pltpu.VMEM((SRC, 8, PART, 128), BF16),
            pltpu.VMEM((C, 1024), F32),
            pltpu.SemaphoreType.DMA((2,)),
        ]
        + [pltpu.VMEM((SRC, PART, 128), BF16), pltpu.VMEM((TAPS * C, 128), BF16)][: 2 * s],
        compiler_params=pltpu.CompilerParams(vmem_limit_bytes=LIMIT),
        cost_estimate=pl.CostEstimate(
            flops=2 * 768 * C * C * 9, bytes_accessed=12_000_000, transcendentals=0
        ),
        name=f"first_conv_{s}",
    )(part, sums, params, pick, recv, in_vmem(weights), *before)


def second_kernel(
    part_ref, coef_ref, sums_ref, par_ref, pick_ref, near_ref, prev_ref, next_ref,
    hid0, hid1, wv, recv0, recv1, target_hbm,
    noise_hbm, out_ref,
    xs, lat, target, noise_out, sides, scale, offset, sems,
):
    copies = [
        pltpu.make_async_copy(recv0.at[:, 0:6], lat.at[0], sems.at[0]),
        pltpu.make_async_copy(target_hbm.at[0], target.at[0], sems.at[1]),
        pltpu.make_async_copy(recv1.at[:, 0:6], lat.at[1], sems.at[2]),
        pltpu.make_async_copy(target_hbm.at[1], target.at[1], sems.at[3]),
    ]
    for copy in copies:
        copy.start()
    part = part_ref[0]
    result = jnp.zeros((1, 128), F32)
    stores = []
    for s in range(2):
        hid = (hid0, hid1)[s]
        affine(sums_ref, par_ref, s, 1, scale, offset)
        halo = silu(near_ref[...].astype(F32) * scale[...] + offset[...]).astype(BF16)
        sides[...] = jnp.dot(halo, pick_ref[s], preferred_element_type=F32)

        @pl.loop(0, SRC)
        def _(b):
            at = pl.multiple_of(b * PART, PART)
            rows = pl.ds(at, PART)
            a, o = scale[rows, :], offset[rows, :]
            low = lanes(PART) < 64

            def act(x):
                return silu(x * a + o)

            tiles = [act(hid[rows, 128 * q : 128 * (q + 1)]) for q in range(6)]
            above, below = prev_ref[rows, :].astype(F32), next_ref[rows, :].astype(F32)
            if s == 0:
                edge = jnp.where(low, above, roll(below, 64))
            else:
                edge = jnp.where(low, roll(above, 64), below)
            spread_taps(xs, at, PART, tiles, act(edge), sides, part)

        copies[2 * s].wait()
        copies[2 * s + 1].wait()
        bias = par_ref[:, 4:5]
        keep, gain = coef_ref[2 * s], coef_ref[2 * s + 1]
        acc = jnp.zeros((8, 128), F32)
        for n in range(0, 768, 256):
            out = product(wv, xs, n) + bias
            for h in range(2):
                q = n // 128 + h
                mine = lat[s, :, q].reshape(C, 128).astype(F32)
                noise = (out[:, 128 * h : 128 * h + 128] + mine).astype(BF16)
                center = keep * mine + gain * noise.astype(F32)
                diff = target[s, q].astype(F32) - center
                acc += jnp.sum((diff * diff).reshape(C // 8, 8, 128), axis=0)
                plain = noise.T
                noise_out[s, q] = plain[0:64]
                noise_out[s, q + 6] = plain[64:128]
        store = pltpu.make_async_copy(noise_out.at[s], noise_hbm.at[:, s], sems.at[4 + s])
        store.start()
        stores.append(store)
        value = jnp.sum(acc, axis=(0, 1), keepdims=True)
        result = jnp.where(lanes(1) == s, value, result)
    out_ref[...] = jnp.broadcast_to(result, out_ref.shape)
    for store in stores:
        store.wait()


def second_conv(part, coef, sums, params, pick, tiles, hidden, weights, recv, target):
    return pl.pallas_call(
        second_kernel,
        in_specs=[SMEM, SMEM] + [VMEM] * 9 + [ANY] * 3,
        out_specs=[ANY, VMEM],
        out_shape=[
            jax.ShapeDtypeStruct((ROWS, 2, COLS, C), BF16),
            jax.ShapeDtypeStruct((128, 128), F32),
        ],
        scratch_shapes=[
            pltpu.VMEM((3 * C, 1024), BF16),
            pltpu.VMEM((2, SRC, 6, PART, 128), BF16),
            pltpu.VMEM((2, 6, C, 128), BF16),
            pltpu.VMEM((2, ROWS, COLS, C), BF16),
            pltpu.VMEM((C, 1024), F32),
            pltpu.VMEM((C, 128), F32),
            pltpu.VMEM((C, 128), F32),
            pltpu.SemaphoreType.DMA((6,)),
        ],
        compiler_params=pltpu.CompilerParams(vmem_limit_bytes=LIMIT),
        cost_estimate=pl.CostEstimate(
            flops=4 * 768 * C * C * 9, bytes_accessed=20_000_000, transcendentals=0
        ),
        name="second_conv",
    )(
        part, coef, sums, params, pick, *tiles, *[in_vmem(h) for h in hidden],
        in_vmem(weights), *recv, target,
    )


def time_embed(timesteps, time_w1, time_w2):
    half = time_w1.shape[0] // 2
    freqs = jnp.exp(-math.log(10000.0) * jnp.arange(half, dtype=F32) / half)
    angles = timesteps.astype(F32)[:, None] * freqs[None, :]
    features = jnp.concatenate([jnp.cos(angles), jnp.sin(angles)], axis=1)
    hidden = jax.nn.silu(jnp.dot(features, time_w1, precision=lax.Precision.HIGHEST))
    return jnp.dot(hidden, time_w2, precision=lax.Precision.HIGHEST)


def plan(steps):
    frac = steps.astype(F32) / 1000.0
    return jnp.cos((frac + 0.008) / 1.008 * (math.pi / 2.0)) ** 2


def everywhere(rows):
    got = lax.all_to_all(rows.reshape(128, 1, 128), ("lon", "ch"), 0, 0, tiled=True)
    return got.reshape(128, 128)


def ring(axis, step, wrap):
    size = lax.axis_size(axis)
    return [(i, (i + step) % size) for i in range(size) if wrap or 0 <= i + step < size]


def swap(array, axis):
    return lax.all_to_all(array, axis, split_axis=0, concat_axis=0, tiled=True)


def after(value, *others):
    return lax.optimization_barrier((value,) + others)[0]


def butterfly(x):
    for axis in ("lon", "ch"):
        step = 1
        while step < lax.axis_size(axis):
            pairs = [(i, i ^ step) for i in range(lax.axis_size(axis))]
            x = x + lax.ppermute(x, axis, pairs)
            step *= 2
    return x


def body(
    latents, next_latents, timesteps, resume_steps, conv_weights, conv_bias,
    norm_gain, norm_shift, time_w1, time_w2,
):
    part = lax.axis_index("ch").astype(jnp.int32).reshape(1)
    first_pick = jnp.asarray(side_lanes(lambda r: 16 + r + 2, lambda r: 64 + r + 2))
    second_pick = jnp.asarray(
        np.stack(
            [
                side_lanes(lambda r: halo_lane(s, 0, r), lambda r: halo_lane(s, 1, r))
                for s in range(2)
            ]
        )
    )
    tap_pick = jnp.asarray(halo_taps())

    cells = latents.transpose(1, 2, 3, 0)
    left = lax.ppermute(cells[:, COLS - 2 :], "lon", ring("lon", 1, True))
    right = lax.ppermute(cells[:, :2], "lon", ring("lon", -1, True))
    pay0, sums = pack(0, part, cells, ())
    pay0 = pack_halo(0, cells, left, right, pay0)
    recv0 = swap(pay0, "ch")
    pay1, sums = pack(1, part, after(cells, pay0), (sums,))
    pay1 = pack_halo(1, cells, left, right, pay1)
    conv_weights, time_w1, following = after((conv_weights, time_w1, next_latents), sums)
    sums = butterfly(sums)
    recv1 = swap(after(pay1, recv0), "ch")
    turned = [turn_weights(j, conv_weights) for j in range(2)]
    target = turn_target(following)

    temb = time_embed(timesteps, time_w1, time_w2)
    columns = [
        norm_gain[0], norm_shift[0], norm_gain[1], norm_shift[1], conv_bias[1],
        conv_bias[0] + temb[0], conv_bias[0] + temb[1],
    ]
    params = jnp.pad(jnp.stack(columns, axis=1), ((0, 0), (0, 128 - len(columns))))

    alpha = plan(timesteps)
    prior = plan(timesteps - resume_steps)
    variance = (1.0 - prior) / (1.0 - alpha) * (1.0 - alpha / prior)
    keep = (1.0 - prior) * jnp.sqrt(alpha / (prior * (1.0 - alpha)))
    ratio = jnp.sqrt(prior) / jnp.sqrt(alpha)
    coef = jnp.stack([ratio, keep - ratio * jnp.sqrt(1.0 - alpha)], axis=1).reshape(4)

    hid0, *before = first_conv(0, part, sums, params, first_pick, recv0, turned[0], ())
    hid1, sums, to_next, to_prev, near = first_conv(
        1, part, sums, params, first_pick, recv1, turned[0], (tap_pick, recv0, *before)
    )
    from_prev = lax.ppermute(to_next, "ch", ring("ch", 1, False))
    from_next = lax.ppermute(to_prev, "ch", ring("ch", -1, False))
    sums = everywhere(sums)
    noise, terms = second_conv(
        part, coef, sums, params, second_pick, (near, from_prev, from_next),
        (hid0, hid1), turned[1], (recv0, recv1), target,
    )
    squares = jnp.sum(everywhere(terms), axis=0)[:2]
    logprob = (
        -squares / (2.0 * variance) / float(LAT * 1024 * C)
        - 0.5 * jnp.log(variance)
        - 0.5 * math.log(2.0 * math.pi)
    )
    return (noise, logprob)


def solution(mesh):
    return jax.shard_map(
        body,
        mesh=mesh,
        in_specs=(
            P(None, None, "lon", "ch"),
            P("ch", None, "lon", None),
            P(), P(), P(), P(), P(), P(), P(), P(),
        ),
        out_specs=(P("ch", None, "lon", None), P()),
        check_vma=False,
    )
```

```python
import functools
import math

import jax
import jax.numpy as jnp
import numpy as np
from jax import lax
from jax.experimental import pallas as pl
from jax.experimental.pallas import tpu as pltpu
from jax.sharding import PartitionSpec as P

GROUPS = 32
C = 640
LAT = 96
ROWS = 12
COLS = 64
SRC = 8
PART = C // SRC
WIDTH = C // GROUPS
TAPS = 9
F32 = jnp.float32
BF16 = jnp.bfloat16
VMEM = pl.BlockSpec(memory_space=pltpu.VMEM)
SMEM = pl.BlockSpec(memory_space=pltpu.SMEM)
ANY = pl.BlockSpec(memory_space=pl.ANY)
CHUNK = 16
LIMIT = 56 * 2**20
SUMS = 96


def roll(x, by):
    by %= 128
    return x if by == 0 else pltpu.roll(x, by, 1)


def side_lanes(of_left, of_right):
    out = np.zeros((128, 1024), np.float32)
    for q in range(-1, 7):
        at = 128 * (q + 1)
        out[of_left(q), at] = 1
        out[of_left(q + 6), at + 64] = 1
        out[of_right(q), at + 63] = 1
        out[of_right(q + 6), at + 127] = 1
    return out.astype(BF16)


def halo_lane(s, side, row):
    return 32 * s + 16 * side + row + 1


def halo_taps():
    out = np.zeros((256, TAPS * 128), np.float32)
    for i in range(3):
        for k in range(3):
            for s in range(2):
                for side in range(2):
                    for row in range(-1, 13):
                        source = 128 * s + 16 * (3 * side + k) + row + i - 1 + 2
                        out[source, 128 * (3 * i + k) + halo_lane(s, side, row)] = 1
    return out.astype(BF16)


def lanes(rows):
    return lax.broadcasted_iota(jnp.int32, (rows, 128), 1)


def members(rows, first, base):
    chan = lax.broadcasted_iota(jnp.int32, (rows, 128), 0) + first
    low = (lanes(rows) - base) * WIDTH
    return (chan >= low) & (chan < low + WIDTH)


def silu(x):
    return 0.5 * x * (1.0 + jnp.tanh(0.5 * x))


def sums_kernel(x_ref, sums_ref, first_ref, last_ref):
    s, c = pl.program_id(0), pl.program_id(1)
    x = x_ref[0].astype(F32)

    @pl.when((s == 0) & (c == 0))
    def _():
        sums_ref[...] = jnp.zeros_like(sums_ref)

    @pl.when(c == 0)
    def _():
        first_ref[0] = x_ref[0, 0:2]

    @pl.when(c == COLS // 16 - 1)
    def _():
        last_ref[0] = x_ref[0, 14:16]

    row = jnp.zeros((1, 128), F32)
    for k in range(2):
        column = jnp.sum(jnp.sum(x * x if k else x, axis=0), axis=1, keepdims=True)
        own = members(PART, 0, 64 * k + 32 * s)
        row += jnp.sum(jnp.where(own, column, 0.0), axis=0, keepdims=True)
    sums_ref[...] += jnp.broadcast_to(row, sums_ref.shape)


def local_sums(latents):
    pair = pl.BlockSpec((1, 2, PART, LAT), lambda s, c: (s, 0, 0, 0))
    return pl.pallas_call(
        sums_kernel,
        grid=(2, COLS // 16),
        in_specs=[pl.BlockSpec((1, 16, PART, LAT), lambda s, c: (s, c, 0, 0))],
        out_specs=[pl.BlockSpec((16, 128), lambda s, c: (0, 0)), pair, pair],
        out_shape=[
            jax.ShapeDtypeStruct((16, 128), F32),
            jax.ShapeDtypeStruct((2, 2, PART, LAT), BF16),
            jax.ShapeDtypeStruct((2, 2, PART, LAT), BF16),
        ],
        compiler_params=pltpu.CompilerParams(vmem_limit_bytes=LIMIT),
        name="local_sums",
    )(latents)


def pack_kernel(main_ref, pay_ref, taken, turned):
    @pl.when((pl.program_id(0) == 0) & (pl.program_id(1) == 0))
    def _():
        taken[...] = jnp.zeros_like(taken)
        turned[...] = jnp.zeros_like(turned)

    taken[:, 0:LAT] = main_ref[0].astype(F32).reshape(COLS * CHUNK, LAT)
    for j in range(CHUNK):
        plain = taken[pl.ds(j, COLS, stride=CHUNK), :]
        both = jnp.concatenate([plain, roll(plain, -6)], axis=0).T
        turned[pl.ds(CHUNK + j, LAT, stride=CHUNK), :] = both[0:LAT, :]

    low = lanes(CHUNK) < 64

    def tile(r):
        return turned[CHUNK * (r + 1) : CHUNK * (r + 2), :]

    for d in range(SRC):
        for q in range(6):
            pay_ref[d, q] = tile(d * ROWS + q).astype(BF16)
        edge = jnp.where(low, tile(d * ROWS - 1), tile(d * ROWS + 6))
        pay_ref[d, 6] = edge.astype(BF16)
        pay_ref[d, 7] = jnp.zeros((CHUNK, 128), BF16)


def pack(latents):
    return pl.pallas_call(
        pack_kernel,
        grid=(2, PART // CHUNK),
        in_specs=[pl.BlockSpec((1, COLS, CHUNK, LAT), lambda s, e: (s, 0, e, 0))],
        out_specs=pl.BlockSpec((SRC, 8, CHUNK, 128), lambda s, e: (0, s, e, 0)),
        out_shape=jax.ShapeDtypeStruct((SRC, 16, PART, 128), BF16),
        scratch_shapes=[
            pltpu.VMEM((COLS * CHUNK, 128), F32),
            pltpu.VMEM(((LAT + 8) * CHUNK, 128), F32),
        ],
        compiler_params=pltpu.CompilerParams(vmem_limit_bytes=LIMIT),
        cost_estimate=pl.CostEstimate(
            flops=1_000_000_000, bytes_accessed=8_000_000, transcendentals=0
        ),
        name="pack_latents",
    )(latents)


def halo_kernel(sums_ref, left_ref, first_ref, last_ref, right_ref, _, pay_ref):
    s = pl.program_id(0)
    lane = lanes(PART)
    pad = jnp.zeros((PART, 128 - LAT), F32)
    near = [left_ref[0, 0], left_ref[0, 1], first_ref[0, 0], last_ref[0, 0],
            right_ref[0, 0], right_ref[0, 1]]
    near = [jnp.concatenate([col.astype(F32), pad], axis=1) for col in near]
    row = jnp.sum(sums_ref[...], axis=0, keepdims=True)
    carried = jnp.zeros((PART, 128), F32)
    for k in range(2):
        own = members(PART, 0, 64 * k + 32 * s)
        value = jnp.sum(jnp.where(own, row, 0.0), axis=1, keepdims=True)
        for piece in range(3):
            part = value.astype(BF16).astype(F32)
            carried = jnp.where(lane == SUMS + 3 * k + piece, part, carried)
            value = value - part
    for d in range(SRC):
        halo = carried
        for kind in range(6):
            own = (lane >= 16 * kind) & (lane < 16 * kind + 16)
            halo = jnp.where(own, roll(near[kind], 16 * kind + 2 - d * ROWS), halo)
        pay_ref[d, 0] = halo.astype(BF16)


def pack_halo(sums, latents, left, right, pay):
    pair = (1, 2, PART, LAT)
    one = (1, 1, PART, LAT)
    return pl.pallas_call(
        halo_kernel,
        grid=(2,),
        in_specs=[
            pl.BlockSpec((16, 128), lambda s: (0, 0)),
            pl.BlockSpec(pair, lambda s: (s, 0, 0, 0)),
            pl.BlockSpec(one, lambda s: (s, 0, 0, 0)),
            pl.BlockSpec(one, lambda s: (s, COLS - 1, 0, 0)),
            pl.BlockSpec(pair, lambda s: (s, 0, 0, 0)),
            ANY,
        ],
        out_specs=pl.BlockSpec((SRC, 1, PART, 128), lambda s: (0, 8 * s + 7, 0, 0)),
        out_shape=jax.ShapeDtypeStruct((SRC, 16, PART, 128), BF16),
        input_output_aliases={5: 0},
        compiler_params=pltpu.CompilerParams(vmem_limit_bytes=LIMIT),
        name="pack_halo",
    )(sums, left, latents, latents, right, pay)


def weight_kernel(w_ref, o_ref):
    o_ref[...] = w_ref[0, 0].T


def turn_weights(j, weights):
    taps = weights.reshape(2, TAPS, C, C)
    return pl.pallas_call(
        weight_kernel,
        grid=(TAPS,),
        in_specs=[pl.BlockSpec((1, 1, C, C), lambda t: (j, t, 0, 0))],
        out_specs=pl.BlockSpec((C, C), lambda t: (0, t)),
        out_shape=jax.ShapeDtypeStruct((C, TAPS * C), BF16),
        compiler_params=pltpu.CompilerParams(vmem_limit_bytes=LIMIT),
        cost_estimate=pl.CostEstimate(
            flops=TAPS * 2 * C * C * 256, bytes_accessed=15_000_000, transcendentals=0
        ),
        name=f"turn_weights_{j}",
    )(taps)


def target_kernel(upper_ref, lower_ref, o_ref):
    o_ref[0, 0] = jnp.concatenate([upper_ref[0, 0], lower_ref[0, 0]], axis=0).T


def turn_target(target):
    block = (1, 1, COLS, C)
    return pl.pallas_call(
        target_kernel,
        grid=(2, 6),
        in_specs=[
            pl.BlockSpec(block, lambda s, q: (q, s, 0, 0)),
            pl.BlockSpec(block, lambda s, q: (q + 6, s, 0, 0)),
        ],
        out_specs=pl.BlockSpec((1, 1, C, 128), lambda s, q: (s, q, 0, 0)),
        out_shape=jax.ShapeDtypeStruct((2, 6, C, 128), BF16),
        compiler_params=pltpu.CompilerParams(vmem_limit_bytes=LIMIT),
        name="turn_target",
    )(target, target)


def affine(total, square, par_ref, j, scale, offset):
    count = float(LAT * 1024 * WIDTH)
    mean = total / count
    spread = square / count - mean * mean
    factor = lax.rsqrt(spread + 1e-05) * par_ref[:, 2 * j : 2 * j + 1]
    rest = par_ref[:, 2 * j + 1 : 2 * j + 2] - mean * factor
    scale[...] = jnp.broadcast_to(factor, scale.shape)
    offset[...] = jnp.broadcast_to(rest, offset.shape)


def spread_taps(xs, at, tiles, edge, sides, part):
    rows = PART
    lane = lanes(rows)
    low = lane < 64
    first = (lane == 0) | (lane == 64)
    last = (lane == 63) | (lane == 127)
    for q in range(-1, 7):
        if q == -1:
            tile = jnp.where(low, edge, roll(tiles[5], 64))
        elif q == 6:
            tile = jnp.where(low, roll(tiles[0], 64), edge)
        else:
            tile = tiles[q]
        side = sides[pl.ds(at, rows), 128 * (q + 1) : 128 * (q + 2)]
        taps = (jnp.where(first, side, roll(tile, 1)), tile, jnp.where(last, side, roll(tile, -1)))
        for k, tap in enumerate(taps):
            if q == -1:
                tap = jnp.where(low & (part == 0), 0.0, tap)
            elif q == 6:
                tap = jnp.where((~low) & (part == SRC - 1), 0.0, tap)
            xs[pl.ds(k * C + at, rows), 128 * (q + 1) : 128 * (q + 2)] = tap.astype(BF16)


def product(wv, xs, n):
    x = jnp.concatenate([xs[:, n + 128 * i : n + 128 * i + 256] for i in range(3)], axis=0)
    return jnp.dot(wv[...], x, preferred_element_type=F32)


def first_kernel(
    part_ref, par_ref, pick_ref, taps_ref, recv_hbm, w_hbm,
    hid_hbm, out_sums, to_next, to_prev, out_halo,
    xs, wv, scale, offset, recv, hid, sides, xh, sems,
):
    fetches = [
        pltpu.make_async_copy(recv_hbm.at[:, 8 * s : 8 * s + 8], recv.at[s], sems.at[s])
        for s in range(2)
    ]
    weights = pltpu.make_async_copy(w_hbm, wv, sems.at[2])
    for copy in (*fetches, weights):
        copy.start()
    part = part_ref[0]
    lane = lanes(C)

    def act(x, a, o):
        return silu(x.astype(F32) * a + o)

    def columns(s):
        fetches[s].wait()
        tile = recv[s, :, 7].reshape(C, 128).astype(F32)
        total, square = (
            jnp.sum(jnp.where((lane >= at) & (lane < at + 3), tile, 0.0), axis=1, keepdims=True)
            for at in (SUMS, SUMS + 3)
        )
        affine(total, square, par_ref, 0, scale.at[s], offset.at[s])
        r = (lane & 15) - 2
        unused = lane >= SUMS
        outside = ((part == 0) & (r < 0)) | ((part == SRC - 1) & (r >= ROWS)) | unused
        x = jnp.where(unused, 0.0, tile)
        halo = jnp.where(outside, 0.0, act(x, scale[s], offset[s])).astype(BF16)
        sides[s] = jnp.dot(halo, pick_ref[...], preferred_element_type=F32)
        return halo

    def prepare(s, b):
        at = b * PART if isinstance(b, int) else pl.multiple_of(b * PART, PART)
        a, o = scale[s, pl.ds(at, PART), :], offset[s, pl.ds(at, PART), :]
        tiles = [act(recv[s, b, q], a, o) for q in range(7)]
        spread_taps(xs.at[s], at, tiles[:6], tiles[6], sides.at[s], part)

    halo = columns(0)

    @pl.loop(0, SRC)
    def _(b):
        prepare(0, b)

    both = jnp.concatenate([halo, columns(1)], axis=1)
    for t in range(TAPS):
        picked = jnp.dot(both, taps_ref[:, 128 * t : 128 * t + 128], preferred_element_type=F32)
        xh[C * t : C * (t + 1), :] = picked.astype(BF16)

    weights.wait()
    stores = []

    def put(s):
        store = pltpu.make_async_copy(hid.at[s], hid_hbm.at[s], sems.at[s])
        store.start()
        stores.append(store)

    for c, blocks in enumerate(((0, 1, 2), (3, 4, 5), (6, 7))):
        n = 256 * c
        hid[0, :, n : n + 256] = product(wv, xs.at[0], n) + par_ref[:, 5:6]
        for b in blocks:
            prepare(1, b)
    put(0)
    for n in range(0, 768, 256):
        hid[1, :, n : n + 256] = product(wv, xs.at[1], n) + par_ref[:, 6:7]
    put(1)
    halo = jnp.dot(wv[...], xh[...], preferred_element_type=F32)
    bias = jnp.where(lane < 32, par_ref[:, 5:6], par_ref[:, 6:7])
    out_halo[...] = (halo + bias).astype(BF16)

    row = jnp.zeros((1, 128), F32)
    low = lanes(128) < 64
    for at in range(0, C, 128):
        for s in range(2):
            pieces = [hid[s, at : at + 128, 128 * q : 128 * (q + 1)] for q in range(6)]
            for k in range(2):
                column = jnp.sum(sum(p * p if k else p for p in pieces), axis=1, keepdims=True)
                own = members(128, at, 64 * k + 32 * s)
                row += jnp.sum(jnp.where(own, column, 0.0), axis=0, keepdims=True)
        start, end = hid.at[:, at : at + 128, 0:128], hid.at[:, at : at + 128, 640:768]
        to_next[at : at + 128, :] = jnp.where(low, roll(end[0], 64), end[1]).astype(BF16)
        to_prev[at : at + 128, :] = jnp.where(low, start[0], roll(start[1], 64)).astype(BF16)
    out_sums[...] = jnp.broadcast_to(row, out_sums.shape)
    for store in stores:
        store.wait()


def first_conv(part, params, pick, taps, recv, weights):
    tile = jax.ShapeDtypeStruct((C, 128), BF16)
    return pl.pallas_call(
        first_kernel,
        in_specs=[SMEM, VMEM, VMEM, VMEM, ANY, ANY],
        out_specs=[ANY] + [VMEM] * 4,
        out_shape=[
            jax.ShapeDtypeStruct((2, C, 768), F32),
            jax.ShapeDtypeStruct((128, 128), F32),
            tile, tile, tile,
        ],
        scratch_shapes=[
            pltpu.VMEM((2, 3 * C, 1024), BF16),
            pltpu.VMEM((C, TAPS * C), BF16),
            pltpu.VMEM((2, C, 128), F32),
            pltpu.VMEM((2, C, 128), F32),
            pltpu.VMEM((2, SRC, 8, PART, 128), BF16),
            pltpu.VMEM((2, C, 768), F32),
            pltpu.VMEM((2, C, 1024), F32),
            pltpu.VMEM((TAPS * C, 128), BF16),
            pltpu.SemaphoreType.DMA((3,)),
        ],
        compiler_params=pltpu.CompilerParams(vmem_limit_bytes=LIMIT),
        cost_estimate=pl.CostEstimate(
            flops=4 * 768 * C * C * 9, bytes_accessed=20_000_000, transcendentals=0
        ),
        name="first_conv",
    )(part, params, pick, taps, recv, weights)


def second_kernel(
    part_ref, coef_ref, sums_ref, par_ref, pick_ref, near_ref, prev_ref, next_ref,
    hid_hbm, w_hbm, recv_hbm, target_hbm,
    noise_hbm, out_ref,
    xs, wv, hid, lat, target, noise_out, sides, scale, offset, sems,
):
    weights = pltpu.make_async_copy(w_hbm, wv, sems.at[8])
    fetches, later = [], []
    for s in range(2):
        fetches.append(pltpu.make_async_copy(hid_hbm.at[s], hid.at[s], sems.at[s]))
        tiles = recv_hbm.at[:, 8 * s : 8 * s + 6]
        later.append(pltpu.make_async_copy(tiles, lat.at[s], sems.at[2 + s]))
        later.append(pltpu.make_async_copy(target_hbm.at[s], target.at[s], sems.at[4 + s]))
    for copy in (fetches[0], weights, fetches[1], *later):
        copy.start()
    part = part_ref[0]
    row = jnp.sum(sums_ref[...], axis=0, keepdims=True)
    low = lanes(PART) < 64

    def columns(s):
        total, square = (
            jnp.sum(jnp.where(members(C, 0, base), row, 0.0), axis=1, keepdims=True)
            for base in (32 * s, 64 + 32 * s)
        )
        affine(total, square, par_ref, 1, scale.at[s], offset.at[s])
        halo = silu(near_ref[...].astype(F32) * scale[s] + offset[s]).astype(BF16)
        sides[s] = jnp.dot(halo, pick_ref[s], preferred_element_type=F32)
        fetches[s].wait()

    def prepare(s, b):
        at = b * PART if isinstance(b, int) else pl.multiple_of(b * PART, PART)
        rows = pl.ds(at, PART)
        a, o = scale[s, rows, :], offset[s, rows, :]

        def act(x):
            return silu(x * a + o)

        tiles = [act(hid[s, rows, 128 * q : 128 * (q + 1)]) for q in range(6)]
        above, below = prev_ref[rows, :].astype(F32), next_ref[rows, :].astype(F32)
        if s == 0:
            edge = jnp.where(low, above, roll(below, 64))
        else:
            edge = jnp.where(low, roll(above, 64), below)
        spread_taps(xs.at[s], at, tiles, act(edge), sides.at[s], part)

    def finish(s, n, acc):
        keep, gain = coef_ref[2 * s], coef_ref[2 * s + 1]
        out = product(wv, xs.at[s], n) + par_ref[:, 4:5]
        for h in range(2):
            q = n // 128 + h
            mine = lat[s, :, q].reshape(C, 128).astype(F32)
            noise = (out[:, 128 * h : 128 * h + 128] + mine).astype(BF16)
            center = keep * mine + gain * noise.astype(F32)
            diff = target[s, q].astype(F32) - center
            acc += jnp.sum((diff * diff).reshape(C // 8, 8, 128), axis=0)
            plain = noise.T
            noise_out[s, q] = plain[0:64]
            noise_out[s, q + 6] = plain[64:128]
        return acc

    columns(0)

    @pl.loop(0, SRC)
    def _(b):
        prepare(0, b)

    columns(1)
    weights.wait()
    for copy in later:
        copy.wait()
    result = jnp.zeros((1, 128), F32)
    stores = []
    for s in range(2):
        acc = jnp.zeros((8, 128), F32)
        for c, blocks in enumerate(((0, 1, 2), (3, 4, 5), (6, 7))):
            acc = finish(s, 256 * c, acc)
            if s == 0:
                for b in blocks:
                    prepare(1, b)
        store = pltpu.make_async_copy(noise_out.at[s], noise_hbm.at[:, s], sems.at[6 + s])
        store.start()
        stores.append(store)
        value = jnp.sum(acc, axis=(0, 1), keepdims=True)
        result = jnp.where(lanes(1) == s, value, result)
    out_ref[...] = jnp.broadcast_to(result, out_ref.shape)
    for store in stores:
        store.wait()


def second_conv(part, coef, sums, params, pick, tiles, hidden, weights, recv, target):
    return pl.pallas_call(
        second_kernel,
        in_specs=[SMEM, SMEM] + [VMEM] * 6 + [ANY] * 4,
        out_specs=[ANY, VMEM],
        out_shape=[
            jax.ShapeDtypeStruct((ROWS, 2, COLS, C), BF16),
            jax.ShapeDtypeStruct((128, 128), F32),
        ],
        scratch_shapes=[
            pltpu.VMEM((2, 3 * C, 1024), BF16),
            pltpu.VMEM((C, TAPS * C), BF16),
            pltpu.VMEM((2, C, 768), F32),
            pltpu.VMEM((2, SRC, 6, PART, 128), BF16),
            pltpu.VMEM((2, 6, C, 128), BF16),
            pltpu.VMEM((2, ROWS, COLS, C), BF16),
            pltpu.VMEM((2, C, 1024), F32),
            pltpu.VMEM((2, C, 128), F32),
            pltpu.VMEM((2, C, 128), F32),
            pltpu.SemaphoreType.DMA((9,)),
        ],
        compiler_params=pltpu.CompilerParams(vmem_limit_bytes=LIMIT),
        cost_estimate=pl.CostEstimate(
            flops=4 * 768 * C * C * 9, bytes_accessed=20_000_000, transcendentals=0
        ),
        name="second_conv",
    )(part, coef, sums, params, pick, *tiles, hidden, weights, recv, target)


def time_embed(timesteps, time_w1, time_w2):
    half = time_w1.shape[0] // 2
    freqs = jnp.exp(-math.log(10000.0) * jnp.arange(half, dtype=F32) / half)
    angles = timesteps.astype(F32)[:, None] * freqs[None, :]
    features = jnp.concatenate([jnp.cos(angles), jnp.sin(angles)], axis=1)
    hidden = jax.nn.silu(jnp.dot(features, time_w1, precision=lax.Precision.HIGHEST))
    return jnp.dot(hidden, time_w2, precision=lax.Precision.HIGHEST)


def plan(steps):
    frac = steps.astype(F32) / 1000.0
    return jnp.cos((frac + 0.008) / 1.008 * (math.pi / 2.0)) ** 2


def everywhere(rows, axes):
    got = lax.all_to_all(rows.reshape(-1, 1, 128), axes, 0, 0, tiled=True)
    return got.reshape(-1, 128)


def ring(axis, step, wrap):
    size = lax.axis_size(axis)
    return [(i, (i + step) % size) for i in range(size) if wrap or 0 <= i + step < size]


def swap(array, axis):
    return lax.all_to_all(array, axis, split_axis=0, concat_axis=0, tiled=True)


def after(value, *others):
    return lax.optimization_barrier((value,) + others)[0]


def body(
    latents, next_latents, timesteps, resume_steps, conv_weights, conv_bias,
    norm_gain, norm_shift, time_w1, time_w2,
):
    part = lax.axis_index("ch").astype(jnp.int32).reshape(1)
    first_pick = jnp.asarray(side_lanes(lambda r: 16 + r + 2, lambda r: 64 + r + 2))
    second_pick = jnp.asarray(
        np.stack(
            [
                side_lanes(lambda r: halo_lane(s, 0, r), lambda r: halo_lane(s, 1, r))
                for s in range(2)
            ]
        )
    )
    tap_pick = jnp.asarray(halo_taps())

    cells = latents.transpose(1, 2, 3, 0)
    sums, first, last = local_sums(cells)
    sums = everywhere(sums, "lon")
    left = lax.ppermute(last, "lon", ring("lon", 1, True))
    right = lax.ppermute(first, "lon", ring("lon", -1, True))
    pay = pack(after(cells, first))
    pay = pack_halo(sums, cells, left, right, pay)
    recv = swap(pay, "ch")
    conv_weights, time_w1, following = after((conv_weights, time_w1, next_latents), pay)
    turned = [turn_weights(j, conv_weights) for j in range(2)]
    target = turn_target(following)

    temb = time_embed(timesteps, time_w1, time_w2)
    columns = [
        norm_gain[0], norm_shift[0], norm_gain[1], norm_shift[1], conv_bias[1],
        conv_bias[0] + temb[0], conv_bias[0] + temb[1],
    ]
    params = jnp.pad(jnp.stack(columns, axis=1), ((0, 0), (0, 128 - len(columns))))

    alpha = plan(timesteps)
    prior = plan(timesteps - resume_steps)
    variance = (1.0 - prior) / (1.0 - alpha) * (1.0 - alpha / prior)
    keep = (1.0 - prior) * jnp.sqrt(alpha / (prior * (1.0 - alpha)))
    ratio = jnp.sqrt(prior) / jnp.sqrt(alpha)
    coef = jnp.stack([ratio, keep - ratio * jnp.sqrt(1.0 - alpha)], axis=1).reshape(4)

    hidden, sums, to_next, to_prev, near = first_conv(
        part, params, first_pick, tap_pick, recv, turned[0]
    )
    from_prev = lax.ppermute(to_next, "ch", ring("ch", 1, False))
    from_next = lax.ppermute(to_prev, "ch", ring("ch", -1, False))
    sums = everywhere(sums, ("lon", "ch"))
    noise, terms = second_conv(
        part, coef, sums, params, second_pick, (near, from_prev, from_next),
        hidden, turned[1], recv, target,
    )
    squares = jnp.sum(everywhere(terms, ("lon", "ch")), axis=0)[:2]
    logprob = (
        -squares / (2.0 * variance) / float(LAT * 1024 * C)
        - 0.5 * jnp.log(variance)
        - 0.5 * math.log(2.0 * math.pi)
    )
    return (noise, logprob)


def solution(mesh):
    return jax.shard_map(
        body,
        mesh=mesh,
        in_specs=(
            P(None, None, "lon", "ch"),
            P("ch", None, "lon", None),
            P(), P(), P(), P(), P(), P(), P(), P(),
        ),
        out_specs=(P("ch", None, "lon", None), P()),
        check_vma=False,
    )
```

```python
import functools
import math

import jax
import jax.numpy as jnp
import numpy as np
from jax import lax
from jax.experimental import pallas as pl
from jax.experimental.pallas import tpu as pltpu
from jax.sharding import PartitionSpec as P

GROUPS = 32
C = 640
LAT = 96
ROWS = 12
COLS = 64
SRC = 8
PART = C // SRC
WIDTH = C // GROUPS
TAPS = 9
F32 = jnp.float32
BF16 = jnp.bfloat16
VMEM = pl.BlockSpec(memory_space=pltpu.VMEM)
SMEM = pl.BlockSpec(memory_space=pltpu.SMEM)
ANY = pl.BlockSpec(memory_space=pl.ANY)
CHUNK = 16
LIMIT = 56 * 2**20


def roll(x, by):
    by %= 128
    return x if by == 0 else pltpu.roll(x, by, 1)


def side_lanes(of_left, of_right):
    out = np.zeros((128, 1024), np.float32)
    for q in range(-1, 7):
        at = 128 * (q + 1)
        out[of_left(q), at] = 1
        out[of_left(q + 6), at + 64] = 1
        out[of_right(q), at + 63] = 1
        out[of_right(q + 6), at + 127] = 1
    return out.astype(BF16)


def halo_lane(s, side, row):
    return 32 * s + 16 * side + row + 1


def halo_taps():
    out = np.zeros((256, TAPS * 128), np.float32)
    for i in range(3):
        for k in range(3):
            for s in range(2):
                for side in range(2):
                    for row in range(-1, 13):
                        source = 128 * s + 16 * (3 * side + k) + row + i - 1 + 2
                        out[source, 128 * (3 * i + k) + halo_lane(s, side, row)] = 1
    return out.astype(BF16)


def lanes(rows):
    return lax.broadcasted_iota(jnp.int32, (rows, 128), 1)


def members(rows, first, base):
    chan = lax.broadcasted_iota(jnp.int32, (rows, 128), 0) + first
    low = (lanes(rows) - base) * WIDTH
    return (chan >= low) & (chan < low + WIDTH)


def silu(x):
    return 0.5 * x * (1.0 + jnp.tanh(0.5 * x))


PARAMS = pltpu.CompilerParams(vmem_limit_bytes=LIMIT)


def sums_kernel(part_ref, cells_hbm, sums_ref, first_ref, last_ref, x, sems):
    half = COLS // 2
    copies = []
    for s in range(2):
        for c in range(2):
            cut = slice(c * half, (c + 1) * half)
            copies.append(
                pltpu.make_async_copy(cells_hbm.at[s, cut], x.at[s, cut], sems.at[2 * s + c])
            )
            copies[-1].start()
    row = jnp.zeros((1, 128), F32)
    for s in range(2):
        total = jnp.zeros((PART, LAT), F32)
        square = jnp.zeros((PART, LAT), F32)
        for c in range(2):
            copies[2 * s + c].wait()

            def add(i, carry):
                total, square = carry
                for j in range(4):
                    v = x[s, c * half + 4 * i + j].astype(F32)
                    total, square = total + v, square + v * v
                return total, square

            total, square = lax.fori_loop(0, half // 4, add, (total, square))
        for k, acc in enumerate((total, square)):
            column = jnp.sum(acc, axis=1, keepdims=True)
            own = members(PART, part_ref[0] * PART, 64 * k + 32 * s)
            row += jnp.sum(jnp.where(own, column, 0.0), axis=0, keepdims=True)
        first_ref[s] = x[s, 0:2]
        last_ref[s] = x[s, COLS - 2 : COLS]
    sums_ref[...] = row


def local_sums(part, cells):
    return pl.pallas_call(
        sums_kernel,
        in_specs=[SMEM, ANY],
        out_specs=[VMEM] * 3,
        out_shape=[
            jax.ShapeDtypeStruct((1, 128), F32),
            jax.ShapeDtypeStruct((2, 2, PART, LAT), BF16),
            jax.ShapeDtypeStruct((2, 2, PART, LAT), BF16),
        ],
        scratch_shapes=[pltpu.VMEM((2, COLS, PART, LAT), BF16), pltpu.SemaphoreType.DMA((4,))],
        compiler_params=PARAMS,
        name="local_sums",
    )(part, cells)


def pack_kernel(cells_hbm, pay_hbm, x, out, taken, turned, sems):
    fetches = [pltpu.make_async_copy(cells_hbm.at[s], x.at[s], sems.at[s]) for s in range(2)]
    for copy in fetches:
        copy.start()
    taken[...] = jnp.zeros_like(taken)
    turned[...] = jnp.zeros_like(turned)
    low = lanes(CHUNK) < 64

    def tile(r):
        return turned[CHUNK * (r + 1) : CHUNK * (r + 2), :]

    stores = []
    for s in range(2):
        fetches[s].wait()

        @pl.loop(0, PART // CHUNK)
        def _(e):
            own = pl.ds(pl.multiple_of(e * CHUNK, CHUNK), CHUNK)
            taken[:, 0:LAT] = x[s, :, own, :].astype(F32).reshape(COLS * CHUNK, LAT)
            for j in range(CHUNK):
                plain = taken[pl.ds(j, COLS, stride=CHUNK), :]
                both = jnp.concatenate([plain, roll(plain, -6)], axis=0).T
                turned[pl.ds(CHUNK + j, LAT, stride=CHUNK), :] = both[0:LAT, :]
            for d in range(SRC):
                for q in range(6):
                    out[s, d, q, own, :] = tile(d * ROWS + q).astype(BF16)
                edge = jnp.where(low, tile(d * ROWS - 1), tile(d * ROWS + 6))
                out[s, d, 6, own, :] = edge.astype(BF16)

        store = pltpu.make_async_copy(out.at[s], pay_hbm.at[:, 8 * s : 8 * s + 7], sems.at[2 + s])
        store.start()
        stores.append(store)
    for store in stores:
        store.wait()


def pack(cells):
    return pl.pallas_call(
        pack_kernel,
        in_specs=[ANY],
        out_specs=ANY,
        out_shape=jax.ShapeDtypeStruct((SRC, 16, PART, 128), BF16),
        scratch_shapes=[
            pltpu.VMEM((2, COLS, PART, LAT), BF16),
            pltpu.VMEM((2, SRC, 7, PART, 128), BF16),
            pltpu.VMEM((COLS * CHUNK, 128), F32),
            pltpu.VMEM(((LAT + 8) * CHUNK, 128), F32),
            pltpu.SemaphoreType.DMA((4,)),
        ],
        compiler_params=PARAMS,
        cost_estimate=pl.CostEstimate(
            flops=1_000_000_000, bytes_accessed=8_000_000, transcendentals=0
        ),
        name="pack_latents",
    )(cells)


def halo_kernel(first_ref, last_ref, left_ref, right_ref, _, pay_hbm, out, sems):
    lane = lanes(PART)
    pad = jnp.zeros((PART, 128 - LAT), F32)
    stores = []
    for s in range(2):
        near = [left_ref[s, 0], left_ref[s, 1], first_ref[s, 0], last_ref[s, 1],
                right_ref[s, 0], right_ref[s, 1]]
        near = [jnp.concatenate([col.astype(F32), pad], axis=1) for col in near]
        for d in range(SRC):
            halo = jnp.zeros((PART, 128), F32)
            for kind in range(6):
                own = (lane >= 16 * kind) & (lane < 16 * kind + 16)
                halo = jnp.where(own, roll(near[kind], 16 * kind + 2 - d * ROWS), halo)
            out[s, d] = halo.astype(BF16)
        store = pltpu.make_async_copy(out.at[s], pay_hbm.at[:, 8 * s + 7], sems.at[s])
        store.start()
        stores.append(store)
    for store in stores:
        store.wait()


def pack_halo(first, last, left, right, pay):
    return pl.pallas_call(
        halo_kernel,
        in_specs=[VMEM] * 4 + [ANY],
        out_specs=ANY,
        out_shape=jax.ShapeDtypeStruct((SRC, 16, PART, 128), BF16),
        scratch_shapes=[pltpu.VMEM((2, SRC, PART, 128), BF16), pltpu.SemaphoreType.DMA((2,))],
        input_output_aliases={4: 0},
        compiler_params=PARAMS,
        name="pack_halo",
    )(first, last, left, right, pay)


def weight_kernel(j, w_hbm, o_hbm, x, out, sems):
    fetches = [pltpu.make_async_copy(w_hbm.at[j, t], x.at[t], sems.at[t]) for t in range(TAPS)]
    for copy in fetches:
        copy.start()
    stores = []
    for t, copy in enumerate(fetches):
        copy.wait()
        cut = slice(t * C, (t + 1) * C)
        out[:, cut] = x[t].T
        store = pltpu.make_async_copy(out.at[:, cut], o_hbm.at[:, cut], sems.at[TAPS + t])
        store.start()
        stores.append(store)
    for store in stores:
        store.wait()


def turn_weights(j, weights):
    return pl.pallas_call(
        functools.partial(weight_kernel, j),
        in_specs=[ANY],
        out_specs=ANY,
        out_shape=jax.ShapeDtypeStruct((C, TAPS * C), BF16),
        scratch_shapes=[
            pltpu.VMEM((TAPS, C, C), BF16),
            pltpu.VMEM((C, TAPS * C), BF16),
            pltpu.SemaphoreType.DMA((2 * TAPS,)),
        ],
        compiler_params=PARAMS,
        cost_estimate=pl.CostEstimate(
            flops=TAPS * 2 * C * C * 256, bytes_accessed=15_000_000, transcendentals=0
        ),
        name=f"turn_weights_{j}",
    )(weights.reshape(2, TAPS, C, C))


def target_kernel(target_hbm, o_hbm, x, out, sems):
    fetch = pltpu.make_async_copy(target_hbm, x, sems.at[0])
    fetch.start()
    fetch.wait()
    for s in range(2):
        for q in range(6):
            out[s, q] = jnp.concatenate([x[q, s], x[q + 6, s]], axis=0).T
    store = pltpu.make_async_copy(out, o_hbm, sems.at[1])
    store.start()
    store.wait()


def turn_target(target):
    return pl.pallas_call(
        target_kernel,
        in_specs=[ANY],
        out_specs=ANY,
        out_shape=jax.ShapeDtypeStruct((2, 6, C, 128), BF16),
        scratch_shapes=[
            pltpu.VMEM((ROWS, 2, COLS, C), BF16),
            pltpu.VMEM((2, 6, C, 128), BF16),
            pltpu.SemaphoreType.DMA((2,)),
        ],
        compiler_params=PARAMS,
        name="turn_target",
    )(target)


def affine(row, par_ref, s, j, scale, offset):
    count = float(LAT * 1024 * WIDTH)

    def of_channel(base):
        picked = jnp.where(members(C, 0, base), row, 0.0)
        return jnp.sum(picked, axis=1, keepdims=True) / count

    mean = of_channel(32 * s)
    spread = of_channel(64 + 32 * s) - mean * mean
    factor = lax.rsqrt(spread + 1e-05) * par_ref[:, 2 * j : 2 * j + 1]
    rest = par_ref[:, 2 * j + 1 : 2 * j + 2] - mean * factor
    scale[...] = jnp.broadcast_to(factor, scale.shape)
    offset[...] = jnp.broadcast_to(rest, offset.shape)


def spread_taps(xs, at, tiles, edge, sides, part):
    rows = PART
    lane = lanes(rows)
    low = lane < 64
    first = (lane == 0) | (lane == 64)
    last = (lane == 63) | (lane == 127)
    for q in range(-1, 7):
        if q == -1:
            tile = jnp.where(low, edge, roll(tiles[5], 64))
        elif q == 6:
            tile = jnp.where(low, roll(tiles[0], 64), edge)
        else:
            tile = tiles[q]
        side = sides[pl.ds(at, rows), 128 * (q + 1) : 128 * (q + 2)]
        taps = (jnp.where(first, side, roll(tile, 1)), tile, jnp.where(last, side, roll(tile, -1)))
        for k, tap in enumerate(taps):
            if q == -1:
                tap = jnp.where(low & (part == 0), 0.0, tap)
            elif q == 6:
                tap = jnp.where((~low) & (part == SRC - 1), 0.0, tap)
            xs[pl.ds(k * C + at, rows), 128 * (q + 1) : 128 * (q + 2)] = tap.astype(BF16)


def product(wv, xs, n, more=None):
    x = jnp.concatenate([xs[:, n + 128 * i : n + 128 * i + 256] for i in range(3)], axis=0)
    if more is not None:
        x = jnp.concatenate([x, more], axis=1)
    return jnp.dot(wv[...], x, preferred_element_type=F32)


def first_kernel(
    part_ref, sums_ref, par_ref, pick_ref, taps_ref, recv_hbm, w_hbm,
    hid_hbm, out_sums, to_next, to_prev, out_halo,
    xs, wv, scale, offset, recv, hid, sides, xh, sems,
):
    fetches = [
        pltpu.make_async_copy(recv_hbm.at[:, 8 * s : 8 * s + 8], recv.at[s], sems.at[s])
        for s in range(2)
    ]
    weights = pltpu.make_async_copy(w_hbm, wv, sems.at[2])
    for copy in (fetches[0], weights, fetches[1]):
        copy.start()
    part = part_ref[0]
    lane = lanes(C)

    def act(x, a, o):
        return silu(x.astype(F32) * a + o)

    def columns(s):
        fetches[s].wait()
        affine(sums_ref[...], par_ref, s, 0, scale.at[s], offset.at[s])
        r = (lane & 15) - 2
        outside = ((part == 0) & (r < 0)) | ((part == SRC - 1) & (r >= ROWS))
        x = act(recv[s, :, 7].reshape(C, 128), scale[s], offset[s])
        halo = jnp.where(outside, 0.0, x).astype(BF16)
        sides[s] = jnp.dot(halo, pick_ref[...], preferred_element_type=F32)
        return halo

    def prepare(s, b):
        at = b * PART if isinstance(b, int) else pl.multiple_of(b * PART, PART)
        a, o = scale[s, pl.ds(at, PART), :], offset[s, pl.ds(at, PART), :]
        tiles = [act(recv[s, b, q], a, o) for q in range(7)]
        spread_taps(xs.at[s], at, tiles[:6], tiles[6], sides.at[s], part)

    halo = columns(0)

    @pl.loop(0, SRC)
    def _(b):
        prepare(0, b)

    weights.wait()
    stores = []

    def put(s, n, value):
        part = hid.at[s, :, n : n + 256]
        part[...] = value + par_ref[:, 5 + s : 6 + s]
        store = pltpu.make_async_copy(
            part, hid_hbm.at[s, :, n : n + 256], sems.at[3 + 3 * s + n // 256]
        )
        store.start()
        stores.append(store)

    put(0, 0, product(wv, xs.at[0], 0))
    both = jnp.concatenate([halo, columns(1)], axis=1)
    for t in range(TAPS):
        picked = jnp.dot(both, taps_ref[:, 128 * t : 128 * t + 128], preferred_element_type=F32)
        xh[C * t : C * (t + 1), :] = picked.astype(BF16)
    for n, blocks in ((256, (0, 1, 2, 3)), (512, (4, 5, 6, 7))):
        put(0, n, product(wv, xs.at[0], n))
        for b in blocks:
            prepare(1, b)
    put(1, 0, product(wv, xs.at[1], 0))
    put(1, 256, product(wv, xs.at[1], 256))
    out = product(wv, xs.at[1], 512, xh[...])
    put(1, 512, out[:, 0:256])
    bias = jnp.where(lane < 32, par_ref[:, 5:6], par_ref[:, 6:7])
    out_halo[...] = (out[:, 256:384] + bias).astype(BF16)

    row = jnp.zeros((1, 128), F32)
    low = lanes(128) < 64
    for at in range(0, C, 128):
        for s in range(2):
            pieces = [hid[s, at : at + 128, 128 * q : 128 * (q + 1)] for q in range(6)]
            for k in range(2):
                column = jnp.sum(sum(p * p if k else p for p in pieces), axis=1, keepdims=True)
                own = members(128, at, 64 * k + 32 * s)
                row += jnp.sum(jnp.where(own, column, 0.0), axis=0, keepdims=True)
        start, end = hid.at[:, at : at + 128, 0:128], hid.at[:, at : at + 128, 640:768]
        to_next[at : at + 128, :] = jnp.where(low, roll(end[0], 64), end[1]).astype(BF16)
        to_prev[at : at + 128, :] = jnp.where(low, start[0], roll(start[1], 64)).astype(BF16)
    out_sums[...] = jnp.broadcast_to(row, out_sums.shape)
    for store in stores:
        store.wait()


def first_conv(part, sums, params, pick, taps, recv, weights):
    tile = jax.ShapeDtypeStruct((C, 128), BF16)
    return pl.pallas_call(
        first_kernel,
        in_specs=[SMEM] + [VMEM] * 4 + [ANY] * 2,
        out_specs=[ANY] + [VMEM] * 4,
        out_shape=[
            jax.ShapeDtypeStruct((2, C, 768), F32),
            jax.ShapeDtypeStruct((128, 128), F32),
            tile, tile, tile,
        ],
        scratch_shapes=[
            pltpu.VMEM((2, 3 * C, 1024), BF16),
            pltpu.VMEM((C, TAPS * C), BF16),
            pltpu.VMEM((2, C, 128), F32),
            pltpu.VMEM((2, C, 128), F32),
            pltpu.VMEM((2, SRC, 8, PART, 128), BF16),
            pltpu.VMEM((2, C, 768), F32),
            pltpu.VMEM((2, C, 1024), F32),
            pltpu.VMEM((TAPS * C, 128), BF16),
            pltpu.SemaphoreType.DMA((9,)),
        ],
        compiler_params=PARAMS,
        cost_estimate=pl.CostEstimate(
            flops=4 * 768 * C * C * 9, bytes_accessed=20_000_000, transcendentals=0
        ),
        name="first_conv",
    )(part, sums, params, pick, taps, recv, weights)


def second_kernel(
    part_ref, coef_ref, sums_ref, par_ref, pick_ref, near_ref, prev_ref, next_ref,
    hid_hbm, w_hbm, recv_hbm, target_hbm,
    noise_hbm, out_ref,
    xs, wv, hid, lat, target, noise_out, sides, scale, offset, sems,
):
    weights = pltpu.make_async_copy(w_hbm, wv, sems.at[6])
    fetches, later = [], []
    for s in range(2):
        fetches.append(pltpu.make_async_copy(hid_hbm.at[s], hid.at[s], sems.at[s]))
        tiles = recv_hbm.at[:, 8 * s : 8 * s + 6]
        later.append(pltpu.make_async_copy(tiles, lat.at[s], sems.at[2 + s]))
        later.append(pltpu.make_async_copy(target_hbm.at[s], target.at[s], sems.at[4 + s]))
    for copy in (fetches[0], weights, later[0], later[1], fetches[1], later[2], later[3]):
        copy.start()
    part = part_ref[0]
    row = jnp.sum(sums_ref[...], axis=0, keepdims=True)
    low = lanes(PART) < 64

    def columns(s):
        affine(row, par_ref, s, 1, scale.at[s], offset.at[s])
        halo = silu(near_ref[...].astype(F32) * scale[s] + offset[s]).astype(BF16)
        sides[s] = jnp.dot(halo, pick_ref[s], preferred_element_type=F32)
        fetches[s].wait()

    def prepare(s, b):
        at = b * PART if isinstance(b, int) else pl.multiple_of(b * PART, PART)
        rows = pl.ds(at, PART)
        a, o = scale[s, rows, :], offset[s, rows, :]

        def act(x):
            return silu(x * a + o)

        tiles = [act(hid[s, rows, 128 * q : 128 * (q + 1)]) for q in range(6)]
        above, below = prev_ref[rows, :].astype(F32), next_ref[rows, :].astype(F32)
        if s == 0:
            edge = jnp.where(low, above, roll(below, 64))
        else:
            edge = jnp.where(low, roll(above, 64), below)
        spread_taps(xs.at[s], at, tiles, act(edge), sides.at[s], part)

    def finish(s, n, acc):
        keep, gain = coef_ref[2 * s], coef_ref[2 * s + 1]
        out = product(wv, xs.at[s], n) + par_ref[:, 4:5]
        for h in range(2):
            q = n // 128 + h
            mine = lat[s, :, q].reshape(C, 128).astype(F32)
            noise = (out[:, 128 * h : 128 * h + 128] + mine).astype(BF16)
            center = keep * mine + gain * noise.astype(F32)
            diff = target[s, q].astype(F32) - center
            acc += jnp.sum((diff * diff).reshape(C // 8, 8, 128), axis=0)
            plain = noise.T
            for r, piece in ((q, plain[0:64]), (q + 6, plain[64:128])):
                noise_out[s, r] = piece
                store = pltpu.make_async_copy(
                    noise_out.at[s, r], noise_hbm.at[r, s], sems.at[7 + ROWS * s + r]
                )
                store.start()
                stores.append(store)
        return acc

    columns(0)

    @pl.loop(0, SRC)
    def _(b):
        prepare(0, b)

    weights.wait()
    result = jnp.zeros((1, 128), F32)
    stores = []
    for s in range(2):
        acc = jnp.zeros((8, 128), F32)
        later[2 * s].wait()
        later[2 * s + 1].wait()
        for n, blocks in ((0, ()), (256, (0, 1, 2, 3)), (512, (4, 5, 6, 7))):
            acc = finish(s, n, acc)
            if s == 0:
                if n == 0:
                    columns(1)
                for b in blocks:
                    prepare(1, b)
        value = jnp.sum(acc, axis=(0, 1), keepdims=True)
        result = jnp.where(lanes(1) == s, value, result)
    out_ref[...] = jnp.broadcast_to(result, out_ref.shape)
    for store in stores:
        store.wait()


def second_conv(part, coef, sums, params, pick, tiles, hidden, weights, recv, target):
    return pl.pallas_call(
        second_kernel,
        in_specs=[SMEM, SMEM] + [VMEM] * 6 + [ANY] * 4,
        out_specs=[ANY, VMEM],
        out_shape=[
            jax.ShapeDtypeStruct((ROWS, 2, COLS, C), BF16),
            jax.ShapeDtypeStruct((128, 128), F32),
        ],
        scratch_shapes=[
            pltpu.VMEM((2, 3 * C, 1024), BF16),
            pltpu.VMEM((C, TAPS * C), BF16),
            pltpu.VMEM((2, C, 768), F32),
            pltpu.VMEM((2, SRC, 6, PART, 128), BF16),
            pltpu.VMEM((2, 6, C, 128), BF16),
            pltpu.VMEM((2, ROWS, COLS, C), BF16),
            pltpu.VMEM((2, C, 1024), F32),
            pltpu.VMEM((2, C, 128), F32),
            pltpu.VMEM((2, C, 128), F32),
            pltpu.SemaphoreType.DMA((7 + 2 * ROWS,)),
        ],
        compiler_params=PARAMS,
        cost_estimate=pl.CostEstimate(
            flops=4 * 768 * C * C * 9, bytes_accessed=20_000_000, transcendentals=0
        ),
        name="second_conv",
    )(part, coef, sums, params, pick, *tiles, hidden, weights, recv, target)


def time_embed(timesteps, time_w1, time_w2):
    half = time_w1.shape[0] // 2
    freqs = jnp.exp(-math.log(10000.0) * jnp.arange(half, dtype=F32) / half)
    angles = timesteps.astype(F32)[:, None] * freqs[None, :]
    features = jnp.concatenate([jnp.cos(angles), jnp.sin(angles)], axis=1)
    hidden = jax.nn.silu(jnp.dot(features, time_w1, precision=lax.Precision.HIGHEST))
    return jnp.dot(hidden, time_w2, precision=lax.Precision.HIGHEST)


def plan(steps):
    frac = steps.astype(F32) / 1000.0
    return jnp.cos((frac + 0.008) / 1.008 * (math.pi / 2.0)) ** 2


def everywhere(rows, axes):
    got = lax.all_to_all(rows.reshape(-1, 1, 128), axes, 0, 0, tiled=True)
    return got.reshape(-1, 128)


def ring(axis, step, wrap):
    size = lax.axis_size(axis)
    return [(i, (i + step) % size) for i in range(size) if wrap or 0 <= i + step < size]


def swap(array, axis):
    return lax.all_to_all(array, axis, split_axis=0, concat_axis=0, tiled=True)


def after(value, *others):
    return lax.optimization_barrier((value,) + others)[0]


def butterfly(x, axis):
    step = 1
    while step < lax.axis_size(axis):
        pairs = [(i, i ^ step) for i in range(lax.axis_size(axis))]
        x = x + lax.ppermute(x, axis, pairs)
        step *= 2
    return x


def body(
    latents, next_latents, timesteps, resume_steps, conv_weights, conv_bias,
    norm_gain, norm_shift, time_w1, time_w2,
):
    part = lax.axis_index("ch").astype(jnp.int32).reshape(1)
    first_pick = jnp.asarray(side_lanes(lambda r: 16 + r + 2, lambda r: 64 + r + 2))
    second_pick = jnp.asarray(
        np.stack(
            [
                side_lanes(lambda r: halo_lane(s, 0, r), lambda r: halo_lane(s, 1, r))
                for s in range(2)
            ]
        )
    )
    tap_pick = jnp.asarray(halo_taps())

    cells = latents.transpose(1, 2, 3, 0)
    sums, first, last = local_sums(part, cells)
    left = lax.ppermute(last, "lon", ring("lon", 1, True))
    right = lax.ppermute(first, "lon", ring("lon", -1, True))
    sums = butterfly(sums, "ch")
    pay = pack(after(cells, first))
    pay = pack_halo(first, last, left, right, pay)
    pay, sums = lax.optimization_barrier((pay, sums))
    recv = swap(pay, "ch")
    sums = butterfly(sums, "lon")
    conv_weights, time_w1, following = after((conv_weights, time_w1, next_latents), pay)
    turned = [turn_weights(j, conv_weights) for j in range(2)]
    target = turn_target(following)

    temb = time_embed(timesteps, time_w1, time_w2)
    columns = [
        norm_gain[0], norm_shift[0], norm_gain[1], norm_shift[1], conv_bias[1],
        conv_bias[0] + temb[0], conv_bias[0] + temb[1],
    ]
    params = jnp.pad(jnp.stack(columns, axis=1), ((0, 0), (0, 128 - len(columns))))

    alpha = plan(timesteps)
    prior = plan(timesteps - resume_steps)
    variance = (1.0 - prior) / (1.0 - alpha) * (1.0 - alpha / prior)
    keep = (1.0 - prior) * jnp.sqrt(alpha / (prior * (1.0 - alpha)))
    ratio = jnp.sqrt(prior) / jnp.sqrt(alpha)
    coef = jnp.stack([ratio, keep - ratio * jnp.sqrt(1.0 - alpha)], axis=1).reshape(4)

    recv, turned, target = lax.optimization_barrier((recv, turned, target))
    hidden, sums, to_next, to_prev, near = first_conv(
        part, sums, params, first_pick, tap_pick, recv, turned[0]
    )
    from_prev = lax.ppermute(to_next, "ch", ring("ch", 1, False))
    from_next = lax.ppermute(to_prev, "ch", ring("ch", -1, False))
    sums = everywhere(sums, ("lon", "ch"))
    noise, terms = second_conv(
        part, coef, sums, params, second_pick, (near, from_prev, from_next),
        hidden, turned[1], recv, target,
    )
    squares = jnp.sum(everywhere(terms, ("lon", "ch")), axis=0)[:2]
    logprob = (
        -squares / (2.0 * variance) / float(LAT * 1024 * C)
        - 0.5 * jnp.log(variance)
        - 0.5 * math.log(2.0 * math.pi)
    )
    return (noise, logprob)


def solution(mesh):
    return jax.shard_map(
        body,
        mesh=mesh,
        in_specs=(
            P(None, None, "lon", "ch"),
            P("ch", None, "lon", None),
            P(), P(), P(), P(), P(), P(), P(), P(),
        ),
        out_specs=(P("ch", None, "lon", None), P()),
        check_vma=False,
    )
```

```python
import functools
import math

import jax
import jax.numpy as jnp
import numpy as np
from jax import lax
from jax.experimental import pallas as pl
from jax.experimental.pallas import tpu as pltpu
from jax.sharding import PartitionSpec as P

GROUPS = 32
C = 640
LAT = 96
ROWS = 12
COLS = 64
SRC = 8
PART = C // SRC
WIDTH = C // GROUPS
TAPS = 9
F32 = jnp.float32
BF16 = jnp.bfloat16
VMEM = pl.BlockSpec(memory_space=pltpu.VMEM)
SMEM = pl.BlockSpec(memory_space=pltpu.SMEM)
ANY = pl.BlockSpec(memory_space=pl.ANY)
CHUNK = 16
LIMIT = 56 * 2**20


def roll(x, by):
    by %= 128
    return x if by == 0 else pltpu.roll(x, by, 1)


def place(q):
    return 2 * q + 3


def side_lanes(of_left, of_right):
    out = np.zeros((128, 128), np.float32)
    for q in range(-1, 7):
        p = place(q)
        out[of_left(q), p] = 1
        out[of_left(q + 6), p + 64] = 1
        out[of_right(q), p + 63] = 1
        out[of_right(q + 6), p - 1] = 1
    return out.astype(BF16)


def halo_lane(s, side, row):
    return 32 * s + 16 * side + row + 1


def halo_taps():
    out = np.zeros((256, 3 * 128), np.float32)
    for k in range(3):
        for s in range(2):
            for side in range(2):
                for row in range(-2, 14):
                    source = 128 * s + 16 * (3 * side + k) + row + 2
                    out[source, 128 * k + halo_lane(s, side, row + 1)] = 1
    return out.astype(BF16)


def lanes(rows):
    return lax.broadcasted_iota(jnp.int32, (rows, 128), 1)


def members(rows, first, base):
    chan = lax.broadcasted_iota(jnp.int32, (rows, 128), 0) + first
    low = (lanes(rows) - base) * WIDTH
    return (chan >= low) & (chan < low + WIDTH)


def silu(x):
    return 0.5 * x * (1.0 + jnp.tanh(0.5 * x))


PARAMS = pltpu.CompilerParams(vmem_limit_bytes=LIMIT)


def sums_kernel(part_ref, cells_hbm, sums_ref, first_ref, last_ref, x, sems):
    half = COLS // 2
    copies = []
    for s in range(2):
        for c in range(2):
            cut = slice(c * half, (c + 1) * half)
            copies.append(
                pltpu.make_async_copy(cells_hbm.at[s, cut], x.at[s, cut], sems.at[2 * s + c])
            )
            copies[-1].start()
    row = jnp.zeros((1, 128), F32)
    for s in range(2):
        total = jnp.zeros((PART, LAT), F32)
        square = jnp.zeros((PART, LAT), F32)
        for c in range(2):
            copies[2 * s + c].wait()

            def add(i, carry):
                total, square = carry
                for j in range(4):
                    v = x[s, c * half + 4 * i + j].astype(F32)
                    total, square = total + v, square + v * v
                return total, square

            total, square = lax.fori_loop(0, half // 4, add, (total, square))
        for k, acc in enumerate((total, square)):
            column = jnp.sum(acc, axis=1, keepdims=True)
            own = members(PART, part_ref[0] * PART, 64 * k + 32 * s)
            row += jnp.sum(jnp.where(own, column, 0.0), axis=0, keepdims=True)
        first_ref[s] = x[s, 0:2]
        last_ref[s] = x[s, COLS - 2 : COLS]
    sums_ref[...] = row


def local_sums(part, cells):
    return pl.pallas_call(
        sums_kernel,
        in_specs=[SMEM, ANY],
        out_specs=[VMEM] * 3,
        out_shape=[
            jax.ShapeDtypeStruct((1, 128), F32),
            jax.ShapeDtypeStruct((2, 2, PART, LAT), BF16),
            jax.ShapeDtypeStruct((2, 2, PART, LAT), BF16),
        ],
        scratch_shapes=[pltpu.VMEM((2, COLS, PART, LAT), BF16), pltpu.SemaphoreType.DMA((4,))],
        compiler_params=PARAMS,
        name="local_sums",
    )(part, cells)


def pack_kernel(cells_hbm, pay_hbm, x, out, taken, turned, sems):
    fetches = [pltpu.make_async_copy(cells_hbm.at[s], x.at[s], sems.at[s]) for s in range(2)]
    for copy in fetches:
        copy.start()
    taken[...] = jnp.zeros_like(taken)
    turned[...] = jnp.zeros_like(turned)
    def tile(r):
        return turned[CHUNK * (r + 1) : CHUNK * (r + 2), :]

    stores = []
    for s in range(2):
        fetches[s].wait()

        @pl.loop(0, PART // CHUNK)
        def _(e):
            own = pl.ds(pl.multiple_of(e * CHUNK, CHUNK), CHUNK)
            taken[:, 0:LAT] = x[s, :, own, :].astype(F32).reshape(COLS * CHUNK, LAT)
            for j in range(CHUNK):
                across = taken[pl.ds(j, COLS, stride=CHUNK), :].T
                turned[pl.ds(CHUNK + j, LAT, stride=CHUNK), 0:COLS] = across[0:LAT, :]
            for d in range(SRC):
                for q in range(7):
                    upper, lower = (d * ROWS + q, d * ROWS + q + 6)
                    if q == 6:
                        upper, lower = (d * ROWS - 1, d * ROWS + ROWS)
                    out[s, d, q, own, :] = (tile(upper) + roll(tile(lower), 64)).astype(BF16)

        store = pltpu.make_async_copy(out.at[s], pay_hbm.at[:, 8 * s : 8 * s + 7], sems.at[2 + s])
        store.start()
        stores.append(store)
    for store in stores:
        store.wait()


def pack(cells):
    return pl.pallas_call(
        pack_kernel,
        in_specs=[ANY],
        out_specs=ANY,
        out_shape=jax.ShapeDtypeStruct((SRC, 16, PART, 128), BF16),
        scratch_shapes=[
            pltpu.VMEM((2, COLS, PART, LAT), BF16),
            pltpu.VMEM((2, SRC, 7, PART, 128), BF16),
            pltpu.VMEM((COLS * CHUNK, 128), F32),
            pltpu.VMEM(((LAT + 8) * CHUNK, 128), F32),
            pltpu.SemaphoreType.DMA((4,)),
        ],
        compiler_params=PARAMS,
        cost_estimate=pl.CostEstimate(
            flops=1_000_000_000, bytes_accessed=8_000_000, transcendentals=0
        ),
        name="pack_latents",
    )(cells)


def halo_kernel(first_ref, last_ref, left_ref, right_ref, _, pay_hbm, out, sems):
    lane = lanes(PART)
    pad = jnp.zeros((PART, 128 - LAT), F32)
    stores = []
    for s in range(2):
        near = [left_ref[s, 0], left_ref[s, 1], first_ref[s, 0], last_ref[s, 1],
                right_ref[s, 0], right_ref[s, 1]]
        near = [jnp.concatenate([col.astype(F32), pad], axis=1) for col in near]
        for d in range(SRC):
            halo = jnp.zeros((PART, 128), F32)
            for kind in range(6):
                own = (lane >= 16 * kind) & (lane < 16 * kind + 16)
                halo = jnp.where(own, roll(near[kind], 16 * kind + 2 - d * ROWS), halo)
            out[s, d] = halo.astype(BF16)
        store = pltpu.make_async_copy(out.at[s], pay_hbm.at[:, 8 * s + 7], sems.at[s])
        store.start()
        stores.append(store)
    for store in stores:
        store.wait()


def pack_halo(first, last, left, right, pay):
    return pl.pallas_call(
        halo_kernel,
        in_specs=[VMEM] * 4 + [ANY],
        out_specs=ANY,
        out_shape=jax.ShapeDtypeStruct((SRC, 16, PART, 128), BF16),
        scratch_shapes=[pltpu.VMEM((2, SRC, PART, 128), BF16), pltpu.SemaphoreType.DMA((2,))],
        input_output_aliases={4: 0},
        compiler_params=PARAMS,
        name="pack_halo",
    )(first, last, left, right, pay)


def weight_kernel(j, w_hbm, o_hbm, x, out, sems):
    fetches = [pltpu.make_async_copy(w_hbm.at[j, t], x.at[t], sems.at[t]) for t in range(TAPS)]
    for copy in fetches:
        copy.start()
    stores = []
    for t, copy in enumerate(fetches):
        copy.wait()
        cut = slice(t * C, (t + 1) * C)
        out[:, cut] = x[t].T
        store = pltpu.make_async_copy(out.at[:, cut], o_hbm.at[:, cut], sems.at[TAPS + t])
        store.start()
        stores.append(store)
    for store in stores:
        store.wait()


def turn_weights(j, weights):
    return pl.pallas_call(
        functools.partial(weight_kernel, j),
        in_specs=[ANY],
        out_specs=ANY,
        out_shape=jax.ShapeDtypeStruct((C, TAPS * C), BF16),
        scratch_shapes=[
            pltpu.VMEM((TAPS, C, C), BF16),
            pltpu.VMEM((C, TAPS * C), BF16),
            pltpu.SemaphoreType.DMA((2 * TAPS,)),
        ],
        compiler_params=PARAMS,
        cost_estimate=pl.CostEstimate(
            flops=TAPS * 2 * C * C * 256, bytes_accessed=15_000_000, transcendentals=0
        ),
        name=f"turn_weights_{j}",
    )(weights.reshape(2, TAPS, C, C))


def target_kernel(target_hbm, o_hbm, x, out, sems):
    fetch = pltpu.make_async_copy(target_hbm, x, sems.at[0])
    fetch.start()
    fetch.wait()
    for s in range(2):
        for q in range(6):
            out[s, q] = jnp.concatenate([x[q, s], x[q + 6, s]], axis=0).T
    store = pltpu.make_async_copy(out, o_hbm, sems.at[1])
    store.start()
    store.wait()


def turn_target(target):
    return pl.pallas_call(
        target_kernel,
        in_specs=[ANY],
        out_specs=ANY,
        out_shape=jax.ShapeDtypeStruct((2, 6, C, 128), BF16),
        scratch_shapes=[
            pltpu.VMEM((ROWS, 2, COLS, C), BF16),
            pltpu.VMEM((2, 6, C, 128), BF16),
            pltpu.SemaphoreType.DMA((2,)),
        ],
        compiler_params=PARAMS,
        name="turn_target",
    )(target)


def affine(row, par_ref, s, j, scale, offset):
    count = float(LAT * 1024 * WIDTH)

    def of_channel(base):
        picked = jnp.where(members(C, 0, base), row, 0.0)
        return jnp.sum(picked, axis=1, keepdims=True) / count

    mean = of_channel(32 * s)
    spread = of_channel(64 + 32 * s) - mean * mean
    factor = lax.rsqrt(spread + 1e-05) * par_ref[:, 2 * j : 2 * j + 1]
    rest = par_ref[:, 2 * j + 1 : 2 * j + 2] - mean * factor
    scale[...] = jnp.broadcast_to(factor, scale.shape)
    offset[...] = jnp.broadcast_to(rest, offset.shape)


def spread_taps(xs, at, tiles, edge, sides, part):
    rows = PART
    lane = lanes(rows)
    low = lane < 64
    first = (lane == 0) | (lane == 64)
    last = (lane == 63) | (lane == 127)
    for q in range(-1, 7):
        if q == -1:
            tile = jnp.where(low, edge, roll(tiles[5], 64))
        elif q == 6:
            tile = jnp.where(low, roll(tiles[0], 64), edge)
        else:
            tile = tiles[q]
        side = roll(sides[pl.ds(at, rows), :], -place(q))
        taps = (jnp.where(first, side, roll(tile, 1)), tile, jnp.where(last, side, roll(tile, -1)))
        for k, tap in enumerate(taps):
            if q == -1:
                tap = jnp.where(low & (part == 0), 0.0, tap)
            elif q == 6:
                tap = jnp.where((~low) & (part == SRC - 1), 0.0, tap)
            xs[pl.ds(k * C + at, rows), 128 * (q + 1) : 128 * (q + 2)] = tap.astype(BF16)


def product(wv, xs, n, more=None):
    x = jnp.concatenate([xs[:, n + 128 * i : n + 128 * i + 256] for i in range(3)], axis=0)
    if more is not None:
        x = jnp.concatenate([x, more], axis=1)
    return jnp.dot(wv[...], x, preferred_element_type=F32)


def first_kernel(
    part_ref, sums_ref, par_ref, pick_ref, taps_ref, recv_hbm, w_hbm,
    hid_hbm, out_sums, to_next, to_prev, out_halo,
    xs, wv, scale, offset, recv, hid, sides, xh, sems,
):
    fetches = [
        pltpu.make_async_copy(recv_hbm.at[:, 8 * s : 8 * s + 8], recv.at[s], sems.at[s])
        for s in range(2)
    ]
    weights = pltpu.make_async_copy(w_hbm, wv, sems.at[2])
    for copy in (fetches[0], weights, fetches[1]):
        copy.start()
    part = part_ref[0]
    lane = lanes(C)

    def act(x, a, o):
        return silu(x.astype(F32) * a + o)

    def columns(s):
        fetches[s].wait()
        affine(sums_ref[...], par_ref, s, 0, scale.at[s], offset.at[s])
        r = (lane & 15) - 2
        outside = ((part == 0) & (r < 0)) | ((part == SRC - 1) & (r >= ROWS))
        x = act(recv[s, :, 7].reshape(C, 128), scale[s], offset[s])
        halo = jnp.where(outside, 0.0, x).astype(BF16)
        sides[s] = jnp.dot(halo, pick_ref[...], preferred_element_type=F32)
        return halo

    def prepare(s, b):
        at = b * PART if isinstance(b, int) else pl.multiple_of(b * PART, PART)
        a, o = scale[s, pl.ds(at, PART), :], offset[s, pl.ds(at, PART), :]
        tiles = [act(recv[s, b, q], a, o) for q in range(7)]
        spread_taps(xs.at[s], at, tiles[:6], tiles[6], sides.at[s], part)

    halo = columns(0)

    @pl.loop(0, SRC)
    def _(b):
        prepare(0, b)

    weights.wait()
    stores = []

    def put(s, n, value):
        part = hid.at[s, :, n : n + 256]
        part[...] = value + par_ref[:, 5 + s : 6 + s]
        store = pltpu.make_async_copy(
            part, hid_hbm.at[s, :, n : n + 256], sems.at[3 + 3 * s + n // 256]
        )
        store.start()
        stores.append(store)

    put(0, 0, product(wv, xs.at[0], 0))
    both = jnp.concatenate([halo, columns(1)], axis=1)
    for k in range(3):
        picked = jnp.dot(both, taps_ref[:, 128 * k : 128 * k + 128], preferred_element_type=F32)
        for i in range(3):
            t = 3 * i + k
            xh[C * t : C * (t + 1), :] = roll(picked, -i).astype(BF16)
    for n, blocks in ((256, (0, 1, 2, 3)), (512, (4, 5, 6, 7))):
        put(0, n, product(wv, xs.at[0], n))
        for b in blocks:
            prepare(1, b)
    put(1, 0, product(wv, xs.at[1], 0))
    put(1, 256, product(wv, xs.at[1], 256))
    out = product(wv, xs.at[1], 512, xh[...])
    put(1, 512, out[:, 0:256])
    bias = jnp.where(lane < 32, par_ref[:, 5:6], par_ref[:, 6:7])
    out_halo[...] = (out[:, 256:384] + bias).astype(BF16)

    row = jnp.zeros((1, 128), F32)
    low = lanes(128) < 64
    for at in range(0, C, 128):
        for s in range(2):
            pieces = [hid[s, at : at + 128, 128 * q : 128 * (q + 1)] for q in range(6)]
            for k in range(2):
                column = jnp.sum(sum(p * p if k else p for p in pieces), axis=1, keepdims=True)
                own = members(128, at, 64 * k + 32 * s)
                row += jnp.sum(jnp.where(own, column, 0.0), axis=0, keepdims=True)
        start, end = hid.at[:, at : at + 128, 0:128], hid.at[:, at : at + 128, 640:768]
        to_next[at : at + 128, :] = jnp.where(low, roll(end[0], 64), end[1]).astype(BF16)
        to_prev[at : at + 128, :] = jnp.where(low, start[0], roll(start[1], 64)).astype(BF16)
    out_sums[...] = jnp.broadcast_to(row, out_sums.shape)
    for store in stores:
        store.wait()


def first_conv(part, sums, params, pick, taps, recv, weights):
    tile = jax.ShapeDtypeStruct((C, 128), BF16)
    return pl.pallas_call(
        first_kernel,
        in_specs=[SMEM] + [VMEM] * 4 + [ANY] * 2,
        out_specs=[ANY] + [VMEM] * 4,
        out_shape=[
            jax.ShapeDtypeStruct((2, C, 768), F32),
            jax.ShapeDtypeStruct((128, 128), F32),
            tile, tile, tile,
        ],
        scratch_shapes=[
            pltpu.VMEM((2, 3 * C, 1024), BF16),
            pltpu.VMEM((C, TAPS * C), BF16),
            pltpu.VMEM((2, C, 128), F32),
            pltpu.VMEM((2, C, 128), F32),
            pltpu.VMEM((2, SRC, 8, PART, 128), BF16),
            pltpu.VMEM((2, C, 768), F32),
            pltpu.VMEM((2, C, 128), F32),
            pltpu.VMEM((TAPS * C, 128), BF16),
            pltpu.SemaphoreType.DMA((9,)),
        ],
        compiler_params=PARAMS,
        cost_estimate=pl.CostEstimate(
            flops=4 * 768 * C * C * 9, bytes_accessed=20_000_000, transcendentals=0
        ),
        name="first_conv",
    )(part, sums, params, pick, taps, recv, weights)


def second_kernel(
    part_ref, coef_ref, sums_ref, par_ref, pick_ref, near_ref, prev_ref, next_ref,
    hid_hbm, w_hbm, recv_hbm, target_hbm,
    noise_hbm, out_ref,
    xs, wv, hid, lat, target, noise_out, sides, scale, offset, sems,
):
    weights = pltpu.make_async_copy(w_hbm, wv, sems.at[6])
    fetches, later = [], []
    for s in range(2):
        fetches.append(pltpu.make_async_copy(hid_hbm.at[s], hid.at[s], sems.at[s]))
        tiles = recv_hbm.at[:, 8 * s : 8 * s + 6]
        later.append(pltpu.make_async_copy(tiles, lat.at[s], sems.at[2 + s]))
        later.append(pltpu.make_async_copy(target_hbm.at[s], target.at[s], sems.at[4 + s]))
    for copy in (fetches[0], weights, fetches[1], *later):
        copy.start()
    part = part_ref[0]
    row = jnp.sum(sums_ref[...], axis=0, keepdims=True)
    low = lanes(PART) < 64

    def columns(s):
        affine(row, par_ref, s, 1, scale.at[s], offset.at[s])
        halo = silu(near_ref[...].astype(F32) * scale[s] + offset[s]).astype(BF16)
        sides[s] = jnp.dot(halo, pick_ref[s], preferred_element_type=F32)
        fetches[s].wait()

    def prepare(s, b):
        at = b * PART if isinstance(b, int) else pl.multiple_of(b * PART, PART)
        rows = pl.ds(at, PART)
        a, o = scale[s, rows, :], offset[s, rows, :]

        def act(x):
            return silu(x * a + o)

        tiles = [act(hid[s, rows, 128 * q : 128 * (q + 1)]) for q in range(6)]
        above, below = prev_ref[rows, :].astype(F32), next_ref[rows, :].astype(F32)
        if s == 0:
            edge = jnp.where(low, above, roll(below, 64))
        else:
            edge = jnp.where(low, roll(above, 64), below)
        spread_taps(xs.at[s], at, tiles, act(edge), sides.at[s], part)

    def finish(s, n, acc):
        keep, gain = coef_ref[2 * s], coef_ref[2 * s + 1]
        out = product(wv, xs.at[s], n) + par_ref[:, 4:5]
        for h in range(2):
            q = n // 128 + h
            mine = lat[s, :, q].reshape(C, 128).astype(F32)
            noise = (out[:, 128 * h : 128 * h + 128] + mine).astype(BF16)
            center = keep * mine + gain * noise.astype(F32)
            diff = target[s, q].astype(F32) - center
            acc += jnp.sum((diff * diff).reshape(C // 8, 8, 128), axis=0)
            plain = noise.T
            noise_out[s, q] = plain[0:64]
            noise_out[s, q + 6] = plain[64:128]
        return acc

    columns(0)

    @pl.loop(0, SRC)
    def _(b):
        prepare(0, b)

    columns(1)
    weights.wait()
    for copy in later:
        copy.wait()
    result = jnp.zeros((1, 128), F32)
    stores = []
    for s in range(2):
        acc = jnp.zeros((8, 128), F32)
        for n, blocks in ((0, (0, 1, 2)), (256, (3, 4, 5)), (512, (6, 7))):
            acc = finish(s, n, acc)
            if s == 0:
                for b in blocks:
                    prepare(1, b)
        store = pltpu.make_async_copy(noise_out.at[s], noise_hbm.at[:, s], sems.at[7 + s])
        store.start()
        stores.append(store)
        value = jnp.sum(acc, axis=(0, 1), keepdims=True)
        result = jnp.where(lanes(1) == s, value, result)
    out_ref[...] = jnp.broadcast_to(result, out_ref.shape)
    for store in stores:
        store.wait()


def second_conv(part, coef, sums, params, pick, tiles, hidden, weights, recv, target):
    return pl.pallas_call(
        second_kernel,
        in_specs=[SMEM, SMEM] + [VMEM] * 6 + [ANY] * 4,
        out_specs=[ANY, VMEM],
        out_shape=[
            jax.ShapeDtypeStruct((ROWS, 2, COLS, C), BF16),
            jax.ShapeDtypeStruct((128, 128), F32),
        ],
        scratch_shapes=[
            pltpu.VMEM((2, 3 * C, 1024), BF16),
            pltpu.VMEM((C, TAPS * C), BF16),
            pltpu.VMEM((2, C, 768), F32),
            pltpu.VMEM((2, SRC, 6, PART, 128), BF16),
            pltpu.VMEM((2, 6, C, 128), BF16),
            pltpu.VMEM((2, ROWS, COLS, C), BF16),
            pltpu.VMEM((2, C, 128), F32),
            pltpu.VMEM((2, C, 128), F32),
            pltpu.VMEM((2, C, 128), F32),
            pltpu.SemaphoreType.DMA((9,)),
        ],
        compiler_params=PARAMS,
        cost_estimate=pl.CostEstimate(
            flops=4 * 768 * C * C * 9, bytes_accessed=20_000_000, transcendentals=0
        ),
        name="second_conv",
    )(part, coef, sums, params, pick, *tiles, hidden, weights, recv, target)


def time_embed(timesteps, time_w1, time_w2):
    half = time_w1.shape[0] // 2
    freqs = jnp.exp(-math.log(10000.0) * jnp.arange(half, dtype=F32) / half)
    angles = timesteps.astype(F32)[:, None] * freqs[None, :]
    features = jnp.concatenate([jnp.cos(angles), jnp.sin(angles)], axis=1)
    hidden = jax.nn.silu(jnp.dot(features, time_w1, precision=lax.Precision.HIGHEST))
    return jnp.dot(hidden, time_w2, precision=lax.Precision.HIGHEST)


def plan(steps):
    frac = steps.astype(F32) / 1000.0
    return jnp.cos((frac + 0.008) / 1.008 * (math.pi / 2.0)) ** 2


def everywhere(rows, axes):
    got = lax.all_to_all(rows.reshape(-1, 1, 128), axes, 0, 0, tiled=True)
    return got.reshape(-1, 128)


def ring(axis, step, wrap):
    size = lax.axis_size(axis)
    return [(i, (i + step) % size) for i in range(size) if wrap or 0 <= i + step < size]


def swap(array, axis):
    return lax.all_to_all(array, axis, split_axis=0, concat_axis=0, tiled=True)


def after(value, *others):
    return lax.optimization_barrier((value,) + others)[0]


def butterfly(x, axis):
    step = 1
    while step < lax.axis_size(axis):
        pairs = [(i, i ^ step) for i in range(lax.axis_size(axis))]
        x = x + lax.ppermute(x, axis, pairs)
        step *= 2
    return x


def body(
    latents, next_latents, timesteps, resume_steps, conv_weights, conv_bias,
    norm_gain, norm_shift, time_w1, time_w2,
):
    part = lax.axis_index("ch").astype(jnp.int32).reshape(1)
    first_pick = jnp.asarray(side_lanes(lambda r: 16 + r + 2, lambda r: 64 + r + 2))
    second_pick = jnp.asarray(
        np.stack(
            [
                side_lanes(lambda r: halo_lane(s, 0, r), lambda r: halo_lane(s, 1, r))
                for s in range(2)
            ]
        )
    )
    tap_pick = jnp.asarray(halo_taps())

    cells = latents.transpose(1, 2, 3, 0)
    sums, first, last = local_sums(part, cells)
    left = lax.ppermute(last, "lon", ring("lon", 1, True))
    right = lax.ppermute(first, "lon", ring("lon", -1, True))
    sums = butterfly(sums, "ch")
    pay = pack(after(cells, first))
    pay = pack_halo(first, last, left, right, pay)
    pay, sums = lax.optimization_barrier((pay, sums))
    recv = swap(pay, "ch")
    sums = butterfly(sums, "lon")
    conv_weights, time_w1 = after((conv_weights, time_w1), pay)
    later_weights, following = after((conv_weights, next_latents), sums)
    turned = [turn_weights(0, conv_weights), turn_weights(1, later_weights)]
    target = turn_target(following)

    temb = time_embed(timesteps, time_w1, time_w2)
    columns = [
        norm_gain[0], norm_shift[0], norm_gain[1], norm_shift[1], conv_bias[1],
        conv_bias[0] + temb[0], conv_bias[0] + temb[1],
    ]
    params = jnp.pad(jnp.stack(columns, axis=1), ((0, 0), (0, 128 - len(columns))))

    alpha = plan(timesteps)
    prior = plan(timesteps - resume_steps)
    variance = (1.0 - prior) / (1.0 - alpha) * (1.0 - alpha / prior)
    keep = (1.0 - prior) * jnp.sqrt(alpha / (prior * (1.0 - alpha)))
    ratio = jnp.sqrt(prior) / jnp.sqrt(alpha)
    coef = jnp.stack([ratio, keep - ratio * jnp.sqrt(1.0 - alpha)], axis=1).reshape(4)

    recv, turned, target = lax.optimization_barrier((recv, turned, target))
    hidden, sums, to_next, to_prev, near = first_conv(
        part, sums, params, first_pick, tap_pick, recv, turned[0]
    )
    from_prev = lax.ppermute(to_next, "ch", ring("ch", 1, False))
    from_next = lax.ppermute(to_prev, "ch", ring("ch", -1, False))
    sums = everywhere(sums, ("lon", "ch"))
    noise, terms = second_conv(
        part, coef, sums, params, second_pick, (near, from_prev, from_next),
        hidden, turned[1], recv, target,
    )
    squares = jnp.sum(everywhere(terms, ("lon", "ch")), axis=0)[:2]
    logprob = (
        -squares / (2.0 * variance) / float(LAT * 1024 * C)
        - 0.5 * jnp.log(variance)
        - 0.5 * math.log(2.0 * math.pi)
    )
    return (noise, logprob)


def solution(mesh):
    return jax.shard_map(
        body,
        mesh=mesh,
        in_specs=(
            P(None, None, "lon", "ch"),
            P("ch", None, "lon", None),
            P(), P(), P(), P(), P(), P(), P(), P(),
        ),
        out_specs=(P("ch", None, "lon", None), P()),
        check_vma=False,
    )
```

```python
import functools
import math

import jax
import jax.numpy as jnp
import numpy as np
from jax import lax
from jax.experimental import pallas as pl
from jax.experimental.pallas import tpu as pltpu
from jax.sharding import PartitionSpec as P

GROUPS = 32
C = 640
LAT = 96
ROWS = 12
COLS = 64
SRC = 8
PART = C // SRC
WIDTH = C // GROUPS
TAPS = 9
F32 = jnp.float32
BF16 = jnp.bfloat16
VMEM = pl.BlockSpec(memory_space=pltpu.VMEM)
SMEM = pl.BlockSpec(memory_space=pltpu.SMEM)
ANY = pl.BlockSpec(memory_space=pl.ANY)
CHUNK = 16
LIMIT = 56 * 2**20


def roll(x, by):
    by %= 128
    return x if by == 0 else pltpu.roll(x, by, 1)


def place(q):
    return 2 * q + 3


def side_lanes(of_left, of_right):
    out = np.zeros((128, 128), np.float32)
    for q in range(-1, 7):
        p = place(q)
        out[of_left(q), p] = 1
        out[of_left(q + 6), p + 64] = 1
        out[of_right(q), p + 63] = 1
        out[of_right(q + 6), p - 1] = 1
    return out.astype(BF16)


def halo_lane(s, side, row):
    return 32 * s + 16 * side + row + 1


def halo_taps():
    out = np.zeros((256, 3 * 128), np.float32)
    for k in range(3):
        for s in range(2):
            for side in range(2):
                for row in range(-2, 14):
                    source = 128 * s + 16 * (3 * side + k) + row + 2
                    out[source, 128 * k + halo_lane(s, side, row + 1)] = 1
    return out.astype(BF16)


def lanes(rows):
    return lax.broadcasted_iota(jnp.int32, (rows, 128), 1)


def members(rows, first, base):
    chan = lax.broadcasted_iota(jnp.int32, (rows, 128), 0) + first
    low = (lanes(rows) - base) * WIDTH
    return (chan >= low) & (chan < low + WIDTH)


def silu(x):
    return 0.5 * x * (1.0 + jnp.tanh(0.5 * x))


PARAMS = pltpu.CompilerParams(vmem_limit_bytes=LIMIT)


def sums_kernel(part_ref, cells_hbm, sums_ref, first_ref, last_ref, x, sems):
    half = COLS // 2
    copies = []
    for s in range(2):
        for c in range(2):
            cut = slice(c * half, (c + 1) * half)
            copies.append(
                pltpu.make_async_copy(cells_hbm.at[s, cut], x.at[s, cut], sems.at[2 * s + c])
            )
            copies[-1].start()
    row = jnp.zeros((1, 128), F32)
    for s in range(2):
        total = jnp.zeros((PART, LAT), F32)
        square = jnp.zeros((PART, LAT), F32)
        for c in range(2):
            copies[2 * s + c].wait()

            def add(i, carry):
                total, square = carry
                for j in range(4):
                    v = x[s, c * half + 4 * i + j].astype(F32)
                    total, square = total + v, square + v * v
                return total, square

            total, square = lax.fori_loop(0, half // 4, add, (total, square))
        for k, acc in enumerate((total, square)):
            column = jnp.sum(acc, axis=1, keepdims=True)
            own = members(PART, part_ref[0] * PART, 64 * k + 32 * s)
            row += jnp.sum(jnp.where(own, column, 0.0), axis=0, keepdims=True)
        first_ref[s] = x[s, 0:2]
        last_ref[s] = x[s, COLS - 2 : COLS]
    sums_ref[...] = row


def local_sums(part, cells):
    return pl.pallas_call(
        sums_kernel,
        in_specs=[SMEM, ANY],
        out_specs=[VMEM] * 3,
        out_shape=[
            jax.ShapeDtypeStruct((1, 128), F32),
            jax.ShapeDtypeStruct((2, 2, PART, LAT), BF16),
            jax.ShapeDtypeStruct((2, 2, PART, LAT), BF16),
        ],
        scratch_shapes=[pltpu.VMEM((2, COLS, PART, LAT), BF16), pltpu.SemaphoreType.DMA((4,))],
        compiler_params=PARAMS,
        name="local_sums",
    )(part, cells)


def pack_kernel(cells_hbm, pay_hbm, x, out, taken, turned, sems):
    fetches = [pltpu.make_async_copy(cells_hbm.at[s], x.at[s], sems.at[s]) for s in range(2)]
    for copy in fetches:
        copy.start()
    taken[...] = jnp.zeros_like(taken)
    turned[...] = jnp.zeros_like(turned)
    stores = [
        pltpu.make_async_copy(out.at[s], pay_hbm.at[:, 8 * s : 8 * s + 7], sems.at[2 + s])
        for s in range(2)
    ]
    fetches[0].wait()

    @pl.loop(0, 2 * PART // CHUNK)
    def _(step):
        s, e = step // (PART // CHUNK), step % (PART // CHUNK)

        @pl.when(step == PART // CHUNK)
        def _():
            stores[0].start()
            fetches[1].wait()

        own = pl.ds(pl.multiple_of(e * CHUNK, CHUNK), CHUNK)
        taken[:, 0:LAT] = x[s, :, own, :].astype(F32).reshape(COLS * CHUNK, LAT)
        for j in range(CHUNK):
            across = taken[pl.ds(j, COLS, stride=CHUNK), :].T
            turned[pl.ds(CHUNK + j, LAT, stride=CHUNK), 0:COLS] = across[0:LAT, :]

        def tile(r):
            return turned[CHUNK * (r + 1) : CHUNK * (r + 2), :]

        for d in range(SRC):
            for q in range(7):
                upper, lower = (d * ROWS + q, d * ROWS + q + 6)
                if q == 6:
                    upper, lower = (d * ROWS - 1, d * ROWS + ROWS)
                out[s, d, q, own, :] = (tile(upper) + roll(tile(lower), 64)).astype(BF16)

    stores[1].start()
    for store in stores:
        store.wait()


def pack(cells):
    return pl.pallas_call(
        pack_kernel,
        in_specs=[ANY],
        out_specs=ANY,
        out_shape=jax.ShapeDtypeStruct((SRC, 16, PART, 128), BF16),
        scratch_shapes=[
            pltpu.VMEM((2, COLS, PART, LAT), BF16),
            pltpu.VMEM((2, SRC, 7, PART, 128), BF16),
            pltpu.VMEM((COLS * CHUNK, 128), F32),
            pltpu.VMEM(((LAT + 8) * CHUNK, 128), F32),
            pltpu.SemaphoreType.DMA((4,)),
        ],
        compiler_params=PARAMS,
        cost_estimate=pl.CostEstimate(
            flops=1_000_000_000, bytes_accessed=8_000_000, transcendentals=0
        ),
        name="pack_latents",
    )(cells)


def halo_kernel(first_ref, last_ref, left_ref, right_ref, _, pay_hbm, out, sems):
    lane = lanes(PART)
    pad = jnp.zeros((PART, 128 - LAT), F32)

    @pl.loop(0, 2)
    def _(s):
        near = [left_ref[s, 0], left_ref[s, 1], first_ref[s, 0], last_ref[s, 1],
                right_ref[s, 0], right_ref[s, 1]]
        near = [jnp.concatenate([col.astype(F32), pad], axis=1) for col in near]
        for d in range(SRC):
            halo = jnp.zeros((PART, 128), F32)
            for kind in range(6):
                own = (lane >= 16 * kind) & (lane < 16 * kind + 16)
                halo = jnp.where(own, roll(near[kind], 16 * kind + 2 - d * ROWS), halo)
            out[s, d] = halo.astype(BF16)
        pltpu.make_async_copy(out.at[s], pay_hbm.at[:, 8 * s + 7], sems.at[s]).start()

    for s in range(2):
        pltpu.make_async_copy(out.at[s], pay_hbm.at[:, 8 * s + 7], sems.at[s]).wait()


def pack_halo(first, last, left, right, pay):
    return pl.pallas_call(
        halo_kernel,
        in_specs=[VMEM] * 4 + [ANY],
        out_specs=ANY,
        out_shape=jax.ShapeDtypeStruct((SRC, 16, PART, 128), BF16),
        scratch_shapes=[
            pltpu.VMEM((2, SRC, PART, 128), BF16),
            pltpu.SemaphoreType.DMA((2,)),
        ],
        input_output_aliases={4: 0},
        compiler_params=PARAMS,
        name="pack_halo",
    )(first, last, left, right, pay)


def weight_kernel(j, w_hbm, o_hbm, x, out, sems):
    for t in range(TAPS):
        pltpu.make_async_copy(w_hbm.at[j, t], x.at[t], sems.at[t]).start()

    @pl.loop(0, TAPS)
    def _(t):
        pltpu.make_async_copy(w_hbm.at[j, t], x.at[t], sems.at[t]).wait()
        out[t] = x[t].T
        cut = pl.ds(pl.multiple_of(t * C, 128), C)
        pltpu.make_async_copy(out.at[t], o_hbm.at[:, cut], sems.at[TAPS + t]).start()

    for t in range(TAPS):
        cut = slice(t * C, (t + 1) * C)
        pltpu.make_async_copy(out.at[t], o_hbm.at[:, cut], sems.at[TAPS + t]).wait()


def turn_weights(j, weights):
    return pl.pallas_call(
        functools.partial(weight_kernel, j),
        in_specs=[ANY],
        out_specs=ANY,
        out_shape=jax.ShapeDtypeStruct((C, TAPS * C), BF16),
        scratch_shapes=[
            pltpu.VMEM((TAPS, C, C), BF16),
            pltpu.VMEM((TAPS, C, C), BF16),
            pltpu.SemaphoreType.DMA((2 * TAPS,)),
        ],
        compiler_params=PARAMS,
        cost_estimate=pl.CostEstimate(
            flops=TAPS * 2 * C * C * 256, bytes_accessed=15_000_000, transcendentals=0
        ),
        name=f"turn_weights_{j}",
    )(weights.reshape(2, TAPS, C, C))


def target_kernel(target_hbm, o_hbm, x, out, sems):
    fetch = pltpu.make_async_copy(target_hbm, x, sems.at[0])
    fetch.start()
    fetch.wait()

    @pl.loop(0, 6)
    def _(q):
        for s in range(2):
            out[s, q] = jnp.concatenate([x[q, s], x[q + 6, s]], axis=0).T

    store = pltpu.make_async_copy(out, o_hbm, sems.at[1])
    store.start()
    store.wait()


def turn_target(target):
    return pl.pallas_call(
        target_kernel,
        in_specs=[ANY],
        out_specs=ANY,
        out_shape=jax.ShapeDtypeStruct((2, 6, C, 128), BF16),
        scratch_shapes=[
            pltpu.VMEM((ROWS, 2, COLS, C), BF16),
            pltpu.VMEM((2, 6, C, 128), BF16),
            pltpu.SemaphoreType.DMA((2,)),
        ],
        compiler_params=PARAMS,
        name="turn_target",
    )(target)


def affine(row, par_ref, s, j, scale, offset):
    count = float(LAT * 1024 * WIDTH)

    def of_channel(base):
        picked = jnp.where(members(C, 0, base), row, 0.0)
        return jnp.sum(picked, axis=1, keepdims=True) / count

    mean = of_channel(32 * s)
    spread = of_channel(64 + 32 * s) - mean * mean
    factor = lax.rsqrt(spread + 1e-05) * par_ref[:, 2 * j : 2 * j + 1]
    rest = par_ref[:, 2 * j + 1 : 2 * j + 2] - mean * factor
    scale[...] = jnp.broadcast_to(factor, scale.shape)
    offset[...] = jnp.broadcast_to(rest, offset.shape)


def spread_taps(xs, at, tiles, edge, sides, part):
    rows = PART
    lane = lanes(rows)
    low = lane < 64
    first = (lane == 0) | (lane == 64)
    last = (lane == 63) | (lane == 127)
    for q in range(-1, 7):
        if q == -1:
            tile = jnp.where(low, edge, roll(tiles[5], 64))
        elif q == 6:
            tile = jnp.where(low, roll(tiles[0], 64), edge)
        else:
            tile = tiles[q]
        side = roll(sides[pl.ds(at, rows), :], -place(q))
        taps = (jnp.where(first, side, roll(tile, 1)), tile, jnp.where(last, side, roll(tile, -1)))
        for k, tap in enumerate(taps):
            if q == -1:
                tap = jnp.where(low & (part == 0), 0.0, tap)
            elif q == 6:
                tap = jnp.where((~low) & (part == SRC - 1), 0.0, tap)
            xs[pl.ds(k * C + at, rows), 128 * (q + 1) : 128 * (q + 2)] = tap.astype(BF16)


def product(wv, xs, n, more=None):
    x = jnp.concatenate([xs[:, n + 128 * i : n + 128 * i + 256] for i in range(3)], axis=0)
    if more is not None:
        x = jnp.concatenate([x, more], axis=1)
    return jnp.dot(wv[...], x, preferred_element_type=F32)


def first_kernel(
    part_ref, sums_ref, par_ref, pick_ref, taps_ref, recv_hbm, w_hbm,
    hid_hbm, out_sums, to_next, to_prev, out_halo,
    xs, wv, scale, offset, recv, hid, sides, xh, sems,
):
    fetches = [
        pltpu.make_async_copy(recv_hbm.at[:, 8 * s : 8 * s + 8], recv.at[s], sems.at[s])
        for s in range(2)
    ]
    weights = pltpu.make_async_copy(w_hbm, wv, sems.at[2])
    for copy in (fetches[0], weights, fetches[1]):
        copy.start()
    part = part_ref[0]
    lane = lanes(C)

    def act(x, a, o):
        return silu(x.astype(F32) * a + o)

    def columns(s):
        fetches[s].wait()
        affine(sums_ref[...], par_ref, s, 0, scale.at[s], offset.at[s])
        r = (lane & 15) - 2
        outside = ((part == 0) & (r < 0)) | ((part == SRC - 1) & (r >= ROWS))
        x = act(recv[s, :, 7].reshape(C, 128), scale[s], offset[s])
        halo = jnp.where(outside, 0.0, x).astype(BF16)
        sides[s] = jnp.dot(halo, pick_ref[...], preferred_element_type=F32)
        return halo

    def prepare(s, b):
        at = b * PART if isinstance(b, int) else pl.multiple_of(b * PART, PART)
        a, o = scale[s, pl.ds(at, PART), :], offset[s, pl.ds(at, PART), :]
        tiles = [act(recv[s, b, q], a, o) for q in range(7)]
        spread_taps(xs.at[s], at, tiles[:6], tiles[6], sides.at[s], part)

    halo = columns(0)

    @pl.loop(0, SRC)
    def _(b):
        prepare(0, b)

    weights.wait()
    stores = []

    def put(s, n, value):
        part = hid.at[s, :, n : n + 256]
        part[...] = value + par_ref[:, 5 + s : 6 + s]
        store = pltpu.make_async_copy(
            part, hid_hbm.at[s, :, n : n + 256], sems.at[3 + 3 * s + n // 256]
        )
        store.start()
        stores.append(store)

    put(0, 0, product(wv, xs.at[0], 0))
    both = jnp.concatenate([halo, columns(1)], axis=1)
    for k in range(3):
        picked = jnp.dot(both, taps_ref[:, 128 * k : 128 * k + 128], preferred_element_type=F32)
        for i in range(3):
            t = 3 * i + k
            xh[C * t : C * (t + 1), :] = roll(picked, -i).astype(BF16)
    for n, blocks in ((256, (0, 1, 2, 3)), (512, (4, 5, 6, 7))):
        put(0, n, product(wv, xs.at[0], n))
        for b in blocks:
            prepare(1, b)
    put(1, 0, product(wv, xs.at[1], 0))
    put(1, 256, product(wv, xs.at[1], 256))
    out = product(wv, xs.at[1], 512, xh[...])
    put(1, 512, out[:, 0:256])
    bias = jnp.where(lane < 32, par_ref[:, 5:6], par_ref[:, 6:7])
    out_halo[...] = (out[:, 256:384] + bias).astype(BF16)

    row = jnp.zeros((1, 128), F32)
    low = lanes(128) < 64
    for at in range(0, C, 128):
        for s in range(2):
            pieces = [hid[s, at : at + 128, 128 * q : 128 * (q + 1)] for q in range(6)]
            for k in range(2):
                column = jnp.sum(sum(p * p if k else p for p in pieces), axis=1, keepdims=True)
                own = members(128, at, 64 * k + 32 * s)
                row += jnp.sum(jnp.where(own, column, 0.0), axis=0, keepdims=True)
        start, end = hid.at[:, at : at + 128, 0:128], hid.at[:, at : at + 128, 640:768]
        to_next[at : at + 128, :] = jnp.where(low, roll(end[0], 64), end[1]).astype(BF16)
        to_prev[at : at + 128, :] = jnp.where(low, start[0], roll(start[1], 64)).astype(BF16)
    out_sums[...] = jnp.broadcast_to(row, out_sums.shape)
    for store in stores:
        store.wait()


def first_conv(part, sums, params, pick, taps, recv, weights):
    tile = jax.ShapeDtypeStruct((C, 128), BF16)
    return pl.pallas_call(
        first_kernel,
        in_specs=[SMEM] + [VMEM] * 4 + [ANY] * 2,
        out_specs=[ANY] + [VMEM] * 4,
        out_shape=[
            jax.ShapeDtypeStruct((2, C, 768), F32),
            jax.ShapeDtypeStruct((128, 128), F32),
            tile, tile, tile,
        ],
        scratch_shapes=[
            pltpu.VMEM((2, 3 * C, 1024), BF16),
            pltpu.VMEM((C, TAPS * C), BF16),
            pltpu.VMEM((2, C, 128), F32),
            pltpu.VMEM((2, C, 128), F32),
            pltpu.VMEM((2, SRC, 8, PART, 128), BF16),
            pltpu.VMEM((2, C, 768), F32),
            pltpu.VMEM((2, C, 128), F32),
            pltpu.VMEM((TAPS * C, 128), BF16),
            pltpu.SemaphoreType.DMA((9,)),
        ],
        compiler_params=PARAMS,
        cost_estimate=pl.CostEstimate(
            flops=4 * 768 * C * C * 9, bytes_accessed=20_000_000, transcendentals=0
        ),
        name="first_conv",
    )(part, sums, params, pick, taps, recv, weights)


def second_kernel(
    part_ref, coef_ref, sums_ref, par_ref, pick_ref, near_ref, prev_ref, next_ref,
    hid_hbm, w_hbm, recv_hbm, target_hbm,
    noise_hbm, out_ref,
    xs, wv, hid, lat, target, noise_out, sides, scale, offset, sems,
):
    weights = pltpu.make_async_copy(w_hbm, wv, sems.at[6])
    fetches, later = [], []
    for s in range(2):
        fetches.append(pltpu.make_async_copy(hid_hbm.at[s], hid.at[s], sems.at[s]))
        tiles = recv_hbm.at[:, 8 * s : 8 * s + 6]
        later.append(pltpu.make_async_copy(tiles, lat.at[s], sems.at[2 + s]))
        later.append(pltpu.make_async_copy(target_hbm.at[s], target.at[s], sems.at[4 + s]))
    for copy in (fetches[0], weights, fetches[1], *later):
        copy.start()
    part = part_ref[0]
    row = jnp.sum(sums_ref[...], axis=0, keepdims=True)
    low = lanes(PART) < 64

    def columns(s):
        affine(row, par_ref, s, 1, scale.at[s], offset.at[s])
        halo = silu(near_ref[...].astype(F32) * scale[s] + offset[s]).astype(BF16)
        sides[s] = jnp.dot(halo, pick_ref[s], preferred_element_type=F32)
        fetches[s].wait()

    def prepare(s, b):
        at = b * PART if isinstance(b, int) else pl.multiple_of(b * PART, PART)
        rows = pl.ds(at, PART)
        a, o = scale[s, rows, :], offset[s, rows, :]

        def act(x):
            return silu(x * a + o)

        tiles = [act(hid[s, rows, 128 * q : 128 * (q + 1)]) for q in range(6)]
        above, below = prev_ref[rows, :].astype(F32), next_ref[rows, :].astype(F32)
        if s == 0:
            edge = jnp.where(low, above, roll(below, 64))
        else:
            edge = jnp.where(low, roll(above, 64), below)
        spread_taps(xs.at[s], at, tiles, act(edge), sides.at[s], part)

    def finish(s, n, acc):
        keep, gain = coef_ref[2 * s], coef_ref[2 * s + 1]
        out = product(wv, xs.at[s], n) + par_ref[:, 4:5]
        for h in range(2):
            q = n // 128 + h
            mine = lat[s, :, q].reshape(C, 128).astype(F32)
            noise = (out[:, 128 * h : 128 * h + 128] + mine).astype(BF16)
            center = keep * mine + gain * noise.astype(F32)
            diff = target[s, q].astype(F32) - center
            acc += jnp.sum((diff * diff).reshape(C // 8, 8, 128), axis=0)
            plain = noise.T
            noise_out[s, q] = plain[0:64]
            noise_out[s, q + 6] = plain[64:128]
        return acc

    columns(0)

    @pl.loop(0, SRC)
    def _(b):
        prepare(0, b)

    columns(1)
    weights.wait()
    for copy in later:
        copy.wait()
    result = jnp.zeros((1, 128), F32)
    stores = []
    for s in range(2):
        acc = jnp.zeros((8, 128), F32)
        for n, blocks in ((0, (0, 1, 2)), (256, (3, 4, 5)), (512, (6, 7))):
            acc = finish(s, n, acc)
            if s == 0:
                for b in blocks:
                    prepare(1, b)
        store = pltpu.make_async_copy(noise_out.at[s], noise_hbm.at[:, s], sems.at[7 + s])
        store.start()
        stores.append(store)
        value = jnp.sum(acc, axis=(0, 1), keepdims=True)
        result = jnp.where(lanes(1) == s, value, result)
    out_ref[...] = jnp.broadcast_to(result, out_ref.shape)
    for store in stores:
        store.wait()


def second_conv(part, coef, sums, params, pick, tiles, hidden, weights, recv, target):
    return pl.pallas_call(
        second_kernel,
        in_specs=[SMEM, SMEM] + [VMEM] * 6 + [ANY] * 4,
        out_specs=[ANY, VMEM],
        out_shape=[
            jax.ShapeDtypeStruct((ROWS, 2, COLS, C), BF16),
            jax.ShapeDtypeStruct((128, 128), F32),
        ],
        scratch_shapes=[
            pltpu.VMEM((2, 3 * C, 1024), BF16),
            pltpu.VMEM((C, TAPS * C), BF16),
            pltpu.VMEM((2, C, 768), F32),
            pltpu.VMEM((2, SRC, 6, PART, 128), BF16),
            pltpu.VMEM((2, 6, C, 128), BF16),
            pltpu.VMEM((2, ROWS, COLS, C), BF16),
            pltpu.VMEM((2, C, 128), F32),
            pltpu.VMEM((2, C, 128), F32),
            pltpu.VMEM((2, C, 128), F32),
            pltpu.SemaphoreType.DMA((9,)),
        ],
        compiler_params=PARAMS,
        cost_estimate=pl.CostEstimate(
            flops=4 * 768 * C * C * 9, bytes_accessed=20_000_000, transcendentals=0
        ),
        name="second_conv",
    )(part, coef, sums, params, pick, *tiles, hidden, weights, recv, target)


def time_embed(timesteps, time_w1, time_w2):
    half = time_w1.shape[0] // 2
    freqs = jnp.exp(-math.log(10000.0) * jnp.arange(half, dtype=F32) / half)
    angles = timesteps.astype(F32)[:, None] * freqs[None, :]
    features = jnp.concatenate([jnp.cos(angles), jnp.sin(angles)], axis=1)
    hidden = jax.nn.silu(jnp.dot(features, time_w1, precision=lax.Precision.HIGHEST))
    return jnp.dot(hidden, time_w2, precision=lax.Precision.HIGHEST)


def plan(steps):
    frac = steps.astype(F32) / 1000.0
    return jnp.cos((frac + 0.008) / 1.008 * (math.pi / 2.0)) ** 2


def everywhere(rows, axes):
    got = lax.all_to_all(rows.reshape(-1, 1, 128), axes, 0, 0, tiled=True)
    return got.reshape(-1, 128)


def ring(axis, step, wrap):
    size = lax.axis_size(axis)
    return [(i, (i + step) % size) for i in range(size) if wrap or 0 <= i + step < size]


def swap(array, axis):
    return lax.all_to_all(array, axis, split_axis=0, concat_axis=0, tiled=True)


def after(value, *others):
    return lax.optimization_barrier((value,) + others)[0]


def add_partner(x, axis, step):
    size = lax.axis_size(axis)
    return x + lax.ppermute(x, axis, [(i, i ^ step) for i in range(size)])


def body(
    latents, next_latents, timesteps, resume_steps, conv_weights, conv_bias,
    norm_gain, norm_shift, time_w1, time_w2,
):
    part = lax.axis_index("ch").astype(jnp.int32).reshape(1)
    first_pick = jnp.asarray(side_lanes(lambda r: 16 + r + 2, lambda r: 64 + r + 2))
    second_pick = jnp.asarray(
        np.stack(
            [
                side_lanes(lambda r: halo_lane(s, 0, r), lambda r: halo_lane(s, 1, r))
                for s in range(2)
            ]
        )
    )
    tap_pick = jnp.asarray(halo_taps())

    cells = latents.transpose(1, 2, 3, 0)
    sums, first, last = local_sums(part, cells)
    left = lax.ppermute(last, "lon", ring("lon", 1, True))
    right = lax.ppermute(first, "lon", ring("lon", -1, True))
    for step in (1, 2, 4):
        sums = add_partner(sums, "ch", step)
    pay = pack(after(cells, first))
    sums = add_partner(after(sums, pay), "lon", 8)
    pay = pack_halo(first, last, left, right, pay)
    pay, sums = lax.optimization_barrier((pay, sums))
    recv = swap(pay, "ch")
    for step in (1, 2, 4):
        sums = add_partner(sums, "lon", step)
    conv_weights, time_w1, following = after((conv_weights, time_w1, next_latents), pay)
    turned = [turn_weights(j, conv_weights) for j in range(2)]
    target = turn_target(following)

    temb = time_embed(timesteps, time_w1, time_w2)
    columns = [
        norm_gain[0], norm_shift[0], norm_gain[1], norm_shift[1], conv_bias[1],
        conv_bias[0] + temb[0], conv_bias[0] + temb[1],
    ]
    params = jnp.pad(jnp.stack(columns, axis=1), ((0, 0), (0, 128 - len(columns))))

    alpha = plan(timesteps)
    prior = plan(timesteps - resume_steps)
    variance = (1.0 - prior) / (1.0 - alpha) * (1.0 - alpha / prior)
    keep = (1.0 - prior) * jnp.sqrt(alpha / (prior * (1.0 - alpha)))
    ratio = jnp.sqrt(prior) / jnp.sqrt(alpha)
    coef = jnp.stack([ratio, keep - ratio * jnp.sqrt(1.0 - alpha)], axis=1).reshape(4)

    recv, turned, target = lax.optimization_barrier((recv, turned, target))
    hidden, sums, to_next, to_prev, near = first_conv(
        part, sums, params, first_pick, tap_pick, recv, turned[0]
    )
    from_prev = lax.ppermute(to_next, "ch", ring("ch", 1, False))
    from_next = lax.ppermute(to_prev, "ch", ring("ch", -1, False))
    sums = everywhere(sums, ("lon", "ch"))
    noise, terms = second_conv(
        part, coef, sums, params, second_pick, (near, from_prev, from_next),
        hidden, turned[1], recv, target,
    )
    squares = jnp.sum(everywhere(terms, ("lon", "ch")), axis=0)[:2]
    logprob = (
        -squares / (2.0 * variance) / float(LAT * 1024 * C)
        - 0.5 * jnp.log(variance)
        - 0.5 * math.log(2.0 * math.pi)
    )
    return (noise, logprob)


def solution(mesh):
    return jax.shard_map(
        body,
        mesh=mesh,
        in_specs=(
            P(None, None, "lon", "ch"),
            P("ch", None, "lon", None),
            P(), P(), P(), P(), P(), P(), P(), P(),
        ),
        out_specs=(P("ch", None, "lon", None), P()),
        check_vma=False,
    )
```

```python
import functools
import math

import jax
import jax.numpy as jnp
import numpy as np
from jax import lax
from jax.experimental import pallas as pl
from jax.experimental.pallas import tpu as pltpu
from jax.sharding import PartitionSpec as P

GROUPS = 32
C = 640
LAT = 96
ROWS = 12
COLS = 64
SRC = 8
PART = C // SRC
WIDTH = C // GROUPS
TAPS = 9
F32 = jnp.float32
BF16 = jnp.bfloat16
VMEM = pl.BlockSpec(memory_space=pltpu.VMEM)
SMEM = pl.BlockSpec(memory_space=pltpu.SMEM)
ANY = pl.BlockSpec(memory_space=pl.ANY)
CHUNK = 16
LIMIT = 56 * 2**20
SUMS = 96


def roll(x, by):
    by %= 128
    return x if by == 0 else pltpu.roll(x, by, 1)


def place(q):
    return 2 * q + 3


def side_lanes(of_left, of_right):
    out = np.zeros((128, 128), np.float32)
    for q in range(-1, 7):
        p = place(q)
        out[of_left(q), p] = 1
        out[of_left(q + 6), p + 64] = 1
        out[of_right(q), p + 63] = 1
        out[of_right(q + 6), p - 1] = 1
    return out.astype(BF16)


def halo_lane(s, side, row):
    return 32 * s + 16 * side + row + 1


def halo_taps():
    out = np.zeros((256, 3 * 128), np.float32)
    for k in range(3):
        for s in range(2):
            for side in range(2):
                for row in range(-2, 14):
                    source = 128 * s + 16 * (3 * side + k) + row + 2
                    out[source, 128 * k + halo_lane(s, side, row + 1)] = 1
    return out.astype(BF16)


def lanes(rows):
    return lax.broadcasted_iota(jnp.int32, (rows, 128), 1)


def members(rows, first, base):
    chan = lax.broadcasted_iota(jnp.int32, (rows, 128), 0) + first
    low = (lanes(rows) - base) * WIDTH
    return (chan >= low) & (chan < low + WIDTH)


def silu(x):
    return 0.5 * x * (1.0 + jnp.tanh(0.5 * x))


PARAMS = pltpu.CompilerParams(vmem_limit_bytes=LIMIT)


def sums_kernel(cells_hbm, sums_ref, first_ref, last_ref, x, sems):
    half = COLS // 2
    copies = []
    for s in range(2):
        for c in range(2):
            cut = slice(c * half, (c + 1) * half)
            copies.append(
                pltpu.make_async_copy(cells_hbm.at[s, cut], x.at[s, cut], sems.at[2 * s + c])
            )
            copies[-1].start()
    row = jnp.zeros((1, 128), F32)
    for s in range(2):
        total = jnp.zeros((PART, LAT), F32)
        square = jnp.zeros((PART, LAT), F32)
        for c in range(2):
            copies[2 * s + c].wait()

            def add(i, carry):
                total, square = carry
                for j in range(4):
                    v = x[s, c * half + 4 * i + j].astype(F32)
                    total, square = total + v, square + v * v
                return total, square

            total, square = lax.fori_loop(0, half // 4, add, (total, square))
        for k, acc in enumerate((total, square)):
            column = jnp.sum(acc, axis=1, keepdims=True)
            own = members(PART, 0, 64 * k + 32 * s)
            row += jnp.sum(jnp.where(own, column, 0.0), axis=0, keepdims=True)
        first_ref[s] = x[s, 0:2]
        last_ref[s] = x[s, COLS - 2 : COLS]
    sums_ref[...] = jnp.broadcast_to(row, sums_ref.shape)


def local_sums(cells):
    return pl.pallas_call(
        sums_kernel,
        in_specs=[ANY],
        out_specs=[VMEM] * 3,
        out_shape=[
            jax.ShapeDtypeStruct((16, 128), F32),
            jax.ShapeDtypeStruct((2, 2, PART, LAT), BF16),
            jax.ShapeDtypeStruct((2, 2, PART, LAT), BF16),
        ],
        scratch_shapes=[pltpu.VMEM((2, COLS, PART, LAT), BF16), pltpu.SemaphoreType.DMA((4,))],
        compiler_params=PARAMS,
        name="local_sums",
    )(cells)


def pack_kernel(cells_hbm, pay_hbm, x, out, taken, turned, sems):
    fetches = [pltpu.make_async_copy(cells_hbm.at[s], x.at[s], sems.at[s]) for s in range(2)]
    for copy in fetches:
        copy.start()
    taken[...] = jnp.zeros_like(taken)
    turned[...] = jnp.zeros_like(turned)
    stores = [
        pltpu.make_async_copy(out.at[s], pay_hbm.at[:, 8 * s : 8 * s + 7], sems.at[2 + s])
        for s in range(2)
    ]
    fetches[0].wait()

    @pl.loop(0, 2 * PART // CHUNK)
    def _(step):
        s, e = step // (PART // CHUNK), step % (PART // CHUNK)

        @pl.when(step == PART // CHUNK)
        def _():
            stores[0].start()
            fetches[1].wait()

        own = pl.ds(pl.multiple_of(e * CHUNK, CHUNK), CHUNK)
        taken[:, 0:LAT] = x[s, :, own, :].astype(F32).reshape(COLS * CHUNK, LAT)
        for j in range(CHUNK):
            across = taken[pl.ds(j, COLS, stride=CHUNK), :].T
            turned[pl.ds(CHUNK + j, LAT, stride=CHUNK), 0:COLS] = across[0:LAT, :]

        def tile(r):
            return turned[CHUNK * (r + 1) : CHUNK * (r + 2), :]

        for d in range(SRC):
            for q in range(7):
                upper, lower = (d * ROWS + q, d * ROWS + q + 6)
                if q == 6:
                    upper, lower = (d * ROWS - 1, d * ROWS + ROWS)
                out[s, d, q, own, :] = (tile(upper) + roll(tile(lower), 64)).astype(BF16)

    stores[1].start()
    for store in stores:
        store.wait()


def pack(cells):
    return pl.pallas_call(
        pack_kernel,
        in_specs=[ANY],
        out_specs=ANY,
        out_shape=jax.ShapeDtypeStruct((SRC, 16, PART, 128), BF16),
        scratch_shapes=[
            pltpu.VMEM((2, COLS, PART, LAT), BF16),
            pltpu.VMEM((2, SRC, 7, PART, 128), BF16),
            pltpu.VMEM((COLS * CHUNK, 128), F32),
            pltpu.VMEM(((LAT + 8) * CHUNK, 128), F32),
            pltpu.SemaphoreType.DMA((4,)),
        ],
        compiler_params=PARAMS,
        cost_estimate=pl.CostEstimate(
            flops=1_000_000_000, bytes_accessed=8_000_000, transcendentals=0
        ),
        name="pack_latents",
    )(cells)


def halo_kernel(sums_ref, first_ref, last_ref, left_ref, right_ref, _, pay_hbm, out, sems):
    lane = lanes(PART)
    pad = jnp.zeros((PART, 128 - LAT), F32)
    row = jnp.sum(sums_ref[...], axis=0, keepdims=True)

    @pl.loop(0, 2)
    def _(s):
        near = [left_ref[s, 0], left_ref[s, 1], first_ref[s, 0], last_ref[s, 1],
                right_ref[s, 0], right_ref[s, 1]]
        near = [jnp.concatenate([col.astype(F32), pad], axis=1) for col in near]
        carried = jnp.zeros((PART, 128), F32)
        for k in range(2):
            own = members(PART, 0, 64 * k + 32 * s)
            value = jnp.sum(jnp.where(own, row, 0.0), axis=1, keepdims=True)
            for piece in range(3):
                part = value.astype(BF16).astype(F32)
                carried = jnp.where(lane == SUMS + 3 * k + piece, part, carried)
                value = value - part
        for d in range(SRC):
            halo = carried
            for kind in range(6):
                own = (lane >= 16 * kind) & (lane < 16 * kind + 16)
                halo = jnp.where(own, roll(near[kind], 16 * kind + 2 - d * ROWS), halo)
            out[s, d] = halo.astype(BF16)
        pltpu.make_async_copy(out.at[s], pay_hbm.at[:, 8 * s + 7], sems.at[s]).start()

    for s in range(2):
        pltpu.make_async_copy(out.at[s], pay_hbm.at[:, 8 * s + 7], sems.at[s]).wait()


def pack_halo(sums, first, last, left, right, pay):
    return pl.pallas_call(
        halo_kernel,
        in_specs=[VMEM] * 5 + [ANY],
        out_specs=ANY,
        out_shape=jax.ShapeDtypeStruct((SRC, 16, PART, 128), BF16),
        scratch_shapes=[
            pltpu.VMEM((2, SRC, PART, 128), BF16),
            pltpu.SemaphoreType.DMA((2,)),
        ],
        input_output_aliases={5: 0},
        compiler_params=PARAMS,
        name="pack_halo",
    )(sums, first, last, left, right, pay)


def weight_kernel(j, w_hbm, o_hbm, x, out, sems):
    for t in range(TAPS):
        pltpu.make_async_copy(w_hbm.at[j, t], x.at[t], sems.at[t]).start()

    @pl.loop(0, TAPS)
    def _(t):
        pltpu.make_async_copy(w_hbm.at[j, t], x.at[t], sems.at[t]).wait()
        out[t] = x[t].T
        cut = pl.ds(pl.multiple_of(t * C, 128), C)
        pltpu.make_async_copy(out.at[t], o_hbm.at[:, cut], sems.at[TAPS + t]).start()

    for t in range(TAPS):
        cut = slice(t * C, (t + 1) * C)
        pltpu.make_async_copy(out.at[t], o_hbm.at[:, cut], sems.at[TAPS + t]).wait()


def turn_weights(j, weights):
    return pl.pallas_call(
        functools.partial(weight_kernel, j),
        in_specs=[ANY],
        out_specs=ANY,
        out_shape=jax.ShapeDtypeStruct((C, TAPS * C), BF16),
        scratch_shapes=[
            pltpu.VMEM((TAPS, C, C), BF16),
            pltpu.VMEM((TAPS, C, C), BF16),
            pltpu.SemaphoreType.DMA((2 * TAPS,)),
        ],
        compiler_params=PARAMS,
        cost_estimate=pl.CostEstimate(
            flops=TAPS * 2 * C * C * 256, bytes_accessed=15_000_000, transcendentals=0
        ),
        name=f"turn_weights_{j}",
    )(weights.reshape(2, TAPS, C, C))


def target_kernel(target_hbm, o_hbm, x, out, sems):
    fetch = pltpu.make_async_copy(target_hbm, x, sems.at[0])
    fetch.start()
    fetch.wait()

    @pl.loop(0, 6)
    def _(q):
        for s in range(2):
            out[s, q] = jnp.concatenate([x[q, s], x[q + 6, s]], axis=0).T

    store = pltpu.make_async_copy(out, o_hbm, sems.at[1])
    store.start()
    store.wait()


def turn_target(target):
    return pl.pallas_call(
        target_kernel,
        in_specs=[ANY],
        out_specs=ANY,
        out_shape=jax.ShapeDtypeStruct((2, 6, C, 128), BF16),
        scratch_shapes=[
            pltpu.VMEM((ROWS, 2, COLS, C), BF16),
            pltpu.VMEM((2, 6, C, 128), BF16),
            pltpu.SemaphoreType.DMA((2,)),
        ],
        compiler_params=PARAMS,
        name="turn_target",
    )(target)


def affine(total, square, par_ref, j, scale, offset):
    count = float(LAT * 1024 * WIDTH)
    mean = total / count
    spread = square / count - mean * mean
    factor = lax.rsqrt(spread + 1e-05) * par_ref[:, 2 * j : 2 * j + 1]
    rest = par_ref[:, 2 * j + 1 : 2 * j + 2] - mean * factor
    scale[...] = jnp.broadcast_to(factor, scale.shape)
    offset[...] = jnp.broadcast_to(rest, offset.shape)


def spread_taps(xs, at, tiles, edge, sides, part):
    rows = PART
    lane = lanes(rows)
    low = lane < 64
    first = (lane == 0) | (lane == 64)
    last = (lane == 63) | (lane == 127)
    for q in range(-1, 7):
        if q == -1:
            tile = jnp.where(low, edge, roll(tiles[5], 64))
        elif q == 6:
            tile = jnp.where(low, roll(tiles[0], 64), edge)
        else:
            tile = tiles[q]
        side = roll(sides[pl.ds(at, rows), :], -place(q))
        taps = (jnp.where(first, side, roll(tile, 1)), tile, jnp.where(last, side, roll(tile, -1)))
        for k, tap in enumerate(taps):
            if q == -1:
                tap = jnp.where(low & (part == 0), 0.0, tap)
            elif q == 6:
                tap = jnp.where((~low) & (part == SRC - 1), 0.0, tap)
            xs[pl.ds(k * C + at, rows), 128 * (q + 1) : 128 * (q + 2)] = tap.astype(BF16)


def product(wv, xs, n, more=None):
    x = jnp.concatenate([xs[:, n + 128 * i : n + 128 * i + 256] for i in range(3)], axis=0)
    if more is not None:
        x = jnp.concatenate([x, more], axis=1)
    return jnp.dot(wv[...], x, preferred_element_type=F32)


def first_kernel(
    part_ref, par_ref, pick_ref, taps_ref, recv_hbm, w_hbm,
    hid_hbm, out_sums, to_next, to_prev, out_halo,
    xs, wv, scale, offset, recv, hid, sides, xh, sems,
):
    fetches = [
        pltpu.make_async_copy(recv_hbm.at[:, 8 * s : 8 * s + 8], recv.at[s], sems.at[s])
        for s in range(2)
    ]
    weights = pltpu.make_async_copy(w_hbm, wv, sems.at[2])
    for copy in (fetches[0], weights, fetches[1]):
        copy.start()
    part = part_ref[0]
    lane = lanes(C)

    def act(x, a, o):
        return silu(x.astype(F32) * a + o)

    def columns(s):
        fetches[s].wait()
        tile = recv[s, :, 7].reshape(C, 128).astype(F32)
        total, square = (
            jnp.sum(jnp.where((lane >= at) & (lane < at + 3), tile, 0.0), axis=1, keepdims=True)
            for at in (SUMS, SUMS + 3)
        )
        affine(total, square, par_ref, 0, scale.at[s], offset.at[s])
        r = (lane & 15) - 2
        unused = lane >= SUMS
        outside = ((part == 0) & (r < 0)) | ((part == SRC - 1) & (r >= ROWS)) | unused
        x = act(jnp.where(unused, 0.0, tile), scale[s], offset[s])
        halo = jnp.where(outside, 0.0, x).astype(BF16)
        sides[s] = jnp.dot(halo, pick_ref[...], preferred_element_type=F32)
        return halo

    def prepare(s, b):
        at = b * PART if isinstance(b, int) else pl.multiple_of(b * PART, PART)
        a, o = scale[s, pl.ds(at, PART), :], offset[s, pl.ds(at, PART), :]
        tiles = [act(recv[s, b, q], a, o) for q in range(7)]
        spread_taps(xs.at[s], at, tiles[:6], tiles[6], sides.at[s], part)

    halo = columns(0)

    @pl.loop(0, SRC)
    def _(b):
        prepare(0, b)

    weights.wait()
    stores = []

    def put(s, n, value):
        part = hid.at[s, :, n : n + 256]
        part[...] = value + par_ref[:, 5 + s : 6 + s]
        store = pltpu.make_async_copy(
            part, hid_hbm.at[s, :, n : n + 256], sems.at[3 + 3 * s + n // 256]
        )
        store.start()
        stores.append(store)

    put(0, 0, product(wv, xs.at[0], 0))
    both = jnp.concatenate([halo, columns(1)], axis=1)
    for k in range(3):
        picked = jnp.dot(both, taps_ref[:, 128 * k : 128 * k + 128], preferred_element_type=F32)
        for i in range(3):
            t = 3 * i + k
            xh[C * t : C * (t + 1), :] = roll(picked, -i).astype(BF16)
    for n, blocks in ((256, (0, 1, 2, 3)), (512, (4, 5, 6, 7))):
        put(0, n, product(wv, xs.at[0], n))
        for b in blocks:
            prepare(1, b)
    put(1, 0, product(wv, xs.at[1], 0))
    put(1, 256, product(wv, xs.at[1], 256))
    out = product(wv, xs.at[1], 512, xh[...])
    put(1, 512, out[:, 0:256])
    bias = jnp.where(lane < 32, par_ref[:, 5:6], par_ref[:, 6:7])
    out_halo[...] = (out[:, 256:384] + bias).astype(BF16)

    row = jnp.zeros((1, 128), F32)
    low = lanes(128) < 64
    for at in range(0, C, 128):
        for s in range(2):
            pieces = [hid[s, at : at + 128, 128 * q : 128 * (q + 1)] for q in range(6)]
            for k in range(2):
                column = jnp.sum(sum(p * p if k else p for p in pieces), axis=1, keepdims=True)
                own = members(128, at, 64 * k + 32 * s)
                row += jnp.sum(jnp.where(own, column, 0.0), axis=0, keepdims=True)
        start, end = hid.at[:, at : at + 128, 0:128], hid.at[:, at : at + 128, 640:768]
        to_next[at : at + 128, :] = jnp.where(low, roll(end[0], 64), end[1]).astype(BF16)
        to_prev[at : at + 128, :] = jnp.where(low, start[0], roll(start[1], 64)).astype(BF16)
    out_sums[...] = jnp.broadcast_to(row, out_sums.shape)
    for store in stores:
        store.wait()


def first_conv(part, params, pick, taps, recv, weights):
    tile = jax.ShapeDtypeStruct((C, 128), BF16)
    return pl.pallas_call(
        first_kernel,
        in_specs=[SMEM] + [VMEM] * 3 + [ANY] * 2,
        out_specs=[ANY] + [VMEM] * 4,
        out_shape=[
            jax.ShapeDtypeStruct((2, C, 768), F32),
            jax.ShapeDtypeStruct((128, 128), F32),
            tile, tile, tile,
        ],
        scratch_shapes=[
            pltpu.VMEM((2, 3 * C, 1024), BF16),
            pltpu.VMEM((C, TAPS * C), BF16),
            pltpu.VMEM((2, C, 128), F32),
            pltpu.VMEM((2, C, 128), F32),
            pltpu.VMEM((2, SRC, 8, PART, 128), BF16),
            pltpu.VMEM((2, C, 768), F32),
            pltpu.VMEM((2, C, 128), F32),
            pltpu.VMEM((TAPS * C, 128), BF16),
            pltpu.SemaphoreType.DMA((9,)),
        ],
        compiler_params=PARAMS,
        cost_estimate=pl.CostEstimate(
            flops=4 * 768 * C * C * 9, bytes_accessed=20_000_000, transcendentals=0
        ),
        name="first_conv",
    )(part, params, pick, taps, recv, weights)


def second_kernel(
    part_ref, coef_ref, sums_ref, par_ref, pick_ref, near_ref, prev_ref, next_ref,
    hid_hbm, w_hbm, recv_hbm, target_hbm,
    noise_hbm, out_ref,
    xs, wv, hid, lat, target, noise_out, sides, scale, offset, sems,
):
    weights = pltpu.make_async_copy(w_hbm, wv, sems.at[6])
    fetches, later = [], []
    for s in range(2):
        fetches.append(pltpu.make_async_copy(hid_hbm.at[s], hid.at[s], sems.at[s]))
        tiles = recv_hbm.at[:, 8 * s : 8 * s + 6]
        later.append(pltpu.make_async_copy(tiles, lat.at[s], sems.at[2 + s]))
        later.append(pltpu.make_async_copy(target_hbm.at[s], target.at[s], sems.at[4 + s]))
    for copy in (fetches[0], weights, fetches[1], *later):
        copy.start()
    part = part_ref[0]
    row = jnp.sum(sums_ref[...], axis=0, keepdims=True)
    low = lanes(PART) < 64

    def columns(s):
        total, square = (
            jnp.sum(jnp.where(members(C, 0, base), row, 0.0), axis=1, keepdims=True)
            for base in (32 * s, 64 + 32 * s)
        )
        affine(total, square, par_ref, 1, scale.at[s], offset.at[s])
        halo = silu(near_ref[...].astype(F32) * scale[s] + offset[s]).astype(BF16)
        sides[s] = jnp.dot(halo, pick_ref[s], preferred_element_type=F32)
        fetches[s].wait()

    def prepare(s, b):
        at = b * PART if isinstance(b, int) else pl.multiple_of(b * PART, PART)
        rows = pl.ds(at, PART)
        a, o = scale[s, rows, :], offset[s, rows, :]

        def act(x):
            return silu(x * a + o)

        tiles = [act(hid[s, rows, 128 * q : 128 * (q + 1)]) for q in range(6)]
        above, below = prev_ref[rows, :].astype(F32), next_ref[rows, :].astype(F32)
        if s == 0:
            edge = jnp.where(low, above, roll(below, 64))
        else:
            edge = jnp.where(low, roll(above, 64), below)
        spread_taps(xs.at[s], at, tiles, act(edge), sides.at[s], part)

    def finish(s, n, acc):
        keep, gain = coef_ref[2 * s], coef_ref[2 * s + 1]
        out = product(wv, xs.at[s], n) + par_ref[:, 4:5]
        for h in range(2):
            q = n // 128 + h
            mine = lat[s, :, q].reshape(C, 128).astype(F32)
            noise = (out[:, 128 * h : 128 * h + 128] + mine).astype(BF16)
            center = keep * mine + gain * noise.astype(F32)
            diff = target[s, q].astype(F32) - center
            acc += jnp.sum((diff * diff).reshape(C // 8, 8, 128), axis=0)
            plain = noise.T
            noise_out[s, q] = plain[0:64]
            noise_out[s, q + 6] = plain[64:128]
        return acc

    columns(0)

    @pl.loop(0, SRC)
    def _(b):
        prepare(0, b)

    columns(1)
    weights.wait()
    for copy in later:
        copy.wait()
    result = jnp.zeros((1, 128), F32)
    stores = []
    for s in range(2):
        acc = jnp.zeros((8, 128), F32)
        for n, blocks in ((0, (0, 1, 2)), (256, (3, 4, 5)), (512, (6, 7))):
            acc = finish(s, n, acc)
            if s == 0:
                for b in blocks:
                    prepare(1, b)
        store = pltpu.make_async_copy(noise_out.at[s], noise_hbm.at[:, s], sems.at[7 + s])
        store.start()
        stores.append(store)
        value = jnp.sum(acc, axis=(0, 1), keepdims=True)
        result = jnp.where(lanes(1) == s, value, result)
    out_ref[...] = jnp.broadcast_to(result, out_ref.shape)
    for store in stores:
        store.wait()


def second_conv(part, coef, sums, params, pick, tiles, hidden, weights, recv, target):
    return pl.pallas_call(
        second_kernel,
        in_specs=[SMEM, SMEM] + [VMEM] * 6 + [ANY] * 4,
        out_specs=[ANY, VMEM],
        out_shape=[
            jax.ShapeDtypeStruct((ROWS, 2, COLS, C), BF16),
            jax.ShapeDtypeStruct((128, 128), F32),
        ],
        scratch_shapes=[
            pltpu.VMEM((2, 3 * C, 1024), BF16),
            pltpu.VMEM((C, TAPS * C), BF16),
            pltpu.VMEM((2, C, 768), F32),
            pltpu.VMEM((2, SRC, 6, PART, 128), BF16),
            pltpu.VMEM((2, 6, C, 128), BF16),
            pltpu.VMEM((2, ROWS, COLS, C), BF16),
            pltpu.VMEM((2, C, 128), F32),
            pltpu.VMEM((2, C, 128), F32),
            pltpu.VMEM((2, C, 128), F32),
            pltpu.SemaphoreType.DMA((9,)),
        ],
        compiler_params=PARAMS,
        cost_estimate=pl.CostEstimate(
            flops=4 * 768 * C * C * 9, bytes_accessed=20_000_000, transcendentals=0
        ),
        name="second_conv",
    )(part, coef, sums, params, pick, *tiles, hidden, weights, recv, target)


def time_embed(timesteps, time_w1, time_w2):
    half = time_w1.shape[0] // 2
    freqs = jnp.exp(-math.log(10000.0) * jnp.arange(half, dtype=F32) / half)
    angles = timesteps.astype(F32)[:, None] * freqs[None, :]
    features = jnp.concatenate([jnp.cos(angles), jnp.sin(angles)], axis=1)
    hidden = jax.nn.silu(jnp.dot(features, time_w1, precision=lax.Precision.HIGHEST))
    return jnp.dot(hidden, time_w2, precision=lax.Precision.HIGHEST)


def plan(steps):
    frac = steps.astype(F32) / 1000.0
    return jnp.cos((frac + 0.008) / 1.008 * (math.pi / 2.0)) ** 2


def everywhere(rows, axes):
    got = lax.all_to_all(rows.reshape(-1, 1, 128), axes, 0, 0, tiled=True)
    return got.reshape(-1, 128)


def ring(axis, step, wrap):
    size = lax.axis_size(axis)
    return [(i, (i + step) % size) for i in range(size) if wrap or 0 <= i + step < size]


def swap(array, axis):
    return lax.all_to_all(array, axis, split_axis=0, concat_axis=0, tiled=True)


def after(value, *others):
    return lax.optimization_barrier((value,) + others)[0]


def body(
    latents, next_latents, timesteps, resume_steps, conv_weights, conv_bias,
    norm_gain, norm_shift, time_w1, time_w2,
):
    part = lax.axis_index("ch").astype(jnp.int32).reshape(1)
    first_pick = jnp.asarray(side_lanes(lambda r: 16 + r + 2, lambda r: 64 + r + 2))
    second_pick = jnp.asarray(
        np.stack(
            [
                side_lanes(lambda r: halo_lane(s, 0, r), lambda r: halo_lane(s, 1, r))
                for s in range(2)
            ]
        )
    )
    tap_pick = jnp.asarray(halo_taps())

    cells = latents.transpose(1, 2, 3, 0)
    sums, first, last = local_sums(cells)
    sums = everywhere(sums, "lon")
    left = lax.ppermute(last, "lon", ring("lon", 1, True))
    right = lax.ppermute(first, "lon", ring("lon", -1, True))
    pay = pack(after(cells, first))
    pay = pack_halo(sums, first, last, left, right, pay)
    recv = swap(pay, "ch")
    conv_weights, time_w1, following = after((conv_weights, time_w1, next_latents), pay)
    turned = [turn_weights(j, conv_weights) for j in range(2)]
    target = turn_target(following)

    temb = time_embed(timesteps, time_w1, time_w2)
    columns = [
        norm_gain[0], norm_shift[0], norm_gain[1], norm_shift[1], conv_bias[1],
        conv_bias[0] + temb[0], conv_bias[0] + temb[1],
    ]
    params = jnp.pad(jnp.stack(columns, axis=1), ((0, 0), (0, 128 - len(columns))))

    alpha = plan(timesteps)
    prior = plan(timesteps - resume_steps)
    variance = (1.0 - prior) / (1.0 - alpha) * (1.0 - alpha / prior)
    keep = (1.0 - prior) * jnp.sqrt(alpha / (prior * (1.0 - alpha)))
    ratio = jnp.sqrt(prior) / jnp.sqrt(alpha)
    coef = jnp.stack([ratio, keep - ratio * jnp.sqrt(1.0 - alpha)], axis=1).reshape(4)

    recv, turned, target = lax.optimization_barrier((recv, turned, target))
    hidden, sums, to_next, to_prev, near = first_conv(
        part, params, first_pick, tap_pick, recv, turned[0]
    )
    from_prev = lax.ppermute(to_next, "ch", ring("ch", 1, False))
    from_next = lax.ppermute(to_prev, "ch", ring("ch", -1, False))
    sums = everywhere(sums, ("lon", "ch"))
    noise, terms = second_conv(
        part, coef, sums, params, second_pick, (near, from_prev, from_next),
        hidden, turned[1], recv, target,
    )
    squares = jnp.sum(everywhere(terms, ("lon", "ch")), axis=0)[:2]
    logprob = (
        -squares / (2.0 * variance) / float(LAT * 1024 * C)
        - 0.5 * jnp.log(variance)
        - 0.5 * math.log(2.0 * math.pi)
    )
    return (noise, logprob)


def solution(mesh):
    return jax.shard_map(
        body,
        mesh=mesh,
        in_specs=(
            P(None, None, "lon", "ch"),
            P("ch", None, "lon", None),
            P(), P(), P(), P(), P(), P(), P(), P(),
        ),
        out_specs=(P("ch", None, "lon", None), P()),
        check_vma=False,
    )
```

```python
import functools
import math

import jax
import jax.numpy as jnp
import numpy as np
from jax import lax
from jax.experimental import pallas as pl
from jax.experimental.pallas import tpu as pltpu
from jax.sharding import PartitionSpec as P

GROUPS = 32
C = 640
LAT = 96
ROWS = 12
COLS = 64
SRC = 8
PART = C // SRC
WIDTH = C // GROUPS
TAPS = 9
F32 = jnp.float32
BF16 = jnp.bfloat16
VMEM = pl.BlockSpec(memory_space=pltpu.VMEM)
SMEM = pl.BlockSpec(memory_space=pltpu.SMEM)
ANY = pl.BlockSpec(memory_space=pl.ANY)
CHUNK = 16
LIMIT = 56 * 2**20
SUMS = 96


def roll(x, by):
    by %= 128
    return x if by == 0 else pltpu.roll(x, by, 1)


def place(q):
    return 2 * q + 3


def side_lanes(of_left, of_right):
    out = np.zeros((128, 128), np.float32)
    for q in range(-1, 7):
        p = place(q)
        out[of_left(q), p] = 1
        out[of_left(q + 6), p + 64] = 1
        out[of_right(q), p + 63] = 1
        out[of_right(q + 6), p - 1] = 1
    return out.astype(BF16)


def halo_lane(s, side, row):
    return 32 * s + 16 * side + row + 1


def halo_taps():
    out = np.zeros((256, 3 * 128), np.float32)
    for k in range(3):
        for s in range(2):
            for side in range(2):
                for row in range(-2, 14):
                    source = 128 * s + 16 * (3 * side + k) + row + 2
                    out[source, 128 * k + halo_lane(s, side, row + 1)] = 1
    return out.astype(BF16)


def lanes(rows):
    return lax.broadcasted_iota(jnp.int32, (rows, 128), 1)


def members(rows, first, base):
    chan = lax.broadcasted_iota(jnp.int32, (rows, 128), 0) + first
    low = (lanes(rows) - base) * WIDTH
    return (chan >= low) & (chan < low + WIDTH)


def silu(x):
    return 0.5 * x * (1.0 + jnp.tanh(0.5 * x))


PARAMS = pltpu.CompilerParams(vmem_limit_bytes=LIMIT)


def sums_kernel(cells_hbm, sums_ref, first_ref, last_ref, x, sems):
    half = COLS // 2
    copies = []
    for s in range(2):
        for c in range(2):
            cut = slice(c * half, (c + 1) * half)
            copies.append(
                pltpu.make_async_copy(cells_hbm.at[s, cut], x.at[s, cut], sems.at[2 * s + c])
            )
            copies[-1].start()
    row = jnp.zeros((1, 128), F32)
    for s in range(2):
        total = jnp.zeros((PART, LAT), F32)
        square = jnp.zeros((PART, LAT), F32)
        for c in range(2):
            copies[2 * s + c].wait()

            def add(i, carry):
                total, square = carry
                for j in range(4):
                    v = x[s, c * half + 4 * i + j].astype(F32)
                    total, square = total + v, square + v * v
                return total, square

            total, square = lax.fori_loop(0, half // 4, add, (total, square))
        for k, acc in enumerate((total, square)):
            column = jnp.sum(acc, axis=1, keepdims=True)
            own = members(PART, 0, 64 * k + 32 * s)
            row += jnp.sum(jnp.where(own, column, 0.0), axis=0, keepdims=True)
        first_ref[s] = x[s, 0:2]
        last_ref[s] = x[s, COLS - 2 : COLS]
    sums_ref[...] = jnp.broadcast_to(row, sums_ref.shape)


def local_sums(cells):
    return pl.pallas_call(
        sums_kernel,
        in_specs=[ANY],
        out_specs=[VMEM] * 3,
        out_shape=[
            jax.ShapeDtypeStruct((16, 128), F32),
            jax.ShapeDtypeStruct((2, 2, PART, LAT), BF16),
            jax.ShapeDtypeStruct((2, 2, PART, LAT), BF16),
        ],
        scratch_shapes=[pltpu.VMEM((2, COLS, PART, LAT), BF16), pltpu.SemaphoreType.DMA((4,))],
        compiler_params=PARAMS,
        name="local_sums",
    )(cells)


def pack_kernel(cells_hbm, pay_hbm, x, out, taken, turned, sems):
    fetches = [pltpu.make_async_copy(cells_hbm.at[s], x.at[s], sems.at[s]) for s in range(2)]
    for copy in fetches:
        copy.start()
    taken[...] = jnp.zeros_like(taken)
    turned[...] = jnp.zeros_like(turned)
    low = lanes(8) < 64
    stores = [
        pltpu.make_async_copy(out.at[s], pay_hbm.at[:, 8 * s : 8 * s + 7], sems.at[2 + s])
        for s in range(2)
    ]
    fetches[0].wait()

    @pl.loop(0, 2 * PART // CHUNK)
    def _(step):
        s, e = step // (PART // CHUNK), step % (PART // CHUNK)

        @pl.when(step == PART // CHUNK)
        def _():
            stores[0].start()
            fetches[1].wait()

        own = pl.ds(pl.multiple_of(e * CHUNK, CHUNK), CHUNK)
        taken[:, 0:LAT] = x[s, :, own, :].astype(F32).reshape(COLS * CHUNK, LAT)
        for j in range(8):
            pair = [taken[pl.ds(j + 8 * h, COLS, stride=CHUNK), :] for h in range(2)]
            turned[pl.ds(8 + j, LAT, stride=8), :] = jnp.concatenate(pair, axis=0).T[0:LAT, :]

        def tile(upper, lower):
            upper, lower = (turned[8 * (r + 1) : 8 * (r + 2), :] for r in (upper, lower))
            halves = (jnp.where(low, upper, roll(lower, 64)), jnp.where(low, roll(upper, 64), lower))
            return jnp.concatenate(halves, axis=0).astype(BF16)

        for d in range(SRC):
            for q in range(7):
                upper, lower = (d * ROWS + q, d * ROWS + q + 6)
                if q == 6:
                    upper, lower = (d * ROWS - 1, d * ROWS + ROWS)
                out[s, d, q, own, :] = tile(upper, lower)

    stores[1].start()
    for store in stores:
        store.wait()


def pack(cells):
    return pl.pallas_call(
        pack_kernel,
        in_specs=[ANY],
        out_specs=ANY,
        out_shape=jax.ShapeDtypeStruct((SRC, 16, PART, 128), BF16),
        scratch_shapes=[
            pltpu.VMEM((2, COLS, PART, LAT), BF16),
            pltpu.VMEM((2, SRC, 7, PART, 128), BF16),
            pltpu.VMEM((COLS * CHUNK, 128), F32),
            pltpu.VMEM(((LAT + 8) * 8, 128), F32),
            pltpu.SemaphoreType.DMA((4,)),
        ],
        compiler_params=PARAMS,
        cost_estimate=pl.CostEstimate(
            flops=1_000_000_000, bytes_accessed=8_000_000, transcendentals=0
        ),
        name="pack_latents",
    )(cells)


def halo_kernel(sums_ref, first_ref, last_ref, left_ref, right_ref, _, pay_hbm, out, sems):
    lane = lanes(PART)
    pad = jnp.zeros((PART, 128 - LAT), F32)
    row = jnp.sum(sums_ref[...], axis=0, keepdims=True)

    @pl.loop(0, 2)
    def _(s):
        near = [left_ref[s, 0], left_ref[s, 1], first_ref[s, 0], last_ref[s, 1],
                right_ref[s, 0], right_ref[s, 1]]
        near = [jnp.concatenate([col.astype(F32), pad], axis=1) for col in near]
        carried = jnp.zeros((PART, 128), F32)
        for k in range(2):
            own = members(PART, 0, 64 * k + 32 * s)
            value = jnp.sum(jnp.where(own, row, 0.0), axis=1, keepdims=True)
            for piece in range(3):
                part = value.astype(BF16).astype(F32)
                carried = jnp.where(lane == SUMS + 3 * k + piece, part, carried)
                value = value - part
        for d in range(SRC):
            halo = carried
            for kind in range(6):
                own = (lane >= 16 * kind) & (lane < 16 * kind + 16)
                halo = jnp.where(own, roll(near[kind], 16 * kind + 2 - d * ROWS), halo)
            out[s, d] = halo.astype(BF16)
        pltpu.make_async_copy(out.at[s], pay_hbm.at[:, 8 * s + 7], sems.at[s]).start()

    for s in range(2):
        pltpu.make_async_copy(out.at[s], pay_hbm.at[:, 8 * s + 7], sems.at[s]).wait()


def pack_halo(sums, first, last, left, right, pay):
    return pl.pallas_call(
        halo_kernel,
        in_specs=[VMEM] * 5 + [ANY],
        out_specs=ANY,
        out_shape=jax.ShapeDtypeStruct((SRC, 16, PART, 128), BF16),
        scratch_shapes=[
            pltpu.VMEM((2, SRC, PART, 128), BF16),
            pltpu.SemaphoreType.DMA((2,)),
        ],
        input_output_aliases={5: 0},
        compiler_params=PARAMS,
        name="pack_halo",
    )(sums, first, last, left, right, pay)


def weight_kernel(j, w_hbm, o_hbm, x, out, sems):
    for t in range(TAPS):
        pltpu.make_async_copy(w_hbm.at[j, t], x.at[t], sems.at[t]).start()

    @pl.loop(0, TAPS)
    def _(t):
        pltpu.make_async_copy(w_hbm.at[j, t], x.at[t], sems.at[t]).wait()
        out[t] = x[t].T
        cut = pl.ds(pl.multiple_of(t * C, 128), C)
        pltpu.make_async_copy(out.at[t], o_hbm.at[:, cut], sems.at[TAPS + t]).start()

    for t in range(TAPS):
        cut = slice(t * C, (t + 1) * C)
        pltpu.make_async_copy(out.at[t], o_hbm.at[:, cut], sems.at[TAPS + t]).wait()


def turn_weights(j, weights):
    return pl.pallas_call(
        functools.partial(weight_kernel, j),
        in_specs=[ANY],
        out_specs=ANY,
        out_shape=jax.ShapeDtypeStruct((C, TAPS * C), BF16),
        scratch_shapes=[
            pltpu.VMEM((TAPS, C, C), BF16),
            pltpu.VMEM((TAPS, C, C), BF16),
            pltpu.SemaphoreType.DMA((2 * TAPS,)),
        ],
        compiler_params=PARAMS,
        cost_estimate=pl.CostEstimate(
            flops=TAPS * 2 * C * C * 256, bytes_accessed=15_000_000, transcendentals=0
        ),
        name=f"turn_weights_{j}",
    )(weights.reshape(2, TAPS, C, C))


def target_kernel(target_hbm, o_hbm, x, out, sems):
    fetch = pltpu.make_async_copy(target_hbm, x, sems.at[0])
    fetch.start()
    fetch.wait()

    @pl.loop(0, 6)
    def _(q):
        for s in range(2):
            out[s, q] = jnp.concatenate([x[q, s], x[q + 6, s]], axis=0).T

    store = pltpu.make_async_copy(out, o_hbm, sems.at[1])
    store.start()
    store.wait()


def turn_target(target):
    return pl.pallas_call(
        target_kernel,
        in_specs=[ANY],
        out_specs=ANY,
        out_shape=jax.ShapeDtypeStruct((2, 6, C, 128), BF16),
        scratch_shapes=[
            pltpu.VMEM((ROWS, 2, COLS, C), BF16),
            pltpu.VMEM((2, 6, C, 128), BF16),
            pltpu.SemaphoreType.DMA((2,)),
        ],
        compiler_params=PARAMS,
        name="turn_target",
    )(target)


def affine(total, square, par_ref, j, scale, offset):
    count = float(LAT * 1024 * WIDTH)
    mean = total / count
    spread = square / count - mean * mean
    factor = lax.rsqrt(spread + 1e-05) * par_ref[:, 2 * j : 2 * j + 1]
    rest = par_ref[:, 2 * j + 1 : 2 * j + 2] - mean * factor
    scale[...] = jnp.broadcast_to(factor, scale.shape)
    offset[...] = jnp.broadcast_to(rest, offset.shape)


def spread_taps(xs, at, tiles, edge, sides, part):
    rows = PART
    lane = lanes(rows)
    low = lane < 64
    first = (lane == 0) | (lane == 64)
    last = (lane == 63) | (lane == 127)
    for q in range(-1, 7):
        if q == -1:
            tile = jnp.where(low, edge, roll(tiles[5], 64))
        elif q == 6:
            tile = jnp.where(low, roll(tiles[0], 64), edge)
        else:
            tile = tiles[q]
        side = roll(sides[pl.ds(at, rows), :], -place(q))
        taps = (jnp.where(first, side, roll(tile, 1)), tile, jnp.where(last, side, roll(tile, -1)))
        for k, tap in enumerate(taps):
            if q == -1:
                tap = jnp.where(low & (part == 0), 0.0, tap)
            elif q == 6:
                tap = jnp.where((~low) & (part == SRC - 1), 0.0, tap)
            xs[pl.ds(k * C + at, rows), 128 * (q + 1) : 128 * (q + 2)] = tap.astype(BF16)


def product(wv, xs, n, more=None):
    x = jnp.concatenate([xs[:, n + 128 * i : n + 128 * i + 256] for i in range(3)], axis=0)
    if more is not None:
        x = jnp.concatenate([x, more], axis=1)
    return jnp.dot(wv[...], x, preferred_element_type=F32)


def first_kernel(
    part_ref, par_ref, pick_ref, taps_ref, recv_hbm, w_hbm,
    hid_hbm, out_sums, to_next, to_prev, out_halo,
    xs, wv, scale, offset, recv, hid, sides, xh, sems,
):
    fetches = [
        pltpu.make_async_copy(recv_hbm.at[:, 8 * s : 8 * s + 8], recv.at[s], sems.at[s])
        for s in range(2)
    ]
    weights = pltpu.make_async_copy(w_hbm, wv, sems.at[2])
    for copy in (fetches[0], weights, fetches[1]):
        copy.start()
    part = part_ref[0]
    lane = lanes(C)

    def act(x, a, o):
        return silu(x.astype(F32) * a + o)

    def columns(s):
        fetches[s].wait()
        tile = recv[s, :, 7].reshape(C, 128).astype(F32)
        total, square = (
            jnp.sum(jnp.where((lane >= at) & (lane < at + 3), tile, 0.0), axis=1, keepdims=True)
            for at in (SUMS, SUMS + 3)
        )
        affine(total, square, par_ref, 0, scale.at[s], offset.at[s])
        r = (lane & 15) - 2
        unused = lane >= SUMS
        outside = ((part == 0) & (r < 0)) | ((part == SRC - 1) & (r >= ROWS)) | unused
        x = act(jnp.where(unused, 0.0, tile), scale[s], offset[s])
        halo = jnp.where(outside, 0.0, x).astype(BF16)
        sides[s] = jnp.dot(halo, pick_ref[...], preferred_element_type=F32)
        return halo

    def prepare(s, b):
        at = b * PART if isinstance(b, int) else pl.multiple_of(b * PART, PART)
        a, o = scale[s, pl.ds(at, PART), :], offset[s, pl.ds(at, PART), :]
        tiles = [act(recv[s, b, q], a, o) for q in range(7)]
        spread_taps(xs.at[s], at, tiles[:6], tiles[6], sides.at[s], part)

    halo = columns(0)

    @pl.loop(0, SRC)
    def _(b):
        prepare(0, b)

    both = jnp.concatenate([halo, columns(1)], axis=1)
    for k in range(3):
        picked = jnp.dot(both, taps_ref[:, 128 * k : 128 * k + 128], preferred_element_type=F32)
        for i in range(3):
            t = 3 * i + k
            xh[C * t : C * (t + 1), :] = roll(picked, -i).astype(BF16)
    weights.wait()
    stores = []

    def put(s, n, value):
        part = hid.at[s, :, n : n + 256]
        part[...] = value + par_ref[:, 5 + s : 6 + s]
        store = pltpu.make_async_copy(
            part, hid_hbm.at[s, :, n : n + 256], sems.at[3 + 3 * s + n // 256]
        )
        store.start()
        stores.append(store)

    put(0, 0, product(wv, xs.at[0], 0))
    for n, blocks in ((256, (0, 1, 2, 3)), (512, (4, 5, 6, 7))):
        put(0, n, product(wv, xs.at[0], n))
        for b in blocks:
            prepare(1, b)
    put(1, 0, product(wv, xs.at[1], 0))
    put(1, 256, product(wv, xs.at[1], 256))
    out = product(wv, xs.at[1], 512, xh[...])
    put(1, 512, out[:, 0:256])
    bias = jnp.where(lane < 32, par_ref[:, 5:6], par_ref[:, 6:7])
    out_halo[...] = (out[:, 256:384] + bias).astype(BF16)

    row = jnp.zeros((1, 128), F32)
    low = lanes(128) < 64
    for at in range(0, C, 128):
        for s in range(2):
            pieces = [hid[s, at : at + 128, 128 * q : 128 * (q + 1)] for q in range(6)]
            for k in range(2):
                column = jnp.sum(sum(p * p if k else p for p in pieces), axis=1, keepdims=True)
                own = members(128, at, 64 * k + 32 * s)
                row += jnp.sum(jnp.where(own, column, 0.0), axis=0, keepdims=True)
        start, end = hid.at[:, at : at + 128, 0:128], hid.at[:, at : at + 128, 640:768]
        to_next[at : at + 128, :] = jnp.where(low, roll(end[0], 64), end[1]).astype(BF16)
        to_prev[at : at + 128, :] = jnp.where(low, start[0], roll(start[1], 64)).astype(BF16)
    out_sums[...] = jnp.broadcast_to(row, out_sums.shape)
    for store in stores:
        store.wait()


def first_conv(part, params, pick, taps, recv, weights):
    tile = jax.ShapeDtypeStruct((C, 128), BF16)
    return pl.pallas_call(
        first_kernel,
        in_specs=[SMEM] + [VMEM] * 3 + [ANY] * 2,
        out_specs=[ANY] + [VMEM] * 4,
        out_shape=[
            jax.ShapeDtypeStruct((2, C, 768), F32),
            jax.ShapeDtypeStruct((128, 128), F32),
            tile, tile, tile,
        ],
        scratch_shapes=[
            pltpu.VMEM((2, 3 * C, 1024), BF16),
            pltpu.VMEM((C, TAPS * C), BF16),
            pltpu.VMEM((2, C, 128), F32),
            pltpu.VMEM((2, C, 128), F32),
            pltpu.VMEM((2, SRC, 8, PART, 128), BF16),
            pltpu.VMEM((2, C, 768), F32),
            pltpu.VMEM((2, C, 128), F32),
            pltpu.VMEM((TAPS * C, 128), BF16),
            pltpu.SemaphoreType.DMA((9,)),
        ],
        compiler_params=PARAMS,
        cost_estimate=pl.CostEstimate(
            flops=4 * 768 * C * C * 9, bytes_accessed=20_000_000, transcendentals=0
        ),
        name="first_conv",
    )(part, params, pick, taps, recv, weights)


def second_kernel(
    part_ref, coef_ref, sums_ref, par_ref, pick_ref, near_ref, prev_ref, next_ref,
    hid_hbm, w_hbm, recv_hbm, target_hbm,
    noise_hbm, out_ref,
    xs, wv, hid, lat, target, noise_out, sides, scale, offset, sems,
):
    weights = pltpu.make_async_copy(w_hbm, wv, sems.at[6])
    fetches, later = [], []
    for s in range(2):
        fetches.append(pltpu.make_async_copy(hid_hbm.at[s], hid.at[s], sems.at[s]))
        tiles = recv_hbm.at[:, 8 * s : 8 * s + 6]
        later.append(pltpu.make_async_copy(tiles, lat.at[s], sems.at[2 + s]))
        later.append(pltpu.make_async_copy(target_hbm.at[s], target.at[s], sems.at[4 + s]))
    for copy in (fetches[0], weights, fetches[1], *later):
        copy.start()
    part = part_ref[0]
    row = jnp.sum(sums_ref[...], axis=0, keepdims=True)
    low = lanes(PART) < 64

    def columns(s):
        total, square = (
            jnp.sum(jnp.where(members(C, 0, base), row, 0.0), axis=1, keepdims=True)
            for base in (32 * s, 64 + 32 * s)
        )
        affine(total, square, par_ref, 1, scale.at[s], offset.at[s])
        halo = silu(near_ref[...].astype(F32) * scale[s] + offset[s]).astype(BF16)
        sides[s] = jnp.dot(halo, pick_ref[s], preferred_element_type=F32)
        fetches[s].wait()

    def prepare(s, b):
        at = b * PART if isinstance(b, int) else pl.multiple_of(b * PART, PART)
        rows = pl.ds(at, PART)
        a, o = scale[s, rows, :], offset[s, rows, :]

        def act(x):
            return silu(x * a + o)

        tiles = [act(hid[s, rows, 128 * q : 128 * (q + 1)]) for q in range(6)]
        above, below = prev_ref[rows, :].astype(F32), next_ref[rows, :].astype(F32)
        if s == 0:
            edge = jnp.where(low, above, roll(below, 64))
        else:
            edge = jnp.where(low, roll(above, 64), below)
        spread_taps(xs.at[s], at, tiles, act(edge), sides.at[s], part)

    def finish(s, n, acc):
        keep, gain = coef_ref[2 * s], coef_ref[2 * s + 1]
        out = product(wv, xs.at[s], n) + par_ref[:, 4:5]
        for h in range(2):
            q = n // 128 + h
            mine = lat[s, :, q].reshape(C, 128).astype(F32)
            noise = (out[:, 128 * h : 128 * h + 128] + mine).astype(BF16)
            center = keep * mine + gain * noise.astype(F32)
            diff = target[s, q].astype(F32) - center
            acc += jnp.sum((diff * diff).reshape(C // 8, 8, 128), axis=0)
            plain = noise.T
            noise_out[s, q] = plain[0:64]
            noise_out[s, q + 6] = plain[64:128]
        return acc

    columns(0)

    @pl.loop(0, SRC)
    def _(b):
        prepare(0, b)

    columns(1)
    weights.wait()
    for copy in later:
        copy.wait()
    result = jnp.zeros((1, 128), F32)
    stores = []
    for s in range(2):
        acc = jnp.zeros((8, 128), F32)
        for n, blocks in ((0, (0, 1, 2)), (256, (3, 4, 5)), (512, (6, 7))):
            acc = finish(s, n, acc)
            if s == 0:
                for b in blocks:
                    prepare(1, b)
        store = pltpu.make_async_copy(noise_out.at[s], noise_hbm.at[:, s], sems.at[7 + s])
        store.start()
        stores.append(store)
        value = jnp.sum(acc, axis=(0, 1), keepdims=True)
        result = jnp.where(lanes(1) == s, value, result)
    out_ref[...] = jnp.broadcast_to(result, out_ref.shape)
    for store in stores:
        store.wait()


def second_conv(part, coef, sums, params, pick, tiles, hidden, weights, recv, target):
    return pl.pallas_call(
        second_kernel,
        in_specs=[SMEM, SMEM] + [VMEM] * 6 + [ANY] * 4,
        out_specs=[ANY, VMEM],
        out_shape=[
            jax.ShapeDtypeStruct((ROWS, 2, COLS, C), BF16),
            jax.ShapeDtypeStruct((128, 128), F32),
        ],
        scratch_shapes=[
            pltpu.VMEM((2, 3 * C, 1024), BF16),
            pltpu.VMEM((C, TAPS * C), BF16),
            pltpu.VMEM((2, C, 768), F32),
            pltpu.VMEM((2, SRC, 6, PART, 128), BF16),
            pltpu.VMEM((2, 6, C, 128), BF16),
            pltpu.VMEM((2, ROWS, COLS, C), BF16),
            pltpu.VMEM((2, C, 128), F32),
            pltpu.VMEM((2, C, 128), F32),
            pltpu.VMEM((2, C, 128), F32),
            pltpu.SemaphoreType.DMA((9,)),
        ],
        compiler_params=PARAMS,
        cost_estimate=pl.CostEstimate(
            flops=4 * 768 * C * C * 9, bytes_accessed=20_000_000, transcendentals=0
        ),
        name="second_conv",
    )(part, coef, sums, params, pick, *tiles, hidden, weights, recv, target)


def time_embed(timesteps, time_w1, time_w2):
    half = time_w1.shape[0] // 2
    freqs = jnp.exp(-math.log(10000.0) * jnp.arange(half, dtype=F32) / half)
    angles = timesteps.astype(F32)[:, None] * freqs[None, :]
    features = jnp.concatenate([jnp.cos(angles), jnp.sin(angles)], axis=1)
    hidden = jax.nn.silu(jnp.dot(features, time_w1, precision=lax.Precision.HIGHEST))
    return jnp.dot(hidden, time_w2, precision=lax.Precision.HIGHEST)


def plan(steps):
    frac = steps.astype(F32) / 1000.0
    return jnp.cos((frac + 0.008) / 1.008 * (math.pi / 2.0)) ** 2


def everywhere(rows, axes):
    got = lax.all_to_all(rows.reshape(-1, 1, 128), axes, 0, 0, tiled=True)
    return got.reshape(-1, 128)


def ring(axis, step, wrap):
    size = lax.axis_size(axis)
    return [(i, (i + step) % size) for i in range(size) if wrap or 0 <= i + step < size]


def swap(array, axis):
    return lax.all_to_all(array, axis, split_axis=0, concat_axis=0, tiled=True)


def after(value, *others):
    return lax.optimization_barrier((value,) + others)[0]


def body(
    latents, next_latents, timesteps, resume_steps, conv_weights, conv_bias,
    norm_gain, norm_shift, time_w1, time_w2,
):
    part = lax.axis_index("ch").astype(jnp.int32).reshape(1)
    first_pick = jnp.asarray(side_lanes(lambda r: 16 + r + 2, lambda r: 64 + r + 2))
    second_pick = jnp.asarray(
        np.stack(
            [
                side_lanes(lambda r: halo_lane(s, 0, r), lambda r: halo_lane(s, 1, r))
                for s in range(2)
            ]
        )
    )
    tap_pick = jnp.asarray(halo_taps())

    cells = latents.transpose(1, 2, 3, 0)
    sums, first, last = local_sums(cells)
    sums = everywhere(sums, "lon")
    left = lax.ppermute(last, "lon", ring("lon", 1, True))
    right = lax.ppermute(first, "lon", ring("lon", -1, True))
    pay = pack(after(cells, first))
    pay = pack_halo(sums, first, last, left, right, pay)
    recv = swap(pay, "ch")
    conv_weights, time_w1, following = after((conv_weights, time_w1, next_latents), pay)
    turned = [turn_weights(j, conv_weights) for j in range(2)]
    target = turn_target(following)

    temb = time_embed(timesteps, time_w1, time_w2)
    columns = [
        norm_gain[0], norm_shift[0], norm_gain[1], norm_shift[1], conv_bias[1],
        conv_bias[0] + temb[0], conv_bias[0] + temb[1],
    ]
    params = jnp.pad(jnp.stack(columns, axis=1), ((0, 0), (0, 128 - len(columns))))

    alpha = plan(timesteps)
    prior = plan(timesteps - resume_steps)
    variance = (1.0 - prior) / (1.0 - alpha) * (1.0 - alpha / prior)
    keep = (1.0 - prior) * jnp.sqrt(alpha / (prior * (1.0 - alpha)))
    ratio = jnp.sqrt(prior) / jnp.sqrt(alpha)
    coef = jnp.stack([ratio, keep - ratio * jnp.sqrt(1.0 - alpha)], axis=1).reshape(4)

    recv, turned, target = lax.optimization_barrier((recv, turned, target))
    hidden, sums, to_next, to_prev, near = first_conv(
        part, params, first_pick, tap_pick, recv, turned[0]
    )
    from_prev = lax.ppermute(to_next, "ch", ring("ch", 1, False))
    from_next = lax.ppermute(to_prev, "ch", ring("ch", -1, False))
    sums = everywhere(sums, ("lon", "ch"))
    noise, terms = second_conv(
        part, coef, sums, params, second_pick, (near, from_prev, from_next),
        hidden, turned[1], recv, target,
    )
    squares = jnp.sum(everywhere(terms, ("lon", "ch")), axis=0)[:2]
    logprob = (
        -squares / (2.0 * variance) / float(LAT * 1024 * C)
        - 0.5 * jnp.log(variance)
        - 0.5 * math.log(2.0 * math.pi)
    )
    return (noise, logprob)


def solution(mesh):
    return jax.shard_map(
        body,
        mesh=mesh,
        in_specs=(
            P(None, None, "lon", "ch"),
            P("ch", None, "lon", None),
            P(), P(), P(), P(), P(), P(), P(), P(),
        ),
        out_specs=(P("ch", None, "lon", None), P()),
        check_vma=False,
    )
```

```python
import functools
import math

import jax
import jax.numpy as jnp
import numpy as np
from jax import lax
from jax.experimental import pallas as pl
from jax.experimental.pallas import tpu as pltpu
from jax.sharding import PartitionSpec as P

GROUPS = 32
C = 640
LAT = 96
ROWS = 12
COLS = 64
SRC = 8
PART = C // SRC
WIDTH = C // GROUPS
TAPS = 9
F32 = jnp.float32
BF16 = jnp.bfloat16
VMEM = pl.BlockSpec(memory_space=pltpu.VMEM)
SMEM = pl.BlockSpec(memory_space=pltpu.SMEM)
ANY = pl.BlockSpec(memory_space=pl.ANY)
CHUNK = 16
LIMIT = 56 * 2**20
SUMS = 96


def roll(x, by):
    by %= 128
    return x if by == 0 else pltpu.roll(x, by, 1)


def place(q):
    return 2 * q + 3


def side_lanes(of_left, of_right):
    out = np.zeros((128, 128), np.float32)
    for q in range(-1, 7):
        p = place(q)
        out[of_left(q), p] = 1
        out[of_left(q + 6), p + 64] = 1
        out[of_right(q), p + 63] = 1
        out[of_right(q + 6), p - 1] = 1
    return out.astype(BF16)


def halo_lane(s, side, row):
    return 32 * s + 16 * side + row + 1


def halo_taps():
    out = np.zeros((256, 3 * 128), np.float32)
    for k in range(3):
        for s in range(2):
            for side in range(2):
                for row in range(-2, 14):
                    source = 128 * s + 16 * (3 * side + k) + row + 2
                    out[source, 128 * k + halo_lane(s, side, row + 1)] = 1
    return out.astype(BF16)


def lanes(rows):
    return lax.broadcasted_iota(jnp.int32, (rows, 128), 1)


def members(rows, first, base):
    chan = lax.broadcasted_iota(jnp.int32, (rows, 128), 0) + first
    low = (lanes(rows) - base) * WIDTH
    return (chan >= low) & (chan < low + WIDTH)


def silu(x):
    return 0.5 * x * (1.0 + jnp.tanh(0.5 * x))


PARAMS = pltpu.CompilerParams(vmem_limit_bytes=LIMIT)


def sums_kernel(place_ref, cells_hbm, sums_ref, one_ref, other_ref, x, sems):
    half = COLS // 2
    copies = []
    for s in range(2):
        for c in range(2):
            cut = slice(c * half, (c + 1) * half)
            copies.append(
                pltpu.make_async_copy(cells_hbm.at[s, cut], x.at[s, cut], sems.at[2 * s + c])
            )
            copies[-1].start()
    row = jnp.zeros((1, 128), F32)
    for s in range(2):
        total = jnp.zeros((PART, LAT), F32)
        square = jnp.zeros((PART, LAT), F32)
        for c in range(2):
            copies[2 * s + c].wait()

            def add(i, carry):
                total, square = carry
                for j in range(4):
                    v = x[s, c * half + 4 * i + j].astype(F32)
                    total, square = total + v, square + v * v
                return total, square

            total, square = lax.fori_loop(0, half // 4, add, (total, square))
        for k, acc in enumerate((total, square)):
            column = jnp.sum(acc, axis=1, keepdims=True)
            own = members(PART, 0, 64 * k + 32 * s)
            row += jnp.sum(jnp.where(own, column, 0.0), axis=0, keepdims=True)
        even = place_ref[0] % 2 == 0
        first, last = x[s, 0:2].astype(F32), x[s, COLS - 2 : COLS].astype(F32)
        one_ref[s] = jnp.where(even, last, first).astype(BF16)
        other_ref[s] = jnp.where(even, first, last).astype(BF16)
    sums_ref[...] = jnp.broadcast_to(row, sums_ref.shape)


def local_sums(place, cells):
    return pl.pallas_call(
        sums_kernel,
        in_specs=[SMEM, ANY],
        out_specs=[VMEM] * 3,
        out_shape=[
            jax.ShapeDtypeStruct((16, 128), F32),
            jax.ShapeDtypeStruct((2, 2, PART, LAT), BF16),
            jax.ShapeDtypeStruct((2, 2, PART, LAT), BF16),
        ],
        scratch_shapes=[pltpu.VMEM((2, COLS, PART, LAT), BF16), pltpu.SemaphoreType.DMA((4,))],
        compiler_params=PARAMS,
        name="local_sums",
    )(place, cells)


def pack_kernel(cells_hbm, pay_hbm, x, out, taken, turned, sems):
    fetches = [pltpu.make_async_copy(cells_hbm.at[s], x.at[s], sems.at[s]) for s in range(2)]
    for copy in fetches:
        copy.start()
    taken[...] = jnp.zeros_like(taken)
    turned[...] = jnp.zeros_like(turned)
    low = lanes(8) < 64
    stores = [
        pltpu.make_async_copy(out.at[s], pay_hbm.at[:, 8 * s : 8 * s + 7], sems.at[2 + s])
        for s in range(2)
    ]
    fetches[0].wait()

    @pl.loop(0, 2 * PART // CHUNK)
    def _(step):
        s, e = step // (PART // CHUNK), step % (PART // CHUNK)

        @pl.when(step == PART // CHUNK)
        def _():
            stores[0].start()
            fetches[1].wait()

        own = pl.ds(pl.multiple_of(e * CHUNK, CHUNK), CHUNK)
        taken[:, 0:LAT] = x[s, :, own, :].astype(F32).reshape(COLS * CHUNK, LAT)
        for j in range(8):
            pair = [taken[pl.ds(j + 8 * h, COLS, stride=CHUNK), :] for h in range(2)]
            turned[pl.ds(8 + j, LAT, stride=8), :] = jnp.concatenate(pair, axis=0).T[0:LAT, :]

        def tile(upper, lower):
            upper, lower = (turned[8 * (r + 1) : 8 * (r + 2), :] for r in (upper, lower))
            halves = (jnp.where(low, upper, roll(lower, 64)), jnp.where(low, roll(upper, 64), lower))
            return jnp.concatenate(halves, axis=0).astype(BF16)

        for d in range(SRC):
            for q in range(7):
                upper, lower = (d * ROWS + q, d * ROWS + q + 6)
                if q == 6:
                    upper, lower = (d * ROWS - 1, d * ROWS + ROWS)
                out[s, d, q, own, :] = tile(upper, lower)

    stores[1].start()
    for store in stores:
        store.wait()


def pack(cells):
    return pl.pallas_call(
        pack_kernel,
        in_specs=[ANY],
        out_specs=ANY,
        out_shape=jax.ShapeDtypeStruct((SRC, 16, PART, 128), BF16),
        scratch_shapes=[
            pltpu.VMEM((2, COLS, PART, LAT), BF16),
            pltpu.VMEM((2, SRC, 7, PART, 128), BF16),
            pltpu.VMEM((COLS * CHUNK, 128), F32),
            pltpu.VMEM(((LAT + 8) * 8, 128), F32),
            pltpu.SemaphoreType.DMA((4,)),
        ],
        compiler_params=PARAMS,
        cost_estimate=pl.CostEstimate(
            flops=1_000_000_000, bytes_accessed=8_000_000, transcendentals=0
        ),
        name="pack_latents",
    )(cells)


def halo_kernel(
    place_ref, sums_ref, one_ref, other_ref, from_one, from_other, _, pay_hbm, out, sems,
):
    lane = lanes(PART)
    pad = jnp.zeros((PART, 128 - LAT), F32)
    row = jnp.sum(sums_ref[...], axis=0, keepdims=True)

    @pl.loop(0, 2)
    def _(s):
        even = place_ref[0] % 2 == 0
        one, other = one_ref[s].astype(F32), other_ref[s].astype(F32)
        first, last = jnp.where(even, other, one), jnp.where(even, one, other)
        one, other = from_one[s].astype(F32), from_other[s].astype(F32)
        left, right = jnp.where(even, other, one), jnp.where(even, one, other)
        near = [left[0], left[1], first[0], last[1], right[0], right[1]]
        near = [jnp.concatenate([col, pad], axis=1) for col in near]
        carried = jnp.zeros((PART, 128), F32)
        for k in range(2):
            own = members(PART, 0, 64 * k + 32 * s)
            value = jnp.sum(jnp.where(own, row, 0.0), axis=1, keepdims=True)
            for piece in range(3):
                part = value.astype(BF16).astype(F32)
                carried = jnp.where(lane == SUMS + 3 * k + piece, part, carried)
                value = value - part
        for d in range(SRC):
            halo = carried
            for kind in range(6):
                own = (lane >= 16 * kind) & (lane < 16 * kind + 16)
                halo = jnp.where(own, roll(near[kind], 16 * kind + 2 - d * ROWS), halo)
            out[s, d] = halo.astype(BF16)
        pltpu.make_async_copy(out.at[s], pay_hbm.at[:, 8 * s + 7], sems.at[s]).start()

    for s in range(2):
        pltpu.make_async_copy(out.at[s], pay_hbm.at[:, 8 * s + 7], sems.at[s]).wait()


def pack_halo(place, sums, ours, theirs, pay):
    return pl.pallas_call(
        halo_kernel,
        in_specs=[SMEM] + [VMEM] * 5 + [ANY],
        out_specs=ANY,
        out_shape=jax.ShapeDtypeStruct((SRC, 16, PART, 128), BF16),
        scratch_shapes=[
            pltpu.VMEM((2, SRC, PART, 128), BF16),
            pltpu.SemaphoreType.DMA((2,)),
        ],
        input_output_aliases={6: 0},
        compiler_params=PARAMS,
        name="pack_halo",
    )(place, sums, *ours, *theirs, pay)


def weight_kernel(j, w_hbm, o_hbm, x, out, sems):
    for t in range(TAPS):
        pltpu.make_async_copy(w_hbm.at[j, t], x.at[t], sems.at[t]).start()

    @pl.loop(0, TAPS)
    def _(t):
        pltpu.make_async_copy(w_hbm.at[j, t], x.at[t], sems.at[t]).wait()
        out[t] = x[t].T
        cut = pl.ds(pl.multiple_of(t * C, 128), C)
        pltpu.make_async_copy(out.at[t], o_hbm.at[:, cut], sems.at[TAPS + t]).start()

    for t in range(TAPS):
        cut = slice(t * C, (t + 1) * C)
        pltpu.make_async_copy(out.at[t], o_hbm.at[:, cut], sems.at[TAPS + t]).wait()


def turn_weights(j, weights):
    return pl.pallas_call(
        functools.partial(weight_kernel, j),
        in_specs=[ANY],
        out_specs=ANY,
        out_shape=jax.ShapeDtypeStruct((C, TAPS * C), BF16),
        scratch_shapes=[
            pltpu.VMEM((TAPS, C, C), BF16),
            pltpu.VMEM((TAPS, C, C), BF16),
            pltpu.SemaphoreType.DMA((2 * TAPS,)),
        ],
        compiler_params=PARAMS,
        cost_estimate=pl.CostEstimate(
            flops=TAPS * 2 * C * C * 256, bytes_accessed=15_000_000, transcendentals=0
        ),
        name=f"turn_weights_{j}",
    )(weights.reshape(2, TAPS, C, C))


def target_kernel(target_hbm, o_hbm, x, out, sems):
    fetch = pltpu.make_async_copy(target_hbm, x, sems.at[0])
    fetch.start()
    fetch.wait()

    @pl.loop(0, 6)
    def _(q):
        for s in range(2):
            out[s, q] = jnp.concatenate([x[q, s], x[q + 6, s]], axis=0).T

    store = pltpu.make_async_copy(out, o_hbm, sems.at[1])
    store.start()
    store.wait()


def turn_target(target):
    return pl.pallas_call(
        target_kernel,
        in_specs=[ANY],
        out_specs=ANY,
        out_shape=jax.ShapeDtypeStruct((2, 6, C, 128), BF16),
        scratch_shapes=[
            pltpu.VMEM((ROWS, 2, COLS, C), BF16),
            pltpu.VMEM((2, 6, C, 128), BF16),
            pltpu.SemaphoreType.DMA((2,)),
        ],
        compiler_params=PARAMS,
        name="turn_target",
    )(target)


def affine(total, square, par_ref, j, scale, offset):
    count = float(LAT * 1024 * WIDTH)
    mean = total / count
    spread = square / count - mean * mean
    factor = lax.rsqrt(spread + 1e-05) * par_ref[:, 2 * j : 2 * j + 1]
    rest = par_ref[:, 2 * j + 1 : 2 * j + 2] - mean * factor
    scale[...] = jnp.broadcast_to(factor, scale.shape)
    offset[...] = jnp.broadcast_to(rest, offset.shape)


def spread_taps(xs, at, tiles, edge, sides, part):
    rows = PART
    lane = lanes(rows)
    low = lane < 64
    first = (lane == 0) | (lane == 64)
    last = (lane == 63) | (lane == 127)
    for q in range(-1, 7):
        if q == -1:
            tile = jnp.where(low, edge, roll(tiles[5], 64))
        elif q == 6:
            tile = jnp.where(low, roll(tiles[0], 64), edge)
        else:
            tile = tiles[q]
        side = roll(sides[pl.ds(at, rows), :], -place(q))
        taps = (jnp.where(first, side, roll(tile, 1)), tile, jnp.where(last, side, roll(tile, -1)))
        for k, tap in enumerate(taps):
            if q == -1:
                tap = jnp.where(low & (part == 0), 0.0, tap)
            elif q == 6:
                tap = jnp.where((~low) & (part == SRC - 1), 0.0, tap)
            xs[pl.ds(k * C + at, rows), 128 * (q + 1) : 128 * (q + 2)] = tap.astype(BF16)


def product(wv, xs, n, more=None):
    x = jnp.concatenate([xs[:, n + 128 * i : n + 128 * i + 256] for i in range(3)], axis=0)
    if more is not None:
        x = jnp.concatenate([x, more], axis=1)
    return jnp.dot(wv[...], x, preferred_element_type=F32)


def first_kernel(
    part_ref, par_ref, pick_ref, taps_ref, recv_hbm, w_hbm,
    hid_hbm, out_sums, one, other, out_halo,
    xs, wv, scale, offset, recv, hid, sides, xh, sems,
):
    fetches = [
        pltpu.make_async_copy(recv_hbm.at[:, 8 * s : 8 * s + 8], recv.at[s], sems.at[s])
        for s in range(2)
    ]
    weights = pltpu.make_async_copy(w_hbm, wv, sems.at[2])
    for copy in (fetches[0], weights, fetches[1]):
        copy.start()
    part = part_ref[0]
    lane = lanes(C)

    def act(x, a, o):
        return silu(x.astype(F32) * a + o)

    def columns(s):
        fetches[s].wait()
        tile = recv[s, :, 7].reshape(C, 128).astype(F32)
        total, square = (
            jnp.sum(jnp.where((lane >= at) & (lane < at + 3), tile, 0.0), axis=1, keepdims=True)
            for at in (SUMS, SUMS + 3)
        )
        affine(total, square, par_ref, 0, scale.at[s], offset.at[s])
        r = (lane & 15) - 2
        unused = lane >= SUMS
        outside = ((part == 0) & (r < 0)) | ((part == SRC - 1) & (r >= ROWS)) | unused
        x = act(jnp.where(unused, 0.0, tile), scale[s], offset[s])
        halo = jnp.where(outside, 0.0, x).astype(BF16)
        sides[s] = jnp.dot(halo, pick_ref[...], preferred_element_type=F32)
        return halo

    def prepare(s, b):
        at = b * PART if isinstance(b, int) else pl.multiple_of(b * PART, PART)
        a, o = scale[s, pl.ds(at, PART), :], offset[s, pl.ds(at, PART), :]
        tiles = [act(recv[s, b, q], a, o) for q in range(7)]
        spread_taps(xs.at[s], at, tiles[:6], tiles[6], sides.at[s], part)

    halo = columns(0)

    @pl.loop(0, SRC)
    def _(b):
        prepare(0, b)

    both = jnp.concatenate([halo, columns(1)], axis=1)
    for k in range(3):
        picked = jnp.dot(both, taps_ref[:, 128 * k : 128 * k + 128], preferred_element_type=F32)
        for i in range(3):
            t = 3 * i + k
            xh[C * t : C * (t + 1), :] = roll(picked, -i).astype(BF16)
    weights.wait()
    stores = []

    def put(s, n, value):
        part = hid.at[s, :, n : n + 256]
        part[...] = value + par_ref[:, 5 + s : 6 + s]
        store = pltpu.make_async_copy(
            part, hid_hbm.at[s, :, n : n + 256], sems.at[3 + 3 * s + n // 256]
        )
        store.start()
        stores.append(store)

    put(0, 0, product(wv, xs.at[0], 0))
    for n, blocks in ((256, (0, 1, 2, 3)), (512, (4, 5, 6, 7))):
        put(0, n, product(wv, xs.at[0], n))
        for b in blocks:
            prepare(1, b)
    put(1, 0, product(wv, xs.at[1], 0))
    put(1, 256, product(wv, xs.at[1], 256))
    out = product(wv, xs.at[1], 512, xh[...])
    put(1, 512, out[:, 0:256])
    bias = jnp.where(lane < 32, par_ref[:, 5:6], par_ref[:, 6:7])
    out_halo[...] = (out[:, 256:384] + bias).astype(BF16)

    row = jnp.zeros((1, 128), F32)
    low = lanes(128) < 64
    even = part % 2 == 0
    for at in range(0, C, 128):
        for s in range(2):
            pieces = [hid[s, at : at + 128, 128 * q : 128 * (q + 1)] for q in range(6)]
            for k in range(2):
                column = jnp.sum(sum(p * p if k else p for p in pieces), axis=1, keepdims=True)
                own = members(128, at, 64 * k + 32 * s)
                row += jnp.sum(jnp.where(own, column, 0.0), axis=0, keepdims=True)
        start, end = hid.at[:, at : at + 128, 0:128], hid.at[:, at : at + 128, 640:768]
        after = jnp.where(low, roll(end[0], 64), end[1])
        ahead = jnp.where(low, start[0], roll(start[1], 64))
        one[at : at + 128, :] = jnp.where(even, after, ahead).astype(BF16)
        other[at : at + 128, :] = jnp.where(even, ahead, after).astype(BF16)
    out_sums[...] = jnp.broadcast_to(row, out_sums.shape)
    for store in stores:
        store.wait()


def first_conv(part, params, pick, taps, recv, weights):
    tile = jax.ShapeDtypeStruct((C, 128), BF16)
    return pl.pallas_call(
        first_kernel,
        in_specs=[SMEM] + [VMEM] * 3 + [ANY] * 2,
        out_specs=[ANY] + [VMEM] * 4,
        out_shape=[
            jax.ShapeDtypeStruct((2, C, 768), F32),
            jax.ShapeDtypeStruct((128, 128), F32),
            tile, tile, tile,
        ],
        scratch_shapes=[
            pltpu.VMEM((2, 3 * C, 1024), BF16),
            pltpu.VMEM((C, TAPS * C), BF16),
            pltpu.VMEM((2, C, 128), F32),
            pltpu.VMEM((2, C, 128), F32),
            pltpu.VMEM((2, SRC, 8, PART, 128), BF16),
            pltpu.VMEM((2, C, 768), F32),
            pltpu.VMEM((2, C, 128), F32),
            pltpu.VMEM((TAPS * C, 128), BF16),
            pltpu.SemaphoreType.DMA((9,)),
        ],
        compiler_params=PARAMS,
        cost_estimate=pl.CostEstimate(
            flops=4 * 768 * C * C * 9, bytes_accessed=20_000_000, transcendentals=0
        ),
        name="first_conv",
    )(part, params, pick, taps, recv, weights)


def second_kernel(
    part_ref, coef_ref, sums_ref, par_ref, pick_ref, near_ref, one_ref, other_ref,
    hid_hbm, w_hbm, recv_hbm, target_hbm,
    noise_hbm, out_ref,
    xs, wv, hid, lat, target, noise_out, sides, scale, offset, sems,
):
    weights = pltpu.make_async_copy(w_hbm, wv, sems.at[6])
    fetches, later = [], []
    for s in range(2):
        fetches.append(pltpu.make_async_copy(hid_hbm.at[s], hid.at[s], sems.at[s]))
        tiles = recv_hbm.at[:, 8 * s : 8 * s + 6]
        later.append(pltpu.make_async_copy(tiles, lat.at[s], sems.at[2 + s]))
        later.append(pltpu.make_async_copy(target_hbm.at[s], target.at[s], sems.at[4 + s]))
    for copy in (fetches[0], weights, fetches[1], *later):
        copy.start()
    part = part_ref[0]
    row = jnp.sum(sums_ref[...], axis=0, keepdims=True)
    low = lanes(PART) < 64
    even = part % 2 == 0

    def columns(s):
        total, square = (
            jnp.sum(jnp.where(members(C, 0, base), row, 0.0), axis=1, keepdims=True)
            for base in (32 * s, 64 + 32 * s)
        )
        affine(total, square, par_ref, 1, scale.at[s], offset.at[s])
        halo = silu(near_ref[...].astype(F32) * scale[s] + offset[s]).astype(BF16)
        sides[s] = jnp.dot(halo, pick_ref[s], preferred_element_type=F32)
        fetches[s].wait()

    def prepare(s, b):
        at = b * PART if isinstance(b, int) else pl.multiple_of(b * PART, PART)
        rows = pl.ds(at, PART)
        a, o = scale[s, rows, :], offset[s, rows, :]

        def act(x):
            return silu(x * a + o)

        tiles = [act(hid[s, rows, 128 * q : 128 * (q + 1)]) for q in range(6)]
        below, above = one_ref[rows, :].astype(F32), other_ref[rows, :].astype(F32)
        above, below = jnp.where(even, above, below), jnp.where(even, below, above)
        if s == 0:
            edge = jnp.where(low, above, roll(below, 64))
        else:
            edge = jnp.where(low, roll(above, 64), below)
        spread_taps(xs.at[s], at, tiles, act(edge), sides.at[s], part)

    def finish(s, n, acc):
        keep, gain = coef_ref[2 * s], coef_ref[2 * s + 1]
        out = product(wv, xs.at[s], n) + par_ref[:, 4:5]
        for h in range(2):
            q = n // 128 + h
            mine = lat[s, :, q].reshape(C, 128).astype(F32)
            noise = (out[:, 128 * h : 128 * h + 128] + mine).astype(BF16)
            center = keep * mine + gain * noise.astype(F32)
            diff = target[s, q].astype(F32) - center
            acc += jnp.sum((diff * diff).reshape(C // 8, 8, 128), axis=0)
            plain = noise.T
            noise_out[s, q] = plain[0:64]
            noise_out[s, q + 6] = plain[64:128]
        return acc

    columns(0)

    @pl.loop(0, SRC)
    def _(b):
        prepare(0, b)

    columns(1)
    weights.wait()
    for copy in later:
        copy.wait()
    result = jnp.zeros((1, 128), F32)
    stores = []
    for s in range(2):
        acc = jnp.zeros((8, 128), F32)
        for n, blocks in ((0, (0, 1, 2)), (256, (3, 4, 5)), (512, (6, 7))):
            acc = finish(s, n, acc)
            if s == 0:
                for b in blocks:
                    prepare(1, b)
        store = pltpu.make_async_copy(noise_out.at[s], noise_hbm.at[:, s], sems.at[7 + s])
        store.start()
        stores.append(store)
        value = jnp.sum(acc, axis=(0, 1), keepdims=True)
        result = jnp.where(lanes(1) == s, value, result)
    out_ref[...] = jnp.broadcast_to(result, out_ref.shape)
    for store in stores:
        store.wait()


def second_conv(part, coef, sums, params, pick, tiles, hidden, weights, recv, target):
    return pl.pallas_call(
        second_kernel,
        in_specs=[SMEM, SMEM] + [VMEM] * 6 + [ANY] * 4,
        out_specs=[ANY, VMEM],
        out_shape=[
            jax.ShapeDtypeStruct((ROWS, 2, COLS, C), BF16),
            jax.ShapeDtypeStruct((128, 128), F32),
        ],
        scratch_shapes=[
            pltpu.VMEM((2, 3 * C, 1024), BF16),
            pltpu.VMEM((C, TAPS * C), BF16),
            pltpu.VMEM((2, C, 768), F32),
            pltpu.VMEM((2, SRC, 6, PART, 128), BF16),
            pltpu.VMEM((2, 6, C, 128), BF16),
            pltpu.VMEM((2, ROWS, COLS, C), BF16),
            pltpu.VMEM((2, C, 128), F32),
            pltpu.VMEM((2, C, 128), F32),
            pltpu.VMEM((2, C, 128), F32),
            pltpu.SemaphoreType.DMA((9,)),
        ],
        compiler_params=PARAMS,
        cost_estimate=pl.CostEstimate(
            flops=4 * 768 * C * C * 9, bytes_accessed=20_000_000, transcendentals=0
        ),
        name="second_conv",
    )(part, coef, sums, params, pick, *tiles, hidden, weights, recv, target)


def time_embed(timesteps, time_w1, time_w2):
    half = time_w1.shape[0] // 2
    freqs = jnp.exp(-math.log(10000.0) * jnp.arange(half, dtype=F32) / half)
    angles = timesteps.astype(F32)[:, None] * freqs[None, :]
    features = jnp.concatenate([jnp.cos(angles), jnp.sin(angles)], axis=1)
    hidden = jax.nn.silu(jnp.dot(features, time_w1, precision=lax.Precision.HIGHEST))
    return jnp.dot(hidden, time_w2, precision=lax.Precision.HIGHEST)


def plan(steps):
    frac = steps.astype(F32) / 1000.0
    return jnp.cos((frac + 0.008) / 1.008 * (math.pi / 2.0)) ** 2


def everywhere(rows, axes):
    got = lax.all_to_all(rows.reshape(-1, 1, 128), axes, 0, 0, tiled=True)
    return got.reshape(-1, 128)


def swap_neighbours(one, other, axis, wrap):
    size = lax.axis_size(axis)
    pairs = [(i, i ^ 1) for i in range(size)]
    rest = [(i, (i + 1 if i % 2 else i - 1) % size) for i in range(size)]
    if not wrap:
        rest = rest[1:-1]
    return lax.ppermute(one, axis, pairs), lax.ppermute(other, axis, rest)


def swap(array, axis):
    return lax.all_to_all(array, axis, split_axis=0, concat_axis=0, tiled=True)


def after(value, *others):
    return lax.optimization_barrier((value,) + others)[0]


def body(
    latents, next_latents, timesteps, resume_steps, conv_weights, conv_bias,
    norm_gain, norm_shift, time_w1, time_w2,
):
    part = lax.axis_index("ch").astype(jnp.int32).reshape(1)
    first_pick = jnp.asarray(side_lanes(lambda r: 16 + r + 2, lambda r: 64 + r + 2))
    second_pick = jnp.asarray(
        np.stack(
            [
                side_lanes(lambda r: halo_lane(s, 0, r), lambda r: halo_lane(s, 1, r))
                for s in range(2)
            ]
        )
    )
    tap_pick = jnp.asarray(halo_taps())

    cells = latents.transpose(1, 2, 3, 0)
    place = lax.axis_index("lon").astype(jnp.int32).reshape(1)
    sums, *ours = local_sums(place, cells)
    sums = everywhere(sums, "lon")
    theirs = swap_neighbours(*ours, "lon", True)
    pay = pack(after(cells, ours[0]))
    pay = pack_halo(place, sums, ours, theirs, pay)
    recv = swap(pay, "ch")
    conv_weights, time_w1, following = after((conv_weights, time_w1, next_latents), pay)
    turned = [turn_weights(j, conv_weights) for j in range(2)]
    target = turn_target(following)

    temb = time_embed(timesteps, time_w1, time_w2)
    columns = [
        norm_gain[0], norm_shift[0], norm_gain[1], norm_shift[1], conv_bias[1],
        conv_bias[0] + temb[0], conv_bias[0] + temb[1],
    ]
    params = jnp.pad(jnp.stack(columns, axis=1), ((0, 0), (0, 128 - len(columns))))

    alpha = plan(timesteps)
    prior = plan(timesteps - resume_steps)
    variance = (1.0 - prior) / (1.0 - alpha) * (1.0 - alpha / prior)
    keep = (1.0 - prior) * jnp.sqrt(alpha / (prior * (1.0 - alpha)))
    ratio = jnp.sqrt(prior) / jnp.sqrt(alpha)
    coef = jnp.stack([ratio, keep - ratio * jnp.sqrt(1.0 - alpha)], axis=1).reshape(4)

    recv, turned, target = lax.optimization_barrier((recv, turned, target))
    hidden, sums, one, other, near = first_conv(
        part, params, first_pick, tap_pick, recv, turned[0]
    )
    one, other = swap_neighbours(one, other, "ch", False)
    sums = everywhere(sums, ("lon", "ch"))
    noise, terms = second_conv(
        part, coef, sums, params, second_pick, (near, one, other),
        hidden, turned[1], recv, target,
    )
    squares = jnp.sum(everywhere(terms, ("lon", "ch")), axis=0)[:2]
    logprob = (
        -squares / (2.0 * variance) / float(LAT * 1024 * C)
        - 0.5 * jnp.log(variance)
        - 0.5 * math.log(2.0 * math.pi)
    )
    return (noise, logprob)


def solution(mesh):
    return jax.shard_map(
        body,
        mesh=mesh,
        in_specs=(
            P(None, None, "lon", "ch"),
            P("ch", None, "lon", None),
            P(), P(), P(), P(), P(), P(), P(), P(),
        ),
        out_specs=(P("ch", None, "lon", None), P()),
        check_vma=False,
    )
```

```python
import functools
import math

import jax
import jax.numpy as jnp
import numpy as np
from jax import lax
from jax.experimental import pallas as pl
from jax.experimental.pallas import tpu as pltpu
from jax.sharding import PartitionSpec as P

GROUPS = 32
C = 640
LAT = 96
ROWS = 12
COLS = 64
SRC = 8
PART = C // SRC
WIDTH = C // GROUPS
TAPS = 9
F32 = jnp.float32
BF16 = jnp.bfloat16
VMEM = pl.BlockSpec(memory_space=pltpu.VMEM)
SMEM = pl.BlockSpec(memory_space=pltpu.SMEM)
ANY = pl.BlockSpec(memory_space=pl.ANY)
CHUNK = 16
LIMIT = 56 * 2**20
SUMS = 96


def roll(x, by):
    by %= 128
    return x if by == 0 else pltpu.roll(x, by, 1)


def place(q):
    return 2 * q + 3


def side_lanes(of_left, of_right):
    out = np.zeros((128, 128), np.float32)
    for q in range(-1, 7):
        p = place(q)
        out[of_left(q), p] = 1
        out[of_left(q + 6), p + 64] = 1
        out[of_right(q), p + 63] = 1
        out[of_right(q + 6), p - 1] = 1
    return out.astype(BF16)


def halo_lane(s, side, row):
    return 32 * s + 16 * side + row + 1


def halo_taps():
    out = np.zeros((256, 3 * 128), np.float32)
    for k in range(3):
        for s in range(2):
            for side in range(2):
                for row in range(-2, 14):
                    source = 128 * s + 16 * (3 * side + k) + row + 2
                    out[source, 128 * k + halo_lane(s, side, row + 1)] = 1
    return out.astype(BF16)


def lanes(rows):
    return lax.broadcasted_iota(jnp.int32, (rows, 128), 1)


def members(rows, first, base):
    chan = lax.broadcasted_iota(jnp.int32, (rows, 128), 0) + first
    low = (lanes(rows) - base) * WIDTH
    return (chan >= low) & (chan < low + WIDTH)


def silu_of_half(h):
    return h + h * jnp.tanh(h)


PARAMS = pltpu.CompilerParams(vmem_limit_bytes=LIMIT)


def sums_kernel(place_ref, cells_hbm, sums_ref, one_ref, other_ref, x, sems):
    half = COLS // 2
    copies = []
    for s in range(2):
        for c in range(2):
            cut = slice(c * half, (c + 1) * half)
            copies.append(
                pltpu.make_async_copy(cells_hbm.at[s, cut], x.at[s, cut], sems.at[2 * s + c])
            )
            copies[-1].start()
    row = jnp.zeros((1, 128), F32)
    for s in range(2):
        total = jnp.zeros((PART, LAT), F32)
        square = jnp.zeros((PART, LAT), F32)
        for c in range(2):
            copies[2 * s + c].wait()

            def add(i, carry):
                total, square = carry
                for j in range(4):
                    v = x[s, c * half + 4 * i + j].astype(F32)
                    total, square = total + v, square + v * v
                return total, square

            total, square = lax.fori_loop(0, half // 4, add, (total, square))
        for k, acc in enumerate((total, square)):
            column = jnp.sum(acc, axis=1, keepdims=True)
            own = members(PART, 0, 64 * k + 32 * s)
            row += jnp.sum(jnp.where(own, column, 0.0), axis=0, keepdims=True)
        even = place_ref[0] % 2 == 0
        first, last = x[s, 0:2].astype(F32), x[s, COLS - 2 : COLS].astype(F32)
        one_ref[s] = jnp.where(even, last, first).astype(BF16)
        other_ref[s] = jnp.where(even, first, last).astype(BF16)
    sums_ref[...] = jnp.broadcast_to(row, sums_ref.shape)


def local_sums(place, cells):
    return pl.pallas_call(
        sums_kernel,
        in_specs=[SMEM, ANY],
        out_specs=[VMEM] * 3,
        out_shape=[
            jax.ShapeDtypeStruct((16, 128), F32),
            jax.ShapeDtypeStruct((2, 2, PART, LAT), BF16),
            jax.ShapeDtypeStruct((2, 2, PART, LAT), BF16),
        ],
        scratch_shapes=[pltpu.VMEM((2, COLS, PART, LAT), BF16), pltpu.SemaphoreType.DMA((4,))],
        compiler_params=PARAMS,
        name="local_sums",
    )(place, cells)


def pack_kernel(cells_hbm, pay_hbm, x, out, taken, turned, sems):
    fetches = [pltpu.make_async_copy(cells_hbm.at[s], x.at[s], sems.at[s]) for s in range(2)]
    for copy in fetches:
        copy.start()
    taken[...] = jnp.zeros_like(taken)
    turned[...] = jnp.zeros_like(turned)
    low = lanes(8) < 64
    stores = [
        pltpu.make_async_copy(out.at[s], pay_hbm.at[:, 8 * s : 8 * s + 7], sems.at[2 + s])
        for s in range(2)
    ]
    fetches[0].wait()

    @pl.loop(0, 2 * PART // CHUNK)
    def _(step):
        s, e = step // (PART // CHUNK), step % (PART // CHUNK)

        @pl.when(step == PART // CHUNK)
        def _():
            stores[0].start()
            fetches[1].wait()

        own = pl.ds(pl.multiple_of(e * CHUNK, CHUNK), CHUNK)
        taken[:, 0:LAT] = x[s, :, own, :].astype(F32).reshape(COLS * CHUNK, LAT)
        for j in range(8):
            pair = [taken[pl.ds(j + 8 * h, COLS, stride=CHUNK), :] for h in range(2)]
            turned[pl.ds(8 + j, LAT, stride=8), :] = jnp.concatenate(pair, axis=0).T[0:LAT, :]

        def tile(upper, lower):
            upper, lower = (turned[8 * (r + 1) : 8 * (r + 2), :] for r in (upper, lower))
            halves = (jnp.where(low, upper, roll(lower, 64)), jnp.where(low, roll(upper, 64), lower))
            return jnp.concatenate(halves, axis=0).astype(BF16)

        for d in range(SRC):
            for q in range(7):
                upper, lower = (d * ROWS + q, d * ROWS + q + 6)
                if q == 6:
                    upper, lower = (d * ROWS - 1, d * ROWS + ROWS)
                out[s, d, q, own, :] = tile(upper, lower)

    stores[1].start()
    for store in stores:
        store.wait()


def pack(cells):
    return pl.pallas_call(
        pack_kernel,
        in_specs=[ANY],
        out_specs=ANY,
        out_shape=jax.ShapeDtypeStruct((SRC, 16, PART, 128), BF16),
        scratch_shapes=[
            pltpu.VMEM((2, COLS, PART, LAT), BF16),
            pltpu.VMEM((2, SRC, 7, PART, 128), BF16),
            pltpu.VMEM((COLS * CHUNK, 128), F32),
            pltpu.VMEM(((LAT + 8) * 8, 128), F32),
            pltpu.SemaphoreType.DMA((4,)),
        ],
        compiler_params=PARAMS,
        cost_estimate=pl.CostEstimate(
            flops=1_000_000_000, bytes_accessed=8_000_000, transcendentals=0
        ),
        name="pack_latents",
    )(cells)


def halo_kernel(
    place_ref, sums_ref, one_ref, other_ref, from_one, from_other, _, pay_hbm, out, sems,
):
    lane = lanes(PART)
    pad = jnp.zeros((PART, 128 - LAT), F32)
    row = jnp.sum(sums_ref[...], axis=0, keepdims=True)

    @pl.loop(0, 2)
    def _(s):
        even = place_ref[0] % 2 == 0
        one, other = one_ref[s].astype(F32), other_ref[s].astype(F32)
        first, last = jnp.where(even, other, one), jnp.where(even, one, other)
        one, other = from_one[s].astype(F32), from_other[s].astype(F32)
        left, right = jnp.where(even, other, one), jnp.where(even, one, other)
        near = [left[0], left[1], first[0], last[1], right[0], right[1]]
        near = [jnp.concatenate([col, pad], axis=1) for col in near]
        carried = jnp.zeros((PART, 128), F32)
        for k in range(2):
            own = members(PART, 0, 64 * k + 32 * s)
            value = jnp.sum(jnp.where(own, row, 0.0), axis=1, keepdims=True)
            for piece in range(3):
                part = value.astype(BF16).astype(F32)
                carried = jnp.where(lane == SUMS + 3 * k + piece, part, carried)
                value = value - part
        for d in range(SRC):
            halo = carried
            for kind in range(6):
                own = (lane >= 16 * kind) & (lane < 16 * kind + 16)
                halo = jnp.where(own, roll(near[kind], 16 * kind + 2 - d * ROWS), halo)
            out[s, d] = halo.astype(BF16)
        pltpu.make_async_copy(out.at[s], pay_hbm.at[:, 8 * s + 7], sems.at[s]).start()

    for s in range(2):
        pltpu.make_async_copy(out.at[s], pay_hbm.at[:, 8 * s + 7], sems.at[s]).wait()


def pack_halo(place, sums, ours, theirs, pay):
    return pl.pallas_call(
        halo_kernel,
        in_specs=[SMEM] + [VMEM] * 5 + [ANY],
        out_specs=ANY,
        out_shape=jax.ShapeDtypeStruct((SRC, 16, PART, 128), BF16),
        scratch_shapes=[
            pltpu.VMEM((2, SRC, PART, 128), BF16),
            pltpu.SemaphoreType.DMA((2,)),
        ],
        input_output_aliases={6: 0},
        compiler_params=PARAMS,
        name="pack_halo",
    )(place, sums, *ours, *theirs, pay)


def weight_kernel(j, w_hbm, o_hbm, x, out, sems):
    for t in range(TAPS):
        pltpu.make_async_copy(w_hbm.at[j, t], x.at[t], sems.at[t]).start()

    @pl.loop(0, TAPS)
    def _(t):
        pltpu.make_async_copy(w_hbm.at[j, t], x.at[t], sems.at[t]).wait()
        out[t] = x[t].T
        cut = pl.ds(pl.multiple_of(t * C, 128), C)
        pltpu.make_async_copy(out.at[t], o_hbm.at[:, cut], sems.at[TAPS + t]).start()

    for t in range(TAPS):
        cut = slice(t * C, (t + 1) * C)
        pltpu.make_async_copy(out.at[t], o_hbm.at[:, cut], sems.at[TAPS + t]).wait()


def turn_weights(j, weights):
    return pl.pallas_call(
        functools.partial(weight_kernel, j),
        in_specs=[ANY],
        out_specs=ANY,
        out_shape=jax.ShapeDtypeStruct((C, TAPS * C), BF16),
        scratch_shapes=[
            pltpu.VMEM((TAPS, C, C), BF16),
            pltpu.VMEM((TAPS, C, C), BF16),
            pltpu.SemaphoreType.DMA((2 * TAPS,)),
        ],
        compiler_params=PARAMS,
        cost_estimate=pl.CostEstimate(
            flops=TAPS * 2 * C * C * 256, bytes_accessed=15_000_000, transcendentals=0
        ),
        name=f"turn_weights_{j}",
    )(weights.reshape(2, TAPS, C, C))


def target_kernel(target_hbm, o_hbm, x, out, sems):
    fetch = pltpu.make_async_copy(target_hbm, x, sems.at[0])
    fetch.start()
    fetch.wait()

    @pl.loop(0, 6)
    def _(q):
        for s in range(2):
            out[s, q] = jnp.concatenate([x[q, s], x[q + 6, s]], axis=0).T

    store = pltpu.make_async_copy(out, o_hbm, sems.at[1])
    store.start()
    store.wait()


def turn_target(target):
    return pl.pallas_call(
        target_kernel,
        in_specs=[ANY],
        out_specs=ANY,
        out_shape=jax.ShapeDtypeStruct((2, 6, C, 128), BF16),
        scratch_shapes=[
            pltpu.VMEM((ROWS, 2, COLS, C), BF16),
            pltpu.VMEM((2, 6, C, 128), BF16),
            pltpu.SemaphoreType.DMA((2,)),
        ],
        compiler_params=PARAMS,
        name="turn_target",
    )(target)


def affine(total, square, par_ref, j, scale, offset):
    count = float(LAT * 1024 * WIDTH)
    mean = total / count
    spread = square / count - mean * mean
    factor = lax.rsqrt(spread + 1e-05) * par_ref[:, 2 * j : 2 * j + 1]
    rest = par_ref[:, 2 * j + 1 : 2 * j + 2] - mean * factor
    scale[...] = jnp.broadcast_to(0.5 * factor, scale.shape)
    offset[...] = jnp.broadcast_to(0.5 * rest, offset.shape)


def spread_taps(xs, at, tiles, edge, sides, part):
    rows = PART
    lane = lanes(rows)
    low = lane < 64
    first = (lane == 0) | (lane == 64)
    last = (lane == 63) | (lane == 127)
    tiles, edge = [tile.astype(BF16) for tile in tiles], edge.astype(BF16)
    zero = jnp.zeros((rows, 128), BF16)
    for q in range(-1, 7):
        if q == -1:
            tile = jnp.where(low, edge, roll(tiles[5], 64))
        elif q == 6:
            tile = jnp.where(low, roll(tiles[0], 64), edge)
        else:
            tile = tiles[q]
        side = roll(sides[pl.ds(at, rows), :], -place(q))
        taps = (jnp.where(first, side, roll(tile, 1)), tile, jnp.where(last, side, roll(tile, -1)))
        for k, tap in enumerate(taps):
            if q == -1:
                tap = jnp.where(low & (part == 0), zero, tap)
            elif q == 6:
                tap = jnp.where((~low) & (part == SRC - 1), zero, tap)
            xs[pl.ds(k * C + at, rows), 128 * (q + 1) : 128 * (q + 2)] = tap


def product(wv, xs, n, more=None):
    x = jnp.concatenate([xs[:, n + 128 * i : n + 128 * i + 256] for i in range(3)], axis=0)
    if more is not None:
        x = jnp.concatenate([x, more], axis=1)
    return jnp.dot(wv[...], x, preferred_element_type=F32)


def first_kernel(
    part_ref, par_ref, pick_ref, taps_ref, recv_hbm, w_hbm,
    hid_hbm, out_sums, one, other, out_halo,
    xs, wv, scale, offset, recv, hid, sides, xh, sems,
):
    fetches = [
        pltpu.make_async_copy(recv_hbm.at[:, 8 * s : 8 * s + 8], recv.at[s], sems.at[s])
        for s in range(2)
    ]
    weights = pltpu.make_async_copy(w_hbm, wv, sems.at[2])
    for copy in (fetches[0], weights, fetches[1]):
        copy.start()
    part = part_ref[0]
    lane = lanes(C)

    def act(x, a, o):
        return silu_of_half(x.astype(F32) * a + o)

    def columns(s):
        fetches[s].wait()
        tile = recv[s, :, 7].reshape(C, 128).astype(F32)
        total, square = (
            jnp.sum(jnp.where((lane >= at) & (lane < at + 3), tile, 0.0), axis=1, keepdims=True)
            for at in (SUMS, SUMS + 3)
        )
        affine(total, square, par_ref, 0, scale.at[s], offset.at[s])
        r = (lane & 15) - 2
        unused = lane >= SUMS
        outside = ((part == 0) & (r < 0)) | ((part == SRC - 1) & (r >= ROWS)) | unused
        x = act(jnp.where(unused, 0.0, tile), scale[s], offset[s])
        halo = jnp.where(outside, 0.0, x).astype(BF16)
        sides[s] = jnp.dot(halo, pick_ref[...], preferred_element_type=F32).astype(BF16)
        return halo

    def prepare(s, b):
        at = b * PART if isinstance(b, int) else pl.multiple_of(b * PART, PART)
        a, o = scale[s, pl.ds(at, PART), :], offset[s, pl.ds(at, PART), :]
        tiles = [act(recv[s, b, q], a, o) for q in range(7)]
        spread_taps(xs.at[s], at, tiles[:6], tiles[6], sides.at[s], part)

    halo = columns(0)

    @pl.loop(0, SRC)
    def _(b):
        prepare(0, b)

    both = jnp.concatenate([halo, columns(1)], axis=1)
    for k in range(3):
        picked = jnp.dot(both, taps_ref[:, 128 * k : 128 * k + 128], preferred_element_type=F32)
        for i in range(3):
            t = 3 * i + k
            xh[C * t : C * (t + 1), :] = roll(picked, -i).astype(BF16)
    weights.wait()
    stores = []

    def put(s, n, value):
        part = hid.at[s, :, n : n + 256]
        part[...] = value + par_ref[:, 5 + s : 6 + s]
        store = pltpu.make_async_copy(
            part, hid_hbm.at[s, :, n : n + 256], sems.at[3 + 3 * s + n // 256]
        )
        store.start()
        stores.append(store)

    put(0, 0, product(wv, xs.at[0], 0))
    for n, blocks in ((256, (0, 1, 2, 3)), (512, (4, 5, 6, 7))):
        put(0, n, product(wv, xs.at[0], n))
        for b in blocks:
            prepare(1, b)
    put(1, 0, product(wv, xs.at[1], 0))
    put(1, 256, product(wv, xs.at[1], 256))
    out = product(wv, xs.at[1], 512, xh[...])
    put(1, 512, out[:, 0:256])
    bias = jnp.where(lane < 32, par_ref[:, 5:6], par_ref[:, 6:7])
    out_halo[...] = (out[:, 256:384] + bias).astype(BF16)

    row = jnp.zeros((1, 128), F32)
    low = lanes(128) < 64
    even = part % 2 == 0
    for at in range(0, C, 128):
        for s in range(2):
            pieces = [hid[s, at : at + 128, 128 * q : 128 * (q + 1)] for q in range(6)]
            for k in range(2):
                column = jnp.sum(sum(p * p if k else p for p in pieces), axis=1, keepdims=True)
                own = members(128, at, 64 * k + 32 * s)
                row += jnp.sum(jnp.where(own, column, 0.0), axis=0, keepdims=True)
        start, end = hid.at[:, at : at + 128, 0:128], hid.at[:, at : at + 128, 640:768]
        after = jnp.where(low, roll(end[0], 64), end[1])
        ahead = jnp.where(low, start[0], roll(start[1], 64))
        one[at : at + 128, :] = jnp.where(even, after, ahead).astype(BF16)
        other[at : at + 128, :] = jnp.where(even, ahead, after).astype(BF16)
    out_sums[...] = jnp.broadcast_to(row, out_sums.shape)
    for store in stores:
        store.wait()


def first_conv(part, params, pick, taps, recv, weights):
    tile = jax.ShapeDtypeStruct((C, 128), BF16)
    return pl.pallas_call(
        first_kernel,
        in_specs=[SMEM] + [VMEM] * 3 + [ANY] * 2,
        out_specs=[ANY] + [VMEM] * 4,
        out_shape=[
            jax.ShapeDtypeStruct((2, C, 768), F32),
            jax.ShapeDtypeStruct((128, 128), F32),
            tile, tile, tile,
        ],
        scratch_shapes=[
            pltpu.VMEM((2, 3 * C, 1024), BF16),
            pltpu.VMEM((C, TAPS * C), BF16),
            pltpu.VMEM((2, C, 128), F32),
            pltpu.VMEM((2, C, 128), F32),
            pltpu.VMEM((2, SRC, 8, PART, 128), BF16),
            pltpu.VMEM((2, C, 768), F32),
            pltpu.VMEM((2, C, 128), BF16),
            pltpu.VMEM((TAPS * C, 128), BF16),
            pltpu.SemaphoreType.DMA((9,)),
        ],
        compiler_params=PARAMS,
        cost_estimate=pl.CostEstimate(
            flops=4 * 768 * C * C * 9, bytes_accessed=20_000_000, transcendentals=0
        ),
        name="first_conv",
    )(part, params, pick, taps, recv, weights)


def second_kernel(
    part_ref, coef_ref, sums_ref, par_ref, pick_ref, near_ref, one_ref, other_ref,
    hid_hbm, w_hbm, recv_hbm, target_hbm,
    noise_hbm, out_ref,
    xs, wv, hid, lat, target, noise_out, sides, scale, offset, sems,
):
    weights = pltpu.make_async_copy(w_hbm, wv, sems.at[6])
    fetches, later = [], []
    for s in range(2):
        fetches.append(pltpu.make_async_copy(hid_hbm.at[s], hid.at[s], sems.at[s]))
        tiles = recv_hbm.at[:, 8 * s : 8 * s + 6]
        later.append(pltpu.make_async_copy(tiles, lat.at[s], sems.at[2 + s]))
        later.append(pltpu.make_async_copy(target_hbm.at[s], target.at[s], sems.at[4 + s]))
    for copy in (fetches[0], weights, fetches[1], *later):
        copy.start()
    part = part_ref[0]
    row = jnp.sum(sums_ref[...], axis=0, keepdims=True)
    low = lanes(PART) < 64
    even = part % 2 == 0

    def columns(s):
        total, square = (
            jnp.sum(jnp.where(members(C, 0, base), row, 0.0), axis=1, keepdims=True)
            for base in (32 * s, 64 + 32 * s)
        )
        affine(total, square, par_ref, 1, scale.at[s], offset.at[s])
        halo = silu_of_half(near_ref[...].astype(F32) * scale[s] + offset[s]).astype(BF16)
        sides[s] = jnp.dot(halo, pick_ref[s], preferred_element_type=F32).astype(BF16)
        fetches[s].wait()

    def prepare(s, b):
        at = b * PART if isinstance(b, int) else pl.multiple_of(b * PART, PART)
        rows = pl.ds(at, PART)
        a, o = scale[s, rows, :], offset[s, rows, :]

        def act(x):
            return silu_of_half(x * a + o)

        tiles = [act(hid[s, rows, 128 * q : 128 * (q + 1)]) for q in range(6)]
        below, above = one_ref[rows, :].astype(F32), other_ref[rows, :].astype(F32)
        above, below = jnp.where(even, above, below), jnp.where(even, below, above)
        if s == 0:
            edge = jnp.where(low, above, roll(below, 64))
        else:
            edge = jnp.where(low, roll(above, 64), below)
        spread_taps(xs.at[s], at, tiles, act(edge), sides.at[s], part)

    def finish(s, n, acc):
        keep, gain = coef_ref[2 * s], coef_ref[2 * s + 1]
        out = product(wv, xs.at[s], n) + par_ref[:, 4:5]
        for h in range(2):
            q = n // 128 + h
            mine = lat[s, :, q].reshape(C, 128).astype(F32)
            noise = (out[:, 128 * h : 128 * h + 128] + mine).astype(BF16)
            center = keep * mine + gain * noise.astype(F32)
            diff = target[s, q].astype(F32) - center
            acc += jnp.sum((diff * diff).reshape(C // 8, 8, 128), axis=0)
            plain = noise.T
            noise_out[s, q] = plain[0:64]
            noise_out[s, q + 6] = plain[64:128]
        return acc

    columns(0)

    @pl.loop(0, SRC)
    def _(b):
        prepare(0, b)

    columns(1)
    weights.wait()
    for copy in later:
        copy.wait()
    result = jnp.zeros((1, 128), F32)
    stores = []
    for s in range(2):
        acc = jnp.zeros((8, 128), F32)
        for n, blocks in ((0, (0, 1, 2)), (256, (3, 4, 5)), (512, (6, 7))):
            acc = finish(s, n, acc)
            if s == 0:
                for b in blocks:
                    prepare(1, b)
        store = pltpu.make_async_copy(noise_out.at[s], noise_hbm.at[:, s], sems.at[7 + s])
        store.start()
        stores.append(store)
        value = jnp.sum(acc, axis=(0, 1), keepdims=True)
        result = jnp.where(lanes(1) == s, value, result)
    out_ref[...] = jnp.broadcast_to(result, out_ref.shape)
    for store in stores:
        store.wait()


def second_conv(part, coef, sums, params, pick, tiles, hidden, weights, recv, target):
    return pl.pallas_call(
        second_kernel,
        in_specs=[SMEM, SMEM] + [VMEM] * 6 + [ANY] * 4,
        out_specs=[ANY, VMEM],
        out_shape=[
            jax.ShapeDtypeStruct((ROWS, 2, COLS, C), BF16),
            jax.ShapeDtypeStruct((128, 128), F32),
        ],
        scratch_shapes=[
            pltpu.VMEM((2, 3 * C, 1024), BF16),
            pltpu.VMEM((C, TAPS * C), BF16),
            pltpu.VMEM((2, C, 768), F32),
            pltpu.VMEM((2, SRC, 6, PART, 128), BF16),
            pltpu.VMEM((2, 6, C, 128), BF16),
            pltpu.VMEM((2, ROWS, COLS, C), BF16),
            pltpu.VMEM((2, C, 128), BF16),
            pltpu.VMEM((2, C, 128), F32),
            pltpu.VMEM((2, C, 128), F32),
            pltpu.SemaphoreType.DMA((9,)),
        ],
        compiler_params=PARAMS,
        cost_estimate=pl.CostEstimate(
            flops=4 * 768 * C * C * 9, bytes_accessed=20_000_000, transcendentals=0
        ),
        name="second_conv",
    )(part, coef, sums, params, pick, *tiles, hidden, weights, recv, target)


def time_embed(timesteps, time_w1, time_w2):
    half = time_w1.shape[0] // 2
    freqs = jnp.exp(-math.log(10000.0) * jnp.arange(half, dtype=F32) / half)
    angles = timesteps.astype(F32)[:, None] * freqs[None, :]
    features = jnp.concatenate([jnp.cos(angles), jnp.sin(angles)], axis=1)
    hidden = jax.nn.silu(jnp.dot(features, time_w1, precision=lax.Precision.HIGHEST))
    return jnp.dot(hidden, time_w2, precision=lax.Precision.HIGHEST)


def plan(steps):
    frac = steps.astype(F32) / 1000.0
    return jnp.cos((frac + 0.008) / 1.008 * (math.pi / 2.0)) ** 2


def everywhere(rows, axes):
    got = lax.all_to_all(rows.reshape(-1, 1, 128), axes, 0, 0, tiled=True)
    return got.reshape(-1, 128)


def swap_neighbours(one, other, axis, wrap):
    size = lax.axis_size(axis)
    pairs = [(i, i ^ 1) for i in range(size)]
    rest = [(i, (i + 1 if i % 2 else i - 1) % size) for i in range(size)]
    if not wrap:
        rest = rest[1:-1]
    return lax.ppermute(one, axis, pairs), lax.ppermute(other, axis, rest)


def swap(array, axis):
    return lax.all_to_all(array, axis, split_axis=0, concat_axis=0, tiled=True)


def after(value, *others):
    return lax.optimization_barrier((value,) + others)[0]


def body(
    latents, next_latents, timesteps, resume_steps, conv_weights, conv_bias,
    norm_gain, norm_shift, time_w1, time_w2,
):
    part = lax.axis_index("ch").astype(jnp.int32).reshape(1)
    first_pick = jnp.asarray(side_lanes(lambda r: 16 + r + 2, lambda r: 64 + r + 2))
    second_pick = jnp.asarray(
        np.stack(
            [
                side_lanes(lambda r: halo_lane(s, 0, r), lambda r: halo_lane(s, 1, r))
                for s in range(2)
            ]
        )
    )
    tap_pick = jnp.asarray(halo_taps())

    cells = latents.transpose(1, 2, 3, 0)
    place = lax.axis_index("lon").astype(jnp.int32).reshape(1)
    sums, *ours = local_sums(place, cells)
    sums = everywhere(sums, "lon")
    theirs = swap_neighbours(*ours, "lon", True)
    pay = pack(after(cells, ours[0]))
    pay = pack_halo(place, sums, ours, theirs, pay)
    recv = swap(pay, "ch")
    conv_weights, time_w1, following = after((conv_weights, time_w1, next_latents), pay)
    turned = [turn_weights(j, conv_weights) for j in range(2)]
    target = turn_target(following)

    temb = time_embed(timesteps, time_w1, time_w2)
    columns = [
        norm_gain[0], norm_shift[0], norm_gain[1], norm_shift[1], conv_bias[1],
        conv_bias[0] + temb[0], conv_bias[0] + temb[1],
    ]
    params = jnp.pad(jnp.stack(columns, axis=1), ((0, 0), (0, 128 - len(columns))))

    alpha = plan(timesteps)
    prior = plan(timesteps - resume_steps)
    variance = (1.0 - prior) / (1.0 - alpha) * (1.0 - alpha / prior)
    keep = (1.0 - prior) * jnp.sqrt(alpha / (prior * (1.0 - alpha)))
    ratio = jnp.sqrt(prior) / jnp.sqrt(alpha)
    coef = jnp.stack([ratio, keep - ratio * jnp.sqrt(1.0 - alpha)], axis=1).reshape(4)

    recv, turned, target = lax.optimization_barrier((recv, turned, target))
    hidden, sums, one, other, near = first_conv(
        part, params, first_pick, tap_pick, recv, turned[0]
    )
    one, other = swap_neighbours(one, other, "ch", False)
    sums = everywhere(sums, ("lon", "ch"))
    noise, terms = second_conv(
        part, coef, sums, params, second_pick, (near, one, other),
        hidden, turned[1], recv, target,
    )
    squares = jnp.sum(everywhere(terms, ("lon", "ch")), axis=0)[:2]
    logprob = (
        -squares / (2.0 * variance) / float(LAT * 1024 * C)
        - 0.5 * jnp.log(variance)
        - 0.5 * math.log(2.0 * math.pi)
    )
    return (noise, logprob)


def solution(mesh):
    return jax.shard_map(
        body,
        mesh=mesh,
        in_specs=(
            P(None, None, "lon", "ch"),
            P("ch", None, "lon", None),
            P(), P(), P(), P(), P(), P(), P(), P(),
        ),
        out_specs=(P("ch", None, "lon", None), P()),
        check_vma=False,
    )
```

```python
import functools
import math

import jax
import jax.numpy as jnp
import numpy as np
from jax import lax
from jax.experimental import pallas as pl
from jax.experimental.pallas import tpu as pltpu
from jax.sharding import PartitionSpec as P

GROUPS = 32
C = 640
LAT = 96
ROWS = 12
COLS = 64
SRC = 8
PART = C // SRC
WIDTH = C // GROUPS
TAPS = 9
F32 = jnp.float32
BF16 = jnp.bfloat16
VMEM = pl.BlockSpec(memory_space=pltpu.VMEM)
SMEM = pl.BlockSpec(memory_space=pltpu.SMEM)
ANY = pl.BlockSpec(memory_space=pl.ANY)
CHUNK = 16
LIMIT = 56 * 2**20
SUMS = 96


def roll(x, by):
    by %= 128
    return x if by == 0 else pltpu.roll(x, by, 1)


def place(q):
    return 2 * q + 3


def side_lanes(of_left, of_right):
    out = np.zeros((128, 128), np.float32)
    for q in range(-1, 7):
        p = place(q)
        out[of_left(q), p] = 1
        out[of_left(q + 6), p + 64] = 1
        out[of_right(q), p + 63] = 1
        out[of_right(q + 6), p - 1] = 1
    return out.astype(BF16)


def halo_lane(s, side, row):
    return 32 * s + 16 * side + row + 1


def halo_taps():
    out = np.zeros((256, 3 * 128), np.float32)
    for k in range(3):
        for s in range(2):
            for side in range(2):
                for row in range(-2, 14):
                    source = 128 * s + 16 * (3 * side + k) + row + 2
                    out[source, 128 * k + halo_lane(s, side, row + 1)] = 1
    return out.astype(BF16)


def lanes(rows):
    return lax.broadcasted_iota(jnp.int32, (rows, 128), 1)


def members(rows, first, base):
    chan = lax.broadcasted_iota(jnp.int32, (rows, 128), 0) + first
    low = (lanes(rows) - base) * WIDTH
    return (chan >= low) & (chan < low + WIDTH)


def silu_of_half(h):
    return h + h * jnp.tanh(h)


PARAMS = pltpu.CompilerParams(vmem_limit_bytes=LIMIT)


def sums_kernel(place_ref, cells_hbm, sums_ref, one_ref, other_ref, x, sems):
    half = COLS // 2
    copies = []
    for s in range(2):
        for c in range(2):
            cut = slice(c * half, (c + 1) * half)
            copies.append(
                pltpu.make_async_copy(cells_hbm.at[s, cut], x.at[s, cut], sems.at[2 * s + c])
            )
            copies[-1].start()
    row = jnp.zeros((1, 128), F32)
    for s in range(2):
        total = jnp.zeros((PART, LAT), F32)
        square = jnp.zeros((PART, LAT), F32)
        for c in range(2):
            copies[2 * s + c].wait()

            def add(i, carry):
                total, square = carry
                for j in range(4):
                    v = x[s, c * half + 4 * i + j].astype(F32)
                    total, square = total + v, square + v * v
                return total, square

            total, square = lax.fori_loop(0, half // 4, add, (total, square))
        for k, acc in enumerate((total, square)):
            column = jnp.sum(acc, axis=1, keepdims=True)
            own = members(PART, 0, 64 * k + 32 * s)
            row += jnp.sum(jnp.where(own, column, 0.0), axis=0, keepdims=True)
        even = place_ref[0] % 2 == 0
        first, last = x[s, 0:2].astype(F32), x[s, COLS - 2 : COLS].astype(F32)
        one_ref[s] = jnp.where(even, last, first).astype(BF16)
        other_ref[s] = jnp.where(even, first, last).astype(BF16)
    sums_ref[...] = jnp.broadcast_to(row, sums_ref.shape)


def local_sums(place, cells):
    return pl.pallas_call(
        sums_kernel,
        in_specs=[SMEM, ANY],
        out_specs=[VMEM] * 3,
        out_shape=[
            jax.ShapeDtypeStruct((16, 128), F32),
            jax.ShapeDtypeStruct((2, 2, PART, LAT), BF16),
            jax.ShapeDtypeStruct((2, 2, PART, LAT), BF16),
        ],
        scratch_shapes=[pltpu.VMEM((2, COLS, PART, LAT), BF16), pltpu.SemaphoreType.DMA((4,))],
        compiler_params=PARAMS,
        name="local_sums",
    )(place, cells)


def pack_kernel(cells_hbm, pay_hbm, x, out, taken, turned, sems):
    fetches = [pltpu.make_async_copy(cells_hbm.at[s], x.at[s], sems.at[s]) for s in range(2)]
    for copy in fetches:
        copy.start()
    taken[...] = jnp.zeros_like(taken)
    turned[...] = jnp.zeros_like(turned)
    low = lanes(8) < 64
    stores = [
        pltpu.make_async_copy(out.at[s], pay_hbm.at[:, 8 * s : 8 * s + 7], sems.at[2 + s])
        for s in range(2)
    ]
    fetches[0].wait()

    @pl.loop(0, 2 * PART // CHUNK)
    def _(step):
        s, e = step // (PART // CHUNK), step % (PART // CHUNK)

        @pl.when(step == PART // CHUNK)
        def _():
            stores[0].start()
            fetches[1].wait()

        own = pl.ds(pl.multiple_of(e * CHUNK, CHUNK), CHUNK)
        taken[:, 0:LAT] = x[s, :, own, :].astype(F32).reshape(COLS * CHUNK, LAT)
        for j in range(8):
            pair = [taken[pl.ds(j + 8 * h, COLS, stride=CHUNK), :] for h in range(2)]
            turned[pl.ds(8 + j, LAT, stride=8), :] = jnp.concatenate(pair, axis=0).T[0:LAT, :]

        def tile(upper, lower):
            upper, lower = (turned[8 * (r + 1) : 8 * (r + 2), :] for r in (upper, lower))
            halves = (jnp.where(low, upper, roll(lower, 64)), jnp.where(low, roll(upper, 64), lower))
            return jnp.concatenate(halves, axis=0).astype(BF16)

        for d in range(SRC):
            for q in range(7):
                upper, lower = (d * ROWS + q, d * ROWS + q + 6)
                if q == 6:
                    upper, lower = (d * ROWS - 1, d * ROWS + ROWS)
                out[s, d, q, own, :] = tile(upper, lower)

    stores[1].start()
    for store in stores:
        store.wait()


def pack(cells):
    return pl.pallas_call(
        pack_kernel,
        in_specs=[ANY],
        out_specs=ANY,
        out_shape=jax.ShapeDtypeStruct((SRC, 16, PART, 128), BF16),
        scratch_shapes=[
            pltpu.VMEM((2, COLS, PART, LAT), BF16),
            pltpu.VMEM((2, SRC, 7, PART, 128), BF16),
            pltpu.VMEM((COLS * CHUNK, 128), F32),
            pltpu.VMEM(((LAT + 8) * 8, 128), F32),
            pltpu.SemaphoreType.DMA((4,)),
        ],
        compiler_params=PARAMS,
        cost_estimate=pl.CostEstimate(
            flops=1_000_000_000, bytes_accessed=8_000_000, transcendentals=0
        ),
        name="pack_latents",
    )(cells)


def halo_kernel(
    place_ref, sums_ref, one_ref, other_ref, from_one, from_other, _, pay_hbm, out, sems,
):
    lane = lanes(PART)
    pad = jnp.zeros((PART, 128 - LAT), F32)
    row = jnp.sum(sums_ref[...], axis=0, keepdims=True)

    @pl.loop(0, 2)
    def _(s):
        even = place_ref[0] % 2 == 0
        one, other = one_ref[s].astype(F32), other_ref[s].astype(F32)
        first, last = jnp.where(even, other, one), jnp.where(even, one, other)
        one, other = from_one[s].astype(F32), from_other[s].astype(F32)
        left, right = jnp.where(even, other, one), jnp.where(even, one, other)
        near = [left[0], left[1], first[0], last[1], right[0], right[1]]
        near = [jnp.concatenate([col, pad], axis=1).astype(BF16) for col in near]
        carried = jnp.zeros((PART, 128), F32)
        for k in range(2):
            own = members(PART, 0, 64 * k + 32 * s)
            value = jnp.sum(jnp.where(own, row, 0.0), axis=1, keepdims=True)
            for piece in range(3):
                part = value.astype(BF16).astype(F32)
                carried = jnp.where(lane == SUMS + 3 * k + piece, part, carried)
                value = value - part
        carried = carried.astype(BF16)
        for d in range(SRC):
            halo = carried
            for kind in range(6):
                own = (lane >= 16 * kind) & (lane < 16 * kind + 16)
                halo = jnp.where(own, roll(near[kind], 16 * kind + 2 - d * ROWS), halo)
            out[s, d] = halo
        pltpu.make_async_copy(out.at[s], pay_hbm.at[:, 8 * s + 7], sems.at[s]).start()

    for s in range(2):
        pltpu.make_async_copy(out.at[s], pay_hbm.at[:, 8 * s + 7], sems.at[s]).wait()


def pack_halo(place, sums, ours, theirs, pay):
    return pl.pallas_call(
        halo_kernel,
        in_specs=[SMEM] + [VMEM] * 5 + [ANY],
        out_specs=ANY,
        out_shape=jax.ShapeDtypeStruct((SRC, 16, PART, 128), BF16),
        scratch_shapes=[
            pltpu.VMEM((2, SRC, PART, 128), BF16),
            pltpu.SemaphoreType.DMA((2,)),
        ],
        input_output_aliases={6: 0},
        compiler_params=PARAMS,
        name="pack_halo",
    )(place, sums, *ours, *theirs, pay)


def weight_kernel(j, w_hbm, o_hbm, x, out, sems):
    for t in range(TAPS):
        pltpu.make_async_copy(w_hbm.at[j, t], x.at[t], sems.at[t]).start()

    @pl.loop(0, TAPS)
    def _(t):
        pltpu.make_async_copy(w_hbm.at[j, t], x.at[t], sems.at[t]).wait()
        out[t] = x[t].T
        cut = pl.ds(pl.multiple_of(t * C, 128), C)
        pltpu.make_async_copy(out.at[t], o_hbm.at[:, cut], sems.at[TAPS + t]).start()

    for t in range(TAPS):
        cut = slice(t * C, (t + 1) * C)
        pltpu.make_async_copy(out.at[t], o_hbm.at[:, cut], sems.at[TAPS + t]).wait()


def turn_weights(j, weights):
    return pl.pallas_call(
        functools.partial(weight_kernel, j),
        in_specs=[ANY],
        out_specs=ANY,
        out_shape=jax.ShapeDtypeStruct((C, TAPS * C), BF16),
        scratch_shapes=[
            pltpu.VMEM((TAPS, C, C), BF16),
            pltpu.VMEM((TAPS, C, C), BF16),
            pltpu.SemaphoreType.DMA((2 * TAPS,)),
        ],
        compiler_params=PARAMS,
        cost_estimate=pl.CostEstimate(
            flops=TAPS * 2 * C * C * 256, bytes_accessed=15_000_000, transcendentals=0
        ),
        name=f"turn_weights_{j}",
    )(weights.reshape(2, TAPS, C, C))


def target_kernel(target_hbm, o_hbm, x, out, sems):
    fetch = pltpu.make_async_copy(target_hbm, x, sems.at[0])
    fetch.start()
    fetch.wait()

    @pl.loop(0, 6)
    def _(q):
        for s in range(2):
            out[s, q] = jnp.concatenate([x[q, s], x[q + 6, s]], axis=0).T

    store = pltpu.make_async_copy(out, o_hbm, sems.at[1])
    store.start()
    store.wait()


def turn_target(target):
    return pl.pallas_call(
        target_kernel,
        in_specs=[ANY],
        out_specs=ANY,
        out_shape=jax.ShapeDtypeStruct((2, 6, C, 128), BF16),
        scratch_shapes=[
            pltpu.VMEM((ROWS, 2, COLS, C), BF16),
            pltpu.VMEM((2, 6, C, 128), BF16),
            pltpu.SemaphoreType.DMA((2,)),
        ],
        compiler_params=PARAMS,
        name="turn_target",
    )(target)


def affine(total, square, par_ref, j, scale, offset):
    count = float(LAT * 1024 * WIDTH)
    mean = total / count
    spread = square / count - mean * mean
    factor = lax.rsqrt(spread + 1e-05) * par_ref[:, 2 * j : 2 * j + 1]
    rest = par_ref[:, 2 * j + 1 : 2 * j + 2] - mean * factor
    scale[...] = jnp.broadcast_to(0.5 * factor, scale.shape)
    offset[...] = jnp.broadcast_to(0.5 * rest, offset.shape)


def spread_taps(xs, at, tiles, edge, sides, part):
    rows = PART
    lane = lanes(rows)
    low = lane < 64
    first = (lane == 0) | (lane == 64)
    last = (lane == 63) | (lane == 127)
    tiles, edge = [tile.astype(BF16) for tile in tiles], edge.astype(BF16)
    zero = jnp.zeros((rows, 128), BF16)
    for q in range(-1, 7):
        if q == -1:
            tile = jnp.where(low, edge, roll(tiles[5], 64))
        elif q == 6:
            tile = jnp.where(low, roll(tiles[0], 64), edge)
        else:
            tile = tiles[q]
        side = roll(sides[pl.ds(at, rows), :], -place(q))
        taps = (jnp.where(first, side, roll(tile, 1)), tile, jnp.where(last, side, roll(tile, -1)))
        for k, tap in enumerate(taps):
            if q == -1:
                tap = jnp.where(low & (part == 0), zero, tap)
            elif q == 6:
                tap = jnp.where((~low) & (part == SRC - 1), zero, tap)
            xs[pl.ds(k * C + at, rows), 128 * (q + 1) : 128 * (q + 2)] = tap


def product(wv, xs, n, more=None):
    x = jnp.concatenate([xs[:, n + 128 * i : n + 128 * i + 256] for i in range(3)], axis=0)
    if more is not None:
        x = jnp.concatenate([x, more], axis=1)
    return jnp.dot(wv[...], x, preferred_element_type=F32)


def first_kernel(
    part_ref, par_ref, pick_ref, taps_ref, recv_hbm, w_hbm,
    hid_hbm, out_sums, one, other, out_halo,
    xs, wv, scale, offset, recv, hid, sides, xh, sems,
):
    fetches = [
        pltpu.make_async_copy(recv_hbm.at[:, 8 * s : 8 * s + 8], recv.at[s], sems.at[s])
        for s in range(2)
    ]
    weights = pltpu.make_async_copy(w_hbm, wv, sems.at[2])
    for copy in (fetches[0], weights, fetches[1]):
        copy.start()
    part = part_ref[0]
    lane = lanes(C)

    def act(x, a, o):
        return silu_of_half(x.astype(F32) * a + o)

    def columns(s):
        fetches[s].wait()
        tile = recv[s, :, 7].reshape(C, 128).astype(F32)
        total, square = (
            jnp.sum(jnp.where((lane >= at) & (lane < at + 3), tile, 0.0), axis=1, keepdims=True)
            for at in (SUMS, SUMS + 3)
        )
        affine(total, square, par_ref, 0, scale.at[s], offset.at[s])
        r = (lane & 15) - 2
        unused = lane >= SUMS
        outside = ((part == 0) & (r < 0)) | ((part == SRC - 1) & (r >= ROWS)) | unused
        x = act(jnp.where(unused, 0.0, tile), scale[s], offset[s])
        halo = jnp.where(outside, 0.0, x).astype(BF16)
        sides[s] = jnp.dot(halo, pick_ref[...], preferred_element_type=F32).astype(BF16)
        return halo

    def prepare(s, b):
        at = b * PART if isinstance(b, int) else pl.multiple_of(b * PART, PART)
        a, o = scale[s, pl.ds(at, PART), :], offset[s, pl.ds(at, PART), :]
        tiles = [act(recv[s, b, q], a, o) for q in range(7)]
        spread_taps(xs.at[s], at, tiles[:6], tiles[6], sides.at[s], part)

    halo = columns(0)

    @pl.loop(0, SRC)
    def _(b):
        prepare(0, b)

    both = jnp.concatenate([halo, columns(1)], axis=1)
    for k in range(3):
        picked = jnp.dot(both, taps_ref[:, 128 * k : 128 * k + 128], preferred_element_type=F32)
        for i in range(3):
            t = 3 * i + k
            xh[C * t : C * (t + 1), :] = roll(picked, -i).astype(BF16)
    weights.wait()
    stores = []

    def put(s, n, value):
        part = hid.at[s, :, n : n + 256]
        part[...] = value + par_ref[:, 5 + s : 6 + s]
        store = pltpu.make_async_copy(
            part, hid_hbm.at[s, :, n : n + 256], sems.at[3 + 3 * s + n // 256]
        )
        store.start()
        stores.append(store)

    put(0, 0, product(wv, xs.at[0], 0))
    for n, blocks in ((256, (0, 1, 2, 3)), (512, (4, 5, 6, 7))):
        put(0, n, product(wv, xs.at[0], n))
        for b in blocks:
            prepare(1, b)
    put(1, 0, product(wv, xs.at[1], 0))
    put(1, 256, product(wv, xs.at[1], 256))
    out = product(wv, xs.at[1], 512, xh[...])
    put(1, 512, out[:, 0:256])
    bias = jnp.where(lane < 32, par_ref[:, 5:6], par_ref[:, 6:7])
    out_halo[...] = (out[:, 256:384] + bias).astype(BF16)

    row = jnp.zeros((1, 128), F32)
    low = lanes(128) < 64
    even = part % 2 == 0
    for at in range(0, C, 128):
        for s in range(2):
            pieces = [hid[s, at : at + 128, 128 * q : 128 * (q + 1)] for q in range(6)]
            for k in range(2):
                column = jnp.sum(sum(p * p if k else p for p in pieces), axis=1, keepdims=True)
                own = members(128, at, 64 * k + 32 * s)
                row += jnp.sum(jnp.where(own, column, 0.0), axis=0, keepdims=True)
        start, end = hid.at[:, at : at + 128, 0:128], hid.at[:, at : at + 128, 640:768]
        after = jnp.where(low, roll(end[0], 64), end[1])
        ahead = jnp.where(low, start[0], roll(start[1], 64))
        one[at : at + 128, :] = jnp.where(even, after, ahead).astype(BF16)
        other[at : at + 128, :] = jnp.where(even, ahead, after).astype(BF16)
    out_sums[...] = jnp.broadcast_to(row, out_sums.shape)
    for store in stores:
        store.wait()


def first_conv(part, params, pick, taps, recv, weights):
    tile = jax.ShapeDtypeStruct((C, 128), BF16)
    return pl.pallas_call(
        first_kernel,
        in_specs=[SMEM] + [VMEM] * 3 + [ANY] * 2,
        out_specs=[ANY] + [VMEM] * 4,
        out_shape=[
            jax.ShapeDtypeStruct((2, C, 768), F32),
            jax.ShapeDtypeStruct((128, 128), F32),
            tile, tile, tile,
        ],
        scratch_shapes=[
            pltpu.VMEM((2, 3 * C, 1024), BF16),
            pltpu.VMEM((C, TAPS * C), BF16),
            pltpu.VMEM((2, C, 128), F32),
            pltpu.VMEM((2, C, 128), F32),
            pltpu.VMEM((2, SRC, 8, PART, 128), BF16),
            pltpu.VMEM((2, C, 768), F32),
            pltpu.VMEM((2, C, 128), BF16),
            pltpu.VMEM((TAPS * C, 128), BF16),
            pltpu.SemaphoreType.DMA((9,)),
        ],
        compiler_params=PARAMS,
        cost_estimate=pl.CostEstimate(
            flops=4 * 768 * C * C * 9, bytes_accessed=20_000_000, transcendentals=0
        ),
        name="first_conv",
    )(part, params, pick, taps, recv, weights)


def second_kernel(
    part_ref, coef_ref, sums_ref, par_ref, pick_ref, near_ref, one_ref, other_ref,
    hid_hbm, w_hbm, recv_hbm, target_hbm,
    noise_hbm, out_ref,
    xs, wv, hid, lat, target, noise_out, sides, scale, offset, sems,
):
    weights = pltpu.make_async_copy(w_hbm, wv, sems.at[6])
    fetches, later = [], []
    for s in range(2):
        fetches.append(pltpu.make_async_copy(hid_hbm.at[s], hid.at[s], sems.at[s]))
        tiles = recv_hbm.at[:, 8 * s : 8 * s + 6]
        later.append(pltpu.make_async_copy(tiles, lat.at[s], sems.at[2 + s]))
        later.append(pltpu.make_async_copy(target_hbm.at[s], target.at[s], sems.at[4 + s]))
    for copy in (fetches[0], weights, fetches[1], *later):
        copy.start()
    part = part_ref[0]
    row = jnp.sum(sums_ref[...], axis=0, keepdims=True)
    low = lanes(PART) < 64
    even = part % 2 == 0

    def columns(s):
        total, square = (
            jnp.sum(jnp.where(members(C, 0, base), row, 0.0), axis=1, keepdims=True)
            for base in (32 * s, 64 + 32 * s)
        )
        affine(total, square, par_ref, 1, scale.at[s], offset.at[s])
        halo = silu_of_half(near_ref[...].astype(F32) * scale[s] + offset[s]).astype(BF16)
        sides[s] = jnp.dot(halo, pick_ref[s], preferred_element_type=F32).astype(BF16)
        fetches[s].wait()

    def prepare(s, b):
        at = b * PART if isinstance(b, int) else pl.multiple_of(b * PART, PART)
        rows = pl.ds(at, PART)
        a, o = scale[s, rows, :], offset[s, rows, :]

        def act(x):
            return silu_of_half(x * a + o)

        tiles = [act(hid[s, rows, 128 * q : 128 * (q + 1)]) for q in range(6)]
        below, above = one_ref[rows, :].astype(F32), other_ref[rows, :].astype(F32)
        above, below = jnp.where(even, above, below), jnp.where(even, below, above)
        if s == 0:
            edge = jnp.where(low, above, roll(below, 64))
        else:
            edge = jnp.where(low, roll(above, 64), below)
        spread_taps(xs.at[s], at, tiles, act(edge), sides.at[s], part)

    def finish(s, n, acc):
        keep, gain = coef_ref[2 * s], coef_ref[2 * s + 1]
        out = product(wv, xs.at[s], n) + par_ref[:, 4:5]
        for h in range(2):
            q = n // 128 + h
            mine = lat[s, :, q].reshape(C, 128).astype(F32)
            noise = (out[:, 128 * h : 128 * h + 128] + mine).astype(BF16)
            center = keep * mine + gain * noise.astype(F32)
            diff = target[s, q].astype(F32) - center
            acc += jnp.sum((diff * diff).reshape(C // 8, 8, 128), axis=0)
            plain = noise.T
            noise_out[s, q] = plain[0:64]
            noise_out[s, q + 6] = plain[64:128]
        return acc

    columns(0)

    @pl.loop(0, SRC)
    def _(b):
        prepare(0, b)

    columns(1)
    weights.wait()
    for copy in later:
        copy.wait()
    result = jnp.zeros((1, 128), F32)
    stores = []
    for s in range(2):
        acc = jnp.zeros((8, 128), F32)
        for n, blocks in ((0, (0, 1, 2)), (256, (3, 4, 5)), (512, (6, 7))):
            acc = finish(s, n, acc)
            if s == 0:
                for b in blocks:
                    prepare(1, b)
        store = pltpu.make_async_copy(noise_out.at[s], noise_hbm.at[:, s], sems.at[7 + s])
        store.start()
        stores.append(store)
        value = jnp.sum(acc, axis=(0, 1), keepdims=True)
        result = jnp.where(lanes(1) == s, value, result)
    out_ref[...] = jnp.broadcast_to(result, out_ref.shape)
    for store in stores:
        store.wait()


def second_conv(part, coef, sums, params, pick, tiles, hidden, weights, recv, target):
    return pl.pallas_call(
        second_kernel,
        in_specs=[SMEM, SMEM] + [VMEM] * 6 + [ANY] * 4,
        out_specs=[ANY, VMEM],
        out_shape=[
            jax.ShapeDtypeStruct((ROWS, 2, COLS, C), BF16),
            jax.ShapeDtypeStruct((128, 128), F32),
        ],
        scratch_shapes=[
            pltpu.VMEM((2, 3 * C, 1024), BF16),
            pltpu.VMEM((C, TAPS * C), BF16),
            pltpu.VMEM((2, C, 768), F32),
            pltpu.VMEM((2, SRC, 6, PART, 128), BF16),
            pltpu.VMEM((2, 6, C, 128), BF16),
            pltpu.VMEM((2, ROWS, COLS, C), BF16),
            pltpu.VMEM((2, C, 128), BF16),
            pltpu.VMEM((2, C, 128), F32),
            pltpu.VMEM((2, C, 128), F32),
            pltpu.SemaphoreType.DMA((9,)),
        ],
        compiler_params=PARAMS,
        cost_estimate=pl.CostEstimate(
            flops=4 * 768 * C * C * 9, bytes_accessed=20_000_000, transcendentals=0
        ),
        name="second_conv",
    )(part, coef, sums, params, pick, *tiles, hidden, weights, recv, target)


def time_embed(timesteps, time_w1, time_w2):
    half = time_w1.shape[0] // 2
    freqs = jnp.exp(-math.log(10000.0) * jnp.arange(half, dtype=F32) / half)
    angles = timesteps.astype(F32)[:, None] * freqs[None, :]
    features = jnp.concatenate([jnp.cos(angles), jnp.sin(angles)], axis=1)
    hidden = jax.nn.silu(jnp.dot(features, time_w1, precision=lax.Precision.HIGHEST))
    return jnp.dot(hidden, time_w2, precision=lax.Precision.HIGHEST)


def plan(steps):
    frac = steps.astype(F32) / 1000.0
    return jnp.cos((frac + 0.008) / 1.008 * (math.pi / 2.0)) ** 2


def everywhere(rows, axes):
    got = lax.all_to_all(rows.reshape(-1, 1, 128), axes, 0, 0, tiled=True)
    return got.reshape(-1, 128)


def swap_neighbours(one, other, axis):
    size = lax.axis_size(axis)
    pairs = [(i, i ^ 1) for i in range(size)]
    rest = [(i, (i + 1 if i % 2 else i - 1) % size) for i in range(size)]
    return lax.ppermute(one, axis, pairs), lax.ppermute(other, axis, rest)


def swap(array, axis):
    return lax.all_to_all(array, axis, split_axis=0, concat_axis=0, tiled=True)


def after(value, *others):
    return lax.optimization_barrier((value,) + others)[0]


def body(
    latents, next_latents, timesteps, resume_steps, conv_weights, conv_bias,
    norm_gain, norm_shift, time_w1, time_w2,
):
    part = lax.axis_index("ch").astype(jnp.int32).reshape(1)
    first_pick = jnp.asarray(side_lanes(lambda r: 16 + r + 2, lambda r: 64 + r + 2))
    second_pick = jnp.asarray(
        np.stack(
            [
                side_lanes(lambda r: halo_lane(s, 0, r), lambda r: halo_lane(s, 1, r))
                for s in range(2)
            ]
        )
    )
    tap_pick = jnp.asarray(halo_taps())

    cells = latents.transpose(1, 2, 3, 0)
    place = lax.axis_index("lon").astype(jnp.int32).reshape(1)
    sums, *ours = local_sums(place, cells)
    sums = everywhere(sums, "lon")
    theirs = swap_neighbours(*ours, "lon")
    pay = pack(after(cells, ours[0]))
    pay = pack_halo(place, sums, ours, theirs, pay)
    recv = swap(pay, "ch")
    conv_weights, time_w1, following = after((conv_weights, time_w1, next_latents), pay)
    turned = [turn_weights(j, conv_weights) for j in range(2)]
    target = turn_target(following)

    temb = time_embed(timesteps, time_w1, time_w2)
    columns = [
        norm_gain[0], norm_shift[0], norm_gain[1], norm_shift[1], conv_bias[1],
        conv_bias[0] + temb[0], conv_bias[0] + temb[1],
    ]
    params = jnp.pad(jnp.stack(columns, axis=1), ((0, 0), (0, 128 - len(columns))))

    alpha = plan(timesteps)
    prior = plan(timesteps - resume_steps)
    variance = (1.0 - prior) / (1.0 - alpha) * (1.0 - alpha / prior)
    keep = (1.0 - prior) * jnp.sqrt(alpha / (prior * (1.0 - alpha)))
    ratio = jnp.sqrt(prior) / jnp.sqrt(alpha)
    coef = jnp.stack([ratio, keep - ratio * jnp.sqrt(1.0 - alpha)], axis=1).reshape(4)

    recv, turned, target = lax.optimization_barrier((recv, turned, target))
    hidden, sums, one, other, near = first_conv(
        part, params, first_pick, tap_pick, recv, turned[0]
    )
    one, other = swap_neighbours(one, other, "ch")
    sums = everywhere(sums, ("lon", "ch"))
    noise, terms = second_conv(
        part, coef, sums, params, second_pick, (near, one, other),
        hidden, turned[1], recv, target,
    )
    squares = jnp.sum(everywhere(terms, ("lon", "ch")), axis=0)[:2]
    logprob = (
        -squares / (2.0 * variance) / float(LAT * 1024 * C)
        - 0.5 * jnp.log(variance)
        - 0.5 * math.log(2.0 * math.pi)
    )
    return (noise, logprob)


def solution(mesh):
    return jax.shard_map(
        body,
        mesh=mesh,
        in_specs=(
            P(None, None, "lon", "ch"),
            P("ch", None, "lon", None),
            P(), P(), P(), P(), P(), P(), P(), P(),
        ),
        out_specs=(P("ch", None, "lon", None), P()),
        check_vma=False,
    )
```

```python
import functools
import math

import jax
import jax.numpy as jnp
import numpy as np
from jax import lax
from jax.experimental import pallas as pl
from jax.experimental.pallas import tpu as pltpu
from jax.sharding import PartitionSpec as P

GROUPS = 32
C = 640
LAT = 96
ROWS = 12
COLS = 64
SRC = 8
PART = C // SRC
WIDTH = C // GROUPS
TAPS = 9
F32 = jnp.float32
BF16 = jnp.bfloat16
VMEM = pl.BlockSpec(memory_space=pltpu.VMEM)
SMEM = pl.BlockSpec(memory_space=pltpu.SMEM)
ANY = pl.BlockSpec(memory_space=pl.ANY)
CHUNK = 16
LIMIT = 56 * 2**20
SUMS = 96


def roll(x, by):
    by %= 128
    return x if by == 0 else pltpu.roll(x, by, 1)


def place(q):
    return 2 * q + 3


def side_lanes(of_left, of_right):
    out = np.zeros((128, 128), np.float32)
    for q in range(-1, 7):
        p = place(q)
        out[of_left(q), p] = 1
        out[of_left(q + 6), p + 64] = 1
        out[of_right(q), p + 63] = 1
        out[of_right(q + 6), p - 1] = 1
    return out.astype(BF16)


def halo_lane(s, side, row):
    return 32 * s + 16 * side + row + 1


def halo_taps():
    out = np.zeros((256, 3 * 128), np.float32)
    for k in range(3):
        for s in range(2):
            for side in range(2):
                for row in range(-2, 14):
                    source = 128 * s + 16 * (3 * side + k) + row + 2
                    out[source, 128 * k + halo_lane(s, side, row + 1)] = 1
    return out.astype(BF16)


def lanes(rows):
    return lax.broadcasted_iota(jnp.int32, (rows, 128), 1)


def members(rows, first, base):
    chan = lax.broadcasted_iota(jnp.int32, (rows, 128), 0) + first
    low = (lanes(rows) - base) * WIDTH
    return (chan >= low) & (chan < low + WIDTH)


def silu_of_half(h):
    return h + h * jnp.tanh(h)


PARAMS = pltpu.CompilerParams(vmem_limit_bytes=LIMIT)


def sums_kernel(place_ref, cells_hbm, sums_ref, one_ref, other_ref, x, sems):
    half = COLS // 2
    copies = []
    for s in range(2):
        for c in range(2):
            cut = slice(c * half, (c + 1) * half)
            copies.append(
                pltpu.make_async_copy(cells_hbm.at[s, cut], x.at[s, cut], sems.at[2 * s + c])
            )
            copies[-1].start()
    row = jnp.zeros((1, 128), F32)
    for s in range(2):
        total = jnp.zeros((PART, LAT), F32)
        square = jnp.zeros((PART, LAT), F32)
        for c in range(2):
            copies[2 * s + c].wait()

            def add(i, carry):
                total, square = carry
                for j in range(4):
                    v = x[s, c * half + 4 * i + j].astype(F32)
                    total, square = total + v, square + v * v
                return total, square

            total, square = lax.fori_loop(0, half // 4, add, (total, square))
        for k, acc in enumerate((total, square)):
            column = jnp.sum(acc, axis=1, keepdims=True)
            own = members(PART, 0, 64 * k + 32 * s)
            row += jnp.sum(jnp.where(own, column, 0.0), axis=0, keepdims=True)
        even = place_ref[0] % 2 == 0
        first, last = x[s, 0:2].astype(F32), x[s, COLS - 2 : COLS].astype(F32)
        one_ref[s] = jnp.where(even, last, first).astype(BF16)
        other_ref[s] = jnp.where(even, first, last).astype(BF16)
    sums_ref[...] = jnp.broadcast_to(row, sums_ref.shape)


def local_sums(place, cells):
    return pl.pallas_call(
        sums_kernel,
        in_specs=[SMEM, ANY],
        out_specs=[VMEM] * 3,
        out_shape=[
            jax.ShapeDtypeStruct((16, 128), F32),
            jax.ShapeDtypeStruct((2, 2, PART, LAT), BF16),
            jax.ShapeDtypeStruct((2, 2, PART, LAT), BF16),
        ],
        scratch_shapes=[pltpu.VMEM((2, COLS, PART, LAT), BF16), pltpu.SemaphoreType.DMA((4,))],
        compiler_params=PARAMS,
        name="local_sums",
    )(place, cells)


def pack_kernel(cells_hbm, pay_hbm, x, out, taken, turned, sems):
    fetches = [pltpu.make_async_copy(cells_hbm.at[s], x.at[s], sems.at[s]) for s in range(2)]
    for copy in fetches:
        copy.start()
    taken[...] = jnp.zeros_like(taken)
    turned[...] = jnp.zeros_like(turned)
    low = lanes(8) < 64
    stores = [
        pltpu.make_async_copy(out.at[s], pay_hbm.at[:, 8 * s : 8 * s + 7], sems.at[2 + s])
        for s in range(2)
    ]
    fetches[0].wait()

    @pl.loop(0, 2 * PART // CHUNK)
    def _(step):
        s, e = step // (PART // CHUNK), step % (PART // CHUNK)

        @pl.when(step == PART // CHUNK)
        def _():
            stores[0].start()
            fetches[1].wait()

        own = pl.ds(pl.multiple_of(e * CHUNK, CHUNK), CHUNK)
        taken[:, 0:LAT] = x[s, :, own, :].astype(F32).reshape(COLS * CHUNK, LAT)
        for j in range(8):
            pair = [taken[pl.ds(j + 8 * h, COLS, stride=CHUNK), :] for h in range(2)]
            turned[pl.ds(8 + j, LAT, stride=8), :] = jnp.concatenate(pair, axis=0).T[0:LAT, :]

        def tile(upper, lower):
            upper, lower = (turned[8 * (r + 1) : 8 * (r + 2), :] for r in (upper, lower))
            halves = (jnp.where(low, upper, roll(lower, 64)), jnp.where(low, roll(upper, 64), lower))
            return jnp.concatenate(halves, axis=0).astype(BF16)

        for d in range(SRC):
            for q in range(7):
                upper, lower = (d * ROWS + q, d * ROWS + q + 6)
                if q == 6:
                    upper, lower = (d * ROWS - 1, d * ROWS + ROWS)
                out[s, d, q, own, :] = tile(upper, lower)

    stores[1].start()
    for store in stores:
        store.wait()


def pack(cells):
    return pl.pallas_call(
        pack_kernel,
        in_specs=[ANY],
        out_specs=ANY,
        out_shape=jax.ShapeDtypeStruct((SRC, 16, PART, 128), BF16),
        scratch_shapes=[
            pltpu.VMEM((2, COLS, PART, LAT), BF16),
            pltpu.VMEM((2, SRC, 7, PART, 128), BF16),
            pltpu.VMEM((COLS * CHUNK, 128), F32),
            pltpu.VMEM(((LAT + 8) * 8, 128), F32),
            pltpu.SemaphoreType.DMA((4,)),
        ],
        compiler_params=PARAMS,
        cost_estimate=pl.CostEstimate(
            flops=1_000_000_000, bytes_accessed=8_000_000, transcendentals=0
        ),
        name="pack_latents",
    )(cells)


def halo_kernel(
    place_ref, sums_ref, one_ref, other_ref, from_one, from_other, _, pay_hbm, out, sems,
):
    lane = lanes(PART)
    pad = jnp.zeros((PART, 128 - LAT), F32)
    row = jnp.sum(sums_ref[...], axis=0, keepdims=True)

    @pl.loop(0, 2)
    def _(s):
        even = place_ref[0] % 2 == 0
        one, other = one_ref[s].astype(F32), other_ref[s].astype(F32)
        first, last = jnp.where(even, other, one), jnp.where(even, one, other)
        one, other = from_one[s].astype(F32), from_other[s].astype(F32)
        left, right = jnp.where(even, other, one), jnp.where(even, one, other)
        near = [left[0], left[1], first[0], last[1], right[0], right[1]]
        near = [jnp.concatenate([col, pad], axis=1).astype(BF16) for col in near]
        carried = jnp.zeros((PART, 128), F32)
        for k in range(2):
            own = members(PART, 0, 64 * k + 32 * s)
            value = jnp.sum(jnp.where(own, row, 0.0), axis=1, keepdims=True)
            for piece in range(3):
                part = value.astype(BF16).astype(F32)
                carried = jnp.where(lane == SUMS + 3 * k + piece, part, carried)
                value = value - part
        carried = carried.astype(BF16)
        for d in range(SRC):
            halo = carried
            for kind in range(6):
                own = (lane >= 16 * kind) & (lane < 16 * kind + 16)
                halo = jnp.where(own, roll(near[kind], 16 * kind + 2 - d * ROWS), halo)
            out[s, d] = halo
        pltpu.make_async_copy(out.at[s], pay_hbm.at[:, 8 * s + 7], sems.at[s]).start()

    for s in range(2):
        pltpu.make_async_copy(out.at[s], pay_hbm.at[:, 8 * s + 7], sems.at[s]).wait()


def pack_halo(place, sums, ours, theirs, pay):
    return pl.pallas_call(
        halo_kernel,
        in_specs=[SMEM] + [VMEM] * 5 + [ANY],
        out_specs=ANY,
        out_shape=jax.ShapeDtypeStruct((SRC, 16, PART, 128), BF16),
        scratch_shapes=[
            pltpu.VMEM((2, SRC, PART, 128), BF16),
            pltpu.SemaphoreType.DMA((2,)),
        ],
        input_output_aliases={6: 0},
        compiler_params=PARAMS,
        name="pack_halo",
    )(place, sums, *ours, *theirs, pay)


def weight_kernel(j, w_hbm, o_hbm, x, out, sems):
    for t in range(TAPS):
        pltpu.make_async_copy(w_hbm.at[j, t], x.at[t], sems.at[t]).start()

    @pl.loop(0, TAPS)
    def _(t):
        pltpu.make_async_copy(w_hbm.at[j, t], x.at[t], sems.at[t]).wait()
        out[t] = x[t].T
        cut = pl.ds(pl.multiple_of(t * C, 128), C)
        pltpu.make_async_copy(out.at[t], o_hbm.at[:, cut], sems.at[TAPS + t]).start()

    for t in range(TAPS):
        cut = slice(t * C, (t + 1) * C)
        pltpu.make_async_copy(out.at[t], o_hbm.at[:, cut], sems.at[TAPS + t]).wait()


def turn_weights(j, weights):
    return pl.pallas_call(
        functools.partial(weight_kernel, j),
        in_specs=[ANY],
        out_specs=ANY,
        out_shape=jax.ShapeDtypeStruct((C, TAPS * C), BF16),
        scratch_shapes=[
            pltpu.VMEM((TAPS, C, C), BF16),
            pltpu.VMEM((TAPS, C, C), BF16),
            pltpu.SemaphoreType.DMA((2 * TAPS,)),
        ],
        compiler_params=PARAMS,
        cost_estimate=pl.CostEstimate(
            flops=TAPS * 2 * C * C * 256, bytes_accessed=15_000_000, transcendentals=0
        ),
        name=f"turn_weights_{j}",
    )(weights.reshape(2, TAPS, C, C))


def target_kernel(target_hbm, o_hbm, x, out, sems):
    fetch = pltpu.make_async_copy(target_hbm, x, sems.at[0])
    fetch.start()
    fetch.wait()

    @pl.loop(0, 6)
    def _(q):
        for s in range(2):
            out[s, q] = jnp.concatenate([x[q, s], x[q + 6, s]], axis=0).T

    store = pltpu.make_async_copy(out, o_hbm, sems.at[1])
    store.start()
    store.wait()


def turn_target(target):
    return pl.pallas_call(
        target_kernel,
        in_specs=[ANY],
        out_specs=ANY,
        out_shape=jax.ShapeDtypeStruct((2, 6, C, 128), BF16),
        scratch_shapes=[
            pltpu.VMEM((ROWS, 2, COLS, C), BF16),
            pltpu.VMEM((2, 6, C, 128), BF16),
            pltpu.SemaphoreType.DMA((2,)),
        ],
        compiler_params=PARAMS,
        name="turn_target",
    )(target)


def affine(total, square, par_ref, j, scale, offset):
    count = float(LAT * 1024 * WIDTH)
    mean = total / count
    spread = square / count - mean * mean
    factor = lax.rsqrt(spread + 1e-05) * par_ref[:, 2 * j : 2 * j + 1]
    rest = par_ref[:, 2 * j + 1 : 2 * j + 2] - mean * factor
    scale[...] = jnp.broadcast_to(0.5 * factor, scale.shape)
    offset[...] = jnp.broadcast_to(0.5 * rest, offset.shape)


def spread_taps(xs, at, tiles, edge, sides, part):
    rows = PART
    lane = lanes(rows)
    low = lane < 64
    first = (lane == 0) | (lane == 64)
    last = (lane == 63) | (lane == 127)
    tiles, edge = [tile.astype(BF16) for tile in tiles], edge.astype(BF16)
    zero = jnp.zeros((rows, 128), BF16)
    for q in range(-1, 7):
        if q == -1:
            tile = jnp.where(low, edge, roll(tiles[5], 64))
        elif q == 6:
            tile = jnp.where(low, roll(tiles[0], 64), edge)
        else:
            tile = tiles[q]
        side = roll(sides[pl.ds(at, rows), :], -place(q))
        taps = (jnp.where(first, side, roll(tile, 1)), tile, jnp.where(last, side, roll(tile, -1)))
        for k, tap in enumerate(taps):
            if q == -1:
                tap = jnp.where(low & (part == 0), zero, tap)
            elif q == 6:
                tap = jnp.where((~low) & (part == SRC - 1), zero, tap)
            xs[pl.ds(k * C + at, rows), 128 * (q + 1) : 128 * (q + 2)] = tap


def product(wv, xs, n, more=None):
    x = jnp.concatenate([xs[:, n + 128 * i : n + 128 * i + 256] for i in range(3)], axis=0)
    if more is not None:
        x = jnp.concatenate([x, more], axis=1)
    return jnp.dot(wv[...], x, preferred_element_type=F32)


def first_kernel(
    part_ref, par_ref, pick_ref, taps_ref, recv_hbm, w_hbm,
    hid_hbm, out_sums, one, other, out_halo,
    xs, wv, scale, offset, recv, hid, sides, xh, added, sems,
):
    fetches = [
        pltpu.make_async_copy(recv_hbm.at[:, 8 * s : 8 * s + 8], recv.at[s], sems.at[s])
        for s in range(2)
    ]
    weights = pltpu.make_async_copy(w_hbm, wv, sems.at[2])
    for copy in (*fetches, weights):
        copy.start()
    part = part_ref[0]
    lane = lanes(C)

    def act(x, a, o):
        return silu_of_half(x.astype(F32) * a + o)

    def columns(s):
        fetches[s].wait()
        tile = recv[s, :, 7].reshape(C, 128).astype(F32)
        total, square = (
            jnp.sum(jnp.where((lane >= at) & (lane < at + 3), tile, 0.0), axis=1, keepdims=True)
            for at in (SUMS, SUMS + 3)
        )
        affine(total, square, par_ref, 0, scale.at[s], offset.at[s])
        r = (lane & 15) - 2
        unused = lane >= SUMS
        outside = ((part == 0) & (r < 0)) | ((part == SRC - 1) & (r >= ROWS)) | unused
        x = act(jnp.where(unused, 0.0, tile), scale[s], offset[s])
        halo = jnp.where(outside, 0.0, x).astype(BF16)
        sides[s] = jnp.dot(halo, pick_ref[...], preferred_element_type=F32).astype(BF16)
        return halo

    def prepare(s, b):
        at = b * PART if isinstance(b, int) else pl.multiple_of(b * PART, PART)
        a, o = scale[s, pl.ds(at, PART), :], offset[s, pl.ds(at, PART), :]
        tiles = [act(recv[s, b, q], a, o) for q in range(7)]
        spread_taps(xs.at[s], at, tiles[:6], tiles[6], sides.at[s], part)

    for s in range(2):
        added[s] = jnp.broadcast_to(par_ref[:, 5 + s : 6 + s], (C, 128))
    halo = columns(0)

    @pl.loop(0, SRC)
    def _(b):
        prepare(0, b)

    both = jnp.concatenate([halo, columns(1)], axis=1)
    for k in range(3):
        picked = jnp.dot(both, taps_ref[:, 128 * k : 128 * k + 128], preferred_element_type=F32)
        for i in range(3):
            t = 3 * i + k
            xh[C * t : C * (t + 1), :] = roll(picked, -i).astype(BF16)
    weights.wait()
    stores = []

    def put(s, n, value):
        part = hid.at[s, :, n : n + 256]
        for h in range(0, 256, 128):
            hid[s, :, n + h : n + h + 128] = value[:, h : h + 128] + added[s]
        store = pltpu.make_async_copy(
            part, hid_hbm.at[s, :, n : n + 256], sems.at[3 + 3 * s + n // 256]
        )
        store.start()
        stores.append(store)

    put(0, 0, product(wv, xs.at[0], 0))
    for n, blocks in ((256, (0, 1, 2, 3)), (512, (4, 5, 6, 7))):
        put(0, n, product(wv, xs.at[0], n))
        for b in blocks:
            prepare(1, b)
    put(1, 0, product(wv, xs.at[1], 0))
    put(1, 256, product(wv, xs.at[1], 256))
    out = product(wv, xs.at[1], 512, xh[...])
    put(1, 512, out[:, 0:256])
    bias = jnp.where(lane < 32, added[0], added[1])
    out_halo[...] = (out[:, 256:384] + bias).astype(BF16)

    row = jnp.zeros((1, 128), F32)
    low = lanes(128) < 64
    even = part % 2 == 0
    for at in range(0, C, 128):
        for s in range(2):
            pieces = [hid[s, at : at + 128, 128 * q : 128 * (q + 1)] for q in range(6)]
            for k in range(2):
                column = jnp.sum(sum(p * p if k else p for p in pieces), axis=1, keepdims=True)
                own = members(128, at, 64 * k + 32 * s)
                row += jnp.sum(jnp.where(own, column, 0.0), axis=0, keepdims=True)
        start, end = hid.at[:, at : at + 128, 0:128], hid.at[:, at : at + 128, 640:768]
        after = jnp.where(low, roll(end[0], 64), end[1])
        ahead = jnp.where(low, start[0], roll(start[1], 64))
        one[at : at + 128, :] = jnp.where(even, after, ahead).astype(BF16)
        other[at : at + 128, :] = jnp.where(even, ahead, after).astype(BF16)
    out_sums[...] = jnp.broadcast_to(row, out_sums.shape)
    for store in stores:
        store.wait()


def first_conv(part, params, pick, taps, recv, weights):
    tile = jax.ShapeDtypeStruct((C, 128), BF16)
    return pl.pallas_call(
        first_kernel,
        in_specs=[SMEM] + [VMEM] * 3 + [ANY] * 2,
        out_specs=[ANY] + [VMEM] * 4,
        out_shape=[
            jax.ShapeDtypeStruct((2, C, 768), F32),
            jax.ShapeDtypeStruct((128, 128), F32),
            tile, tile, tile,
        ],
        scratch_shapes=[
            pltpu.VMEM((2, 3 * C, 1024), BF16),
            pltpu.VMEM((C, TAPS * C), BF16),
            pltpu.VMEM((2, C, 128), F32),
            pltpu.VMEM((2, C, 128), F32),
            pltpu.VMEM((2, SRC, 8, PART, 128), BF16),
            pltpu.VMEM((2, C, 768), F32),
            pltpu.VMEM((2, C, 128), BF16),
            pltpu.VMEM((TAPS * C, 128), BF16),
            pltpu.VMEM((2, C, 128), F32),
            pltpu.SemaphoreType.DMA((9,)),
        ],
        compiler_params=PARAMS,
        cost_estimate=pl.CostEstimate(
            flops=4 * 768 * C * C * 9, bytes_accessed=20_000_000, transcendentals=0
        ),
        name="first_conv",
    )(part, params, pick, taps, recv, weights)


def second_kernel(
    part_ref, coef_ref, sums_ref, par_ref, pick_ref, near_ref, one_ref, other_ref,
    hid_hbm, w_hbm, recv_hbm, target_hbm,
    noise_hbm, out_ref,
    xs, wv, hid, lat, target, noise_out, sides, scale, offset, added, sems,
):
    weights = pltpu.make_async_copy(w_hbm, wv, sems.at[6])
    fetches, later = [], []
    for s in range(2):
        fetches.append(pltpu.make_async_copy(hid_hbm.at[s], hid.at[s], sems.at[s]))
        tiles = recv_hbm.at[:, 8 * s : 8 * s + 6]
        later.append(pltpu.make_async_copy(tiles, lat.at[s], sems.at[2 + s]))
        later.append(pltpu.make_async_copy(target_hbm.at[s], target.at[s], sems.at[4 + s]))
    for copy in (fetches[0], weights, fetches[1], *later):
        copy.start()
    part = part_ref[0]
    row = jnp.sum(sums_ref[...], axis=0, keepdims=True)
    low = lanes(PART) < 64
    even = part % 2 == 0

    def columns(s):
        total, square = (
            jnp.sum(jnp.where(members(C, 0, base), row, 0.0), axis=1, keepdims=True)
            for base in (32 * s, 64 + 32 * s)
        )
        affine(total, square, par_ref, 1, scale.at[s], offset.at[s])
        halo = silu_of_half(near_ref[...].astype(F32) * scale[s] + offset[s]).astype(BF16)
        sides[s] = jnp.dot(halo, pick_ref[s], preferred_element_type=F32).astype(BF16)
        fetches[s].wait()

    def prepare(s, b):
        at = b * PART if isinstance(b, int) else pl.multiple_of(b * PART, PART)
        rows = pl.ds(at, PART)
        a, o = scale[s, rows, :], offset[s, rows, :]

        def act(x):
            return silu_of_half(x * a + o)

        tiles = [act(hid[s, rows, 128 * q : 128 * (q + 1)]) for q in range(6)]
        below, above = one_ref[rows, :].astype(F32), other_ref[rows, :].astype(F32)
        above, below = jnp.where(even, above, below), jnp.where(even, below, above)
        if s == 0:
            edge = jnp.where(low, above, roll(below, 64))
        else:
            edge = jnp.where(low, roll(above, 64), below)
        spread_taps(xs.at[s], at, tiles, act(edge), sides.at[s], part)

    def finish(s, n, acc):
        keep, gain = coef_ref[2 * s], coef_ref[2 * s + 1]
        out = product(wv, xs.at[s], n)
        for h in range(2):
            q = n // 128 + h
            mine = lat[s, :, q].reshape(C, 128).astype(F32)
            noise = (out[:, 128 * h : 128 * h + 128] + added[...] + mine).astype(BF16)
            center = keep * mine + gain * noise.astype(F32)
            diff = target[s, q].astype(F32) - center
            acc += jnp.sum((diff * diff).reshape(C // 8, 8, 128), axis=0)
            plain = noise.T
            noise_out[s, q] = plain[0:64]
            noise_out[s, q + 6] = plain[64:128]
        return acc

    added[...] = jnp.broadcast_to(par_ref[:, 4:5], added.shape)
    columns(0)

    @pl.loop(0, SRC)
    def _(b):
        prepare(0, b)

    columns(1)
    weights.wait()
    for copy in later:
        copy.wait()
    result = jnp.zeros((1, 128), F32)
    stores = []
    for s in range(2):
        acc = jnp.zeros((8, 128), F32)
        for n, blocks in ((0, (0, 1, 2)), (256, (3, 4, 5)), (512, (6, 7))):
            acc = finish(s, n, acc)
            if s == 0:
                for b in blocks:
                    prepare(1, b)
        store = pltpu.make_async_copy(noise_out.at[s], noise_hbm.at[:, s], sems.at[7 + s])
        store.start()
        stores.append(store)
        value = jnp.sum(acc, axis=(0, 1), keepdims=True)
        result = jnp.where(lanes(1) == s, value, result)
    out_ref[...] = jnp.broadcast_to(result, out_ref.shape)
    for store in stores:
        store.wait()


def second_conv(part, coef, sums, params, pick, tiles, hidden, weights, recv, target):
    return pl.pallas_call(
        second_kernel,
        in_specs=[SMEM, SMEM] + [VMEM] * 6 + [ANY] * 4,
        out_specs=[ANY, VMEM],
        out_shape=[
            jax.ShapeDtypeStruct((ROWS, 2, COLS, C), BF16),
            jax.ShapeDtypeStruct((128, 128), F32),
        ],
        scratch_shapes=[
            pltpu.VMEM((2, 3 * C, 1024), BF16),
            pltpu.VMEM((C, TAPS * C), BF16),
            pltpu.VMEM((2, C, 768), F32),
            pltpu.VMEM((2, SRC, 6, PART, 128), BF16),
            pltpu.VMEM((2, 6, C, 128), BF16),
            pltpu.VMEM((2, ROWS, COLS, C), BF16),
            pltpu.VMEM((2, C, 128), BF16),
            pltpu.VMEM((2, C, 128), F32),
            pltpu.VMEM((2, C, 128), F32),
            pltpu.VMEM((C, 128), F32),
            pltpu.SemaphoreType.DMA((9,)),
        ],
        compiler_params=PARAMS,
        cost_estimate=pl.CostEstimate(
            flops=4 * 768 * C * C * 9, bytes_accessed=20_000_000, transcendentals=0
        ),
        name="second_conv",
    )(part, coef, sums, params, pick, *tiles, hidden, weights, recv, target)


def time_embed(timesteps, time_w1, time_w2):
    half = time_w1.shape[0] // 2
    freqs = jnp.exp(-math.log(10000.0) * jnp.arange(half, dtype=F32) / half)
    angles = timesteps.astype(F32)[:, None] * freqs[None, :]
    features = jnp.concatenate([jnp.cos(angles), jnp.sin(angles)], axis=1)
    hidden = jax.nn.silu(jnp.dot(features, time_w1, precision=lax.Precision.HIGHEST))
    return jnp.dot(hidden, time_w2, precision=lax.Precision.HIGHEST)


def plan(steps):
    frac = steps.astype(F32) / 1000.0
    return jnp.cos((frac + 0.008) / 1.008 * (math.pi / 2.0)) ** 2


def everywhere(rows, axes):
    got = lax.all_to_all(rows.reshape(-1, 1, 128), axes, 0, 0, tiled=True)
    return got.reshape(-1, 128)


def swap_neighbours(one, other, axis):
    size = lax.axis_size(axis)
    pairs = [(i, i ^ 1) for i in range(size)]
    rest = [(i, (i + 1 if i % 2 else i - 1) % size) for i in range(size)]
    return lax.ppermute(one, axis, pairs), lax.ppermute(other, axis, rest)


def swap(array, axis):
    return lax.all_to_all(array, axis, split_axis=0, concat_axis=0, tiled=True)


def after(value, *others):
    return lax.optimization_barrier((value,) + others)[0]


def body(
    latents, next_latents, timesteps, resume_steps, conv_weights, conv_bias,
    norm_gain, norm_shift, time_w1, time_w2,
):
    part = lax.axis_index("ch").astype(jnp.int32).reshape(1)
    first_pick = jnp.asarray(side_lanes(lambda r: 16 + r + 2, lambda r: 64 + r + 2))
    second_pick = jnp.asarray(
        np.stack(
            [
                side_lanes(lambda r: halo_lane(s, 0, r), lambda r: halo_lane(s, 1, r))
                for s in range(2)
            ]
        )
    )
    tap_pick = jnp.asarray(halo_taps())

    cells = latents.transpose(1, 2, 3, 0)
    place = lax.axis_index("lon").astype(jnp.int32).reshape(1)
    sums, *ours = local_sums(place, cells)
    sums = everywhere(sums, "lon")
    theirs = swap_neighbours(*ours, "lon")
    pay = pack(after(cells, ours[0]))
    pay = pack_halo(place, sums, ours, theirs, pay)
    recv = swap(pay, "ch")
    conv_weights, time_w1, following = after((conv_weights, time_w1, next_latents), pay)
    turned = [turn_weights(j, conv_weights) for j in range(2)]
    target = turn_target(following)

    temb = time_embed(timesteps, time_w1, time_w2)
    columns = [
        norm_gain[0], norm_shift[0], norm_gain[1], norm_shift[1], conv_bias[1],
        conv_bias[0] + temb[0], conv_bias[0] + temb[1],
    ]
    params = jnp.pad(jnp.stack(columns, axis=1), ((0, 0), (0, 128 - len(columns))))

    alpha = plan(timesteps)
    prior = plan(timesteps - resume_steps)
    variance = (1.0 - prior) / (1.0 - alpha) * (1.0 - alpha / prior)
    keep = (1.0 - prior) * jnp.sqrt(alpha / (prior * (1.0 - alpha)))
    ratio = jnp.sqrt(prior) / jnp.sqrt(alpha)
    coef = jnp.stack([ratio, keep - ratio * jnp.sqrt(1.0 - alpha)], axis=1).reshape(4)

    recv, turned, target = lax.optimization_barrier((recv, turned, target))
    hidden, sums, one, other, near = first_conv(
        part, params, first_pick, tap_pick, recv, turned[0]
    )
    one, other = swap_neighbours(one, other, "ch")
    sums = everywhere(sums, ("lon", "ch"))
    noise, terms = second_conv(
        part, coef, sums, params, second_pick, (near, one, other),
        hidden, turned[1], recv, target,
    )
    squares = jnp.sum(everywhere(terms, ("lon", "ch")), axis=0)[:2]
    logprob = (
        -squares / (2.0 * variance) / float(LAT * 1024 * C)
        - 0.5 * jnp.log(variance)
        - 0.5 * math.log(2.0 * math.pi)
    )
    return (noise, logprob)


def solution(mesh):
    return jax.shard_map(
        body,
        mesh=mesh,
        in_specs=(
            P(None, None, "lon", "ch"),
            P("ch", None, "lon", None),
            P(), P(), P(), P(), P(), P(), P(), P(),
        ),
        out_specs=(P("ch", None, "lon", None), P()),
        check_vma=False,
    )
```

```python
import functools
import math

import jax
import jax.numpy as jnp
import numpy as np
from jax import lax
from jax.experimental import pallas as pl
from jax.experimental.pallas import tpu as pltpu
from jax.sharding import PartitionSpec as P

GROUPS = 32
C = 640
LAT = 96
ROWS = 12
COLS = 64
SRC = 8
PART = C // SRC
WIDTH = C // GROUPS
TAPS = 9
F32 = jnp.float32
BF16 = jnp.bfloat16
VMEM = pl.BlockSpec(memory_space=pltpu.VMEM)
SMEM = pl.BlockSpec(memory_space=pltpu.SMEM)
ANY = pl.BlockSpec(memory_space=pl.ANY)
CHUNK = 16
LIMIT = 56 * 2**20
SUMS = 96


def roll(x, by):
    by %= 128
    return x if by == 0 else pltpu.roll(x, by, 1)


def place(q):
    return 2 * q + 3


def side_lanes(of_left, of_right):
    out = np.zeros((128, 128), np.float32)
    for q in range(-1, 7):
        p = place(q)
        out[of_left(q), p] = 1
        out[of_left(q + 6), p + 64] = 1
        out[of_right(q), p + 63] = 1
        out[of_right(q + 6), p - 1] = 1
    return out.astype(BF16)


def halo_lane(s, side, row):
    return 32 * s + 16 * side + row + 1


def halo_taps():
    out = np.zeros((256, 3 * 128), np.float32)
    for k in range(3):
        for s in range(2):
            for side in range(2):
                for row in range(-2, 14):
                    source = 128 * s + 16 * (3 * side + k) + row + 2
                    out[source, 128 * k + halo_lane(s, side, row + 1)] = 1
    return out.astype(BF16)


def lanes(rows):
    return lax.broadcasted_iota(jnp.int32, (rows, 128), 1)


def members(rows, first, base):
    chan = lax.broadcasted_iota(jnp.int32, (rows, 128), 0) + first
    low = (lanes(rows) - base) * WIDTH
    return (chan >= low) & (chan < low + WIDTH)


def silu_of_half(h):
    return h + h * jnp.tanh(h)


PARAMS = pltpu.CompilerParams(vmem_limit_bytes=LIMIT)


def sums_kernel(place_ref, cells_hbm, sums_ref, one_ref, other_ref, x, sems):
    half = COLS // 4
    copies = []
    for s in range(2):
        for c in range(4):
            cut = slice(c * half, (c + 1) * half)
            copies.append(
                pltpu.make_async_copy(cells_hbm.at[s, cut], x.at[s, cut], sems.at[4 * s + c])
            )
            copies[-1].start()
    row = jnp.zeros((1, 128), F32)
    for s in range(2):
        total = jnp.zeros((PART, LAT), F32)
        square = jnp.zeros((PART, LAT), F32)
        for c in range(4):
            copies[4 * s + c].wait()

            def add(i, carry):
                total, square = carry
                for j in range(4):
                    v = x[s, c * half + 4 * i + j].astype(F32)
                    total, square = total + v, square + v * v
                return total, square

            total, square = lax.fori_loop(0, half // 4, add, (total, square))
        for k, acc in enumerate((total, square)):
            column = jnp.sum(acc, axis=1, keepdims=True)
            own = members(PART, 0, 64 * k + 32 * s)
            row += jnp.sum(jnp.where(own, column, 0.0), axis=0, keepdims=True)
        even = place_ref[0] % 2 == 0
        first, last = x[s, 0:2].astype(F32), x[s, COLS - 2 : COLS].astype(F32)
        one_ref[s] = jnp.where(even, last, first).astype(BF16)
        other_ref[s] = jnp.where(even, first, last).astype(BF16)
    sums_ref[...] = jnp.broadcast_to(row, sums_ref.shape)


def local_sums(place, cells):
    return pl.pallas_call(
        sums_kernel,
        in_specs=[SMEM, ANY],
        out_specs=[VMEM] * 3,
        out_shape=[
            jax.ShapeDtypeStruct((16, 128), F32),
            jax.ShapeDtypeStruct((2, 2, PART, LAT), BF16),
            jax.ShapeDtypeStruct((2, 2, PART, LAT), BF16),
        ],
        scratch_shapes=[pltpu.VMEM((2, COLS, PART, LAT), BF16), pltpu.SemaphoreType.DMA((8,))],
        compiler_params=PARAMS,
        name="local_sums",
    )(place, cells)


def pack_kernel(cells_hbm, pay_hbm, x, out, taken, turned, sems):
    fetches = [pltpu.make_async_copy(cells_hbm.at[s], x.at[s], sems.at[s]) for s in range(2)]
    for copy in fetches:
        copy.start()
    taken[...] = jnp.zeros_like(taken)
    turned[...] = jnp.zeros_like(turned)
    low = lanes(8) < 64
    stores = [
        pltpu.make_async_copy(out.at[s], pay_hbm.at[:, 8 * s : 8 * s + 7], sems.at[2 + s])
        for s in range(2)
    ]
    fetches[0].wait()

    @pl.loop(0, 2 * PART // CHUNK)
    def _(step):
        s, e = step // (PART // CHUNK), step % (PART // CHUNK)

        @pl.when(step == PART // CHUNK)
        def _():
            stores[0].start()
            fetches[1].wait()

        own = pl.ds(pl.multiple_of(e * CHUNK, CHUNK), CHUNK)
        taken[:, 0:LAT] = x[s, :, own, :].astype(F32).reshape(COLS * CHUNK, LAT)
        for j in range(8):
            pair = [taken[pl.ds(j + 8 * h, COLS, stride=CHUNK), :] for h in range(2)]
            turned[pl.ds(8 + j, LAT, stride=8), :] = jnp.concatenate(pair, axis=0).T[0:LAT, :]

        def tile(upper, lower):
            upper, lower = (turned[8 * (r + 1) : 8 * (r + 2), :] for r in (upper, lower))
            halves = (jnp.where(low, upper, roll(lower, 64)), jnp.where(low, roll(upper, 64), lower))
            return jnp.concatenate(halves, axis=0).astype(BF16)

        for d in range(SRC):
            for q in range(7):
                upper, lower = (d * ROWS + q, d * ROWS + q + 6)
                if q == 6:
                    upper, lower = (d * ROWS - 1, d * ROWS + ROWS)
                out[s, d, q, own, :] = tile(upper, lower)

    stores[1].start()
    for store in stores:
        store.wait()


def pack(cells):
    return pl.pallas_call(
        pack_kernel,
        in_specs=[ANY],
        out_specs=ANY,
        out_shape=jax.ShapeDtypeStruct((SRC, 16, PART, 128), BF16),
        scratch_shapes=[
            pltpu.VMEM((2, COLS, PART, LAT), BF16),
            pltpu.VMEM((2, SRC, 7, PART, 128), BF16),
            pltpu.VMEM((COLS * CHUNK, 128), F32),
            pltpu.VMEM(((LAT + 8) * 8, 128), F32),
            pltpu.SemaphoreType.DMA((4,)),
        ],
        compiler_params=PARAMS,
        cost_estimate=pl.CostEstimate(
            flops=1_000_000_000, bytes_accessed=8_000_000, transcendentals=0
        ),
        name="pack_latents",
    )(cells)


def halo_kernel(
    place_ref, sums_ref, one_ref, other_ref, from_one, from_other, _, pay_hbm, out, sems,
):
    lane = lanes(PART)
    pad = jnp.zeros((PART, 128 - LAT), F32)
    row = jnp.sum(sums_ref[...], axis=0, keepdims=True)

    @pl.loop(0, 2)
    def _(s):
        even = place_ref[0] % 2 == 0
        one, other = one_ref[s].astype(F32), other_ref[s].astype(F32)
        first, last = jnp.where(even, other, one), jnp.where(even, one, other)
        one, other = from_one[s].astype(F32), from_other[s].astype(F32)
        left, right = jnp.where(even, other, one), jnp.where(even, one, other)
        near = [left[0], left[1], first[0], last[1], right[0], right[1]]
        near = [jnp.concatenate([col, pad], axis=1).astype(BF16) for col in near]
        carried = jnp.zeros((PART, 128), F32)
        for k in range(2):
            own = members(PART, 0, 64 * k + 32 * s)
            value = jnp.sum(jnp.where(own, row, 0.0), axis=1, keepdims=True)
            for piece in range(3):
                part = value.astype(BF16).astype(F32)
                carried = jnp.where(lane == SUMS + 3 * k + piece, part, carried)
                value = value - part
        carried = carried.astype(BF16)
        for d in range(SRC):
            halo = carried
            for kind in range(6):
                own = (lane >= 16 * kind) & (lane < 16 * kind + 16)
                halo = jnp.where(own, roll(near[kind], 16 * kind + 2 - d * ROWS), halo)
            out[s, d] = halo
        pltpu.make_async_copy(out.at[s], pay_hbm.at[:, 8 * s + 7], sems.at[s]).start()

    for s in range(2):
        pltpu.make_async_copy(out.at[s], pay_hbm.at[:, 8 * s + 7], sems.at[s]).wait()


def pack_halo(place, sums, ours, theirs, pay):
    return pl.pallas_call(
        halo_kernel,
        in_specs=[SMEM] + [VMEM] * 5 + [ANY],
        out_specs=ANY,
        out_shape=jax.ShapeDtypeStruct((SRC, 16, PART, 128), BF16),
        scratch_shapes=[
            pltpu.VMEM((2, SRC, PART, 128), BF16),
            pltpu.SemaphoreType.DMA((2,)),
        ],
        input_output_aliases={6: 0},
        compiler_params=PARAMS,
        name="pack_halo",
    )(place, sums, *ours, *theirs, pay)


def weight_kernel(j, w_hbm, o_hbm, x, out, sems):
    for t in range(TAPS):
        pltpu.make_async_copy(w_hbm.at[j, t], x.at[t], sems.at[t]).start()

    @pl.loop(0, TAPS)
    def _(t):
        pltpu.make_async_copy(w_hbm.at[j, t], x.at[t], sems.at[t]).wait()
        out[t] = x[t].T
        cut = pl.ds(pl.multiple_of(t * C, 128), C)
        pltpu.make_async_copy(out.at[t], o_hbm.at[:, cut], sems.at[TAPS + t]).start()

    for t in range(TAPS):
        cut = slice(t * C, (t + 1) * C)
        pltpu.make_async_copy(out.at[t], o_hbm.at[:, cut], sems.at[TAPS + t]).wait()


def turn_weights(j, weights):
    return pl.pallas_call(
        functools.partial(weight_kernel, j),
        in_specs=[ANY],
        out_specs=ANY,
        out_shape=jax.ShapeDtypeStruct((C, TAPS * C), BF16),
        scratch_shapes=[
            pltpu.VMEM((TAPS, C, C), BF16),
            pltpu.VMEM((TAPS, C, C), BF16),
            pltpu.SemaphoreType.DMA((2 * TAPS,)),
        ],
        compiler_params=PARAMS,
        cost_estimate=pl.CostEstimate(
            flops=TAPS * 2 * C * C * 256, bytes_accessed=15_000_000, transcendentals=0
        ),
        name=f"turn_weights_{j}",
    )(weights.reshape(2, TAPS, C, C))


def target_kernel(target_hbm, o_hbm, x, out, sems):
    fetch = pltpu.make_async_copy(target_hbm, x, sems.at[0])
    fetch.start()
    fetch.wait()

    @pl.loop(0, 6)
    def _(q):
        for s in range(2):
            out[s, q] = jnp.concatenate([x[q, s], x[q + 6, s]], axis=0).T

    store = pltpu.make_async_copy(out, o_hbm, sems.at[1])
    store.start()
    store.wait()


def turn_target(target):
    return pl.pallas_call(
        target_kernel,
        in_specs=[ANY],
        out_specs=ANY,
        out_shape=jax.ShapeDtypeStruct((2, 6, C, 128), BF16),
        scratch_shapes=[
            pltpu.VMEM((ROWS, 2, COLS, C), BF16),
            pltpu.VMEM((2, 6, C, 128), BF16),
            pltpu.SemaphoreType.DMA((2,)),
        ],
        compiler_params=PARAMS,
        name="turn_target",
    )(target)


def affine(total, square, par_ref, j, scale, offset):
    count = float(LAT * 1024 * WIDTH)
    mean = total / count
    spread = square / count - mean * mean
    factor = lax.rsqrt(spread + 1e-05) * par_ref[:, 2 * j : 2 * j + 1]
    rest = par_ref[:, 2 * j + 1 : 2 * j + 2] - mean * factor
    scale[...] = jnp.broadcast_to(0.5 * factor, scale.shape)
    offset[...] = jnp.broadcast_to(0.5 * rest, offset.shape)


def spread_taps(xs, at, tiles, edge, sides, part):
    rows = PART
    lane = lanes(rows)
    low = lane < 64
    first = (lane == 0) | (lane == 64)
    last = (lane == 63) | (lane == 127)
    tiles, edge = [tile.astype(BF16) for tile in tiles], edge.astype(BF16)
    zero = jnp.zeros((rows, 128), BF16)
    for q in range(-1, 7):
        if q == -1:
            tile = jnp.where(low, edge, roll(tiles[5], 64))
        elif q == 6:
            tile = jnp.where(low, roll(tiles[0], 64), edge)
        else:
            tile = tiles[q]
        side = roll(sides[pl.ds(at, rows), :], -place(q))
        taps = (jnp.where(first, side, roll(tile, 1)), tile, jnp.where(last, side, roll(tile, -1)))
        for k, tap in enumerate(taps):
            if q == -1:
                tap = jnp.where(low & (part == 0), zero, tap)
            elif q == 6:
                tap = jnp.where((~low) & (part == SRC - 1), zero, tap)
            xs[pl.ds(k * C + at, rows), 128 * (q + 1) : 128 * (q + 2)] = tap


def product(wv, xs, n, more=None):
    x = jnp.concatenate([xs[:, n + 128 * i : n + 128 * i + 256] for i in range(3)], axis=0)
    if more is not None:
        x = jnp.concatenate([x, more], axis=1)
    return jnp.dot(wv[...], x, preferred_element_type=F32)


def first_kernel(
    part_ref, par_ref, pick_ref, taps_ref, recv_hbm, w_hbm,
    hid_hbm, out_sums, one, other, out_halo,
    xs, wv, scale, offset, recv, hid, sides, xh, added, sems,
):
    fetches = [
        pltpu.make_async_copy(recv_hbm.at[:, 8 * s : 8 * s + 8], recv.at[s], sems.at[s])
        for s in range(2)
    ]
    weights = pltpu.make_async_copy(w_hbm, wv, sems.at[2])
    for copy in (*fetches, weights):
        copy.start()
    part = part_ref[0]
    lane = lanes(C)

    def act(x, a, o):
        return silu_of_half(x.astype(F32) * a + o)

    def columns(s):
        fetches[s].wait()
        tile = recv[s, :, 7].reshape(C, 128).astype(F32)
        total, square = (
            jnp.sum(jnp.where((lane >= at) & (lane < at + 3), tile, 0.0), axis=1, keepdims=True)
            for at in (SUMS, SUMS + 3)
        )
        affine(total, square, par_ref, 0, scale.at[s], offset.at[s])
        r = (lane & 15) - 2
        unused = lane >= SUMS
        outside = ((part == 0) & (r < 0)) | ((part == SRC - 1) & (r >= ROWS)) | unused
        x = act(jnp.where(unused, 0.0, tile), scale[s], offset[s])
        halo = jnp.where(outside, 0.0, x).astype(BF16)
        sides[s] = jnp.dot(halo, pick_ref[...], preferred_element_type=F32).astype(BF16)
        return halo

    def prepare(s, b):
        at = b * PART if isinstance(b, int) else pl.multiple_of(b * PART, PART)
        a, o = scale[s, pl.ds(at, PART), :], offset[s, pl.ds(at, PART), :]
        tiles = [act(recv[s, b, q], a, o) for q in range(7)]
        spread_taps(xs.at[s], at, tiles[:6], tiles[6], sides.at[s], part)

    for s in range(2):
        added[s] = jnp.broadcast_to(par_ref[:, 5 + s : 6 + s], (C, 128))
    halo = columns(0)

    @pl.loop(0, SRC)
    def _(b):
        prepare(0, b)

    both = jnp.concatenate([halo, columns(1)], axis=1)
    for k in range(3):
        picked = jnp.dot(both, taps_ref[:, 128 * k : 128 * k + 128], preferred_element_type=F32)
        for i in range(3):
            t = 3 * i + k
            xh[C * t : C * (t + 1), :] = roll(picked, -i).astype(BF16)
    weights.wait()
    stores = []

    def put(s, n, value):
        part = hid.at[s, :, n : n + 256]
        for h in range(0, 256, 128):
            hid[s, :, n + h : n + h + 128] = value[:, h : h + 128] + added[s]
        store = pltpu.make_async_copy(
            part, hid_hbm.at[s, :, n : n + 256], sems.at[3 + 3 * s + n // 256]
        )
        store.start()
        stores.append(store)

    put(0, 0, product(wv, xs.at[0], 0))
    for n, blocks in ((256, (0, 1, 2, 3)), (512, (4, 5, 6, 7))):
        put(0, n, product(wv, xs.at[0], n))
        for b in blocks:
            prepare(1, b)
    put(1, 0, product(wv, xs.at[1], 0))
    put(1, 256, product(wv, xs.at[1], 256))
    out = product(wv, xs.at[1], 512, xh[...])
    put(1, 512, out[:, 0:256])
    bias = jnp.where(lane < 32, added[0], added[1])
    out_halo[...] = (out[:, 256:384] + bias).astype(BF16)

    row = jnp.zeros((1, 128), F32)
    low = lanes(128) < 64
    even = part % 2 == 0
    for at in range(0, C, 128):
        for s in range(2):
            pieces = [hid[s, at : at + 128, 128 * q : 128 * (q + 1)] for q in range(6)]
            for k in range(2):
                column = jnp.sum(sum(p * p if k else p for p in pieces), axis=1, keepdims=True)
                own = members(128, at, 64 * k + 32 * s)
                row += jnp.sum(jnp.where(own, column, 0.0), axis=0, keepdims=True)
        start, end = hid.at[:, at : at + 128, 0:128], hid.at[:, at : at + 128, 640:768]
        after = jnp.where(low, roll(end[0], 64), end[1])
        ahead = jnp.where(low, start[0], roll(start[1], 64))
        one[at : at + 128, :] = jnp.where(even, after, ahead).astype(BF16)
        other[at : at + 128, :] = jnp.where(even, ahead, after).astype(BF16)
    out_sums[...] = jnp.broadcast_to(row, out_sums.shape)
    for store in stores:
        store.wait()


def first_conv(part, params, pick, taps, recv, weights):
    tile = jax.ShapeDtypeStruct((C, 128), BF16)
    return pl.pallas_call(
        first_kernel,
        in_specs=[SMEM] + [VMEM] * 3 + [ANY] * 2,
        out_specs=[ANY] + [VMEM] * 4,
        out_shape=[
            jax.ShapeDtypeStruct((2, C, 768), F32),
            jax.ShapeDtypeStruct((128, 128), F32),
            tile, tile, tile,
        ],
        scratch_shapes=[
            pltpu.VMEM((2, 3 * C, 1024), BF16),
            pltpu.VMEM((C, TAPS * C), BF16),
            pltpu.VMEM((2, C, 128), F32),
            pltpu.VMEM((2, C, 128), F32),
            pltpu.VMEM((2, SRC, 8, PART, 128), BF16),
            pltpu.VMEM((2, C, 768), F32),
            pltpu.VMEM((2, C, 128), BF16),
            pltpu.VMEM((TAPS * C, 128), BF16),
            pltpu.VMEM((2, C, 128), F32),
            pltpu.SemaphoreType.DMA((9,)),
        ],
        compiler_params=PARAMS,
        cost_estimate=pl.CostEstimate(
            flops=4 * 768 * C * C * 9, bytes_accessed=20_000_000, transcendentals=0
        ),
        name="first_conv",
    )(part, params, pick, taps, recv, weights)


def second_kernel(
    part_ref, coef_ref, sums_ref, par_ref, pick_ref, near_ref, one_ref, other_ref,
    hid_hbm, w_hbm, recv_hbm, target_hbm,
    noise_hbm, out_ref,
    xs, wv, hid, lat, target, noise_out, sides, scale, offset, added, sems,
):
    weights = pltpu.make_async_copy(w_hbm, wv, sems.at[6])
    fetches, later = [], []
    for s in range(2):
        fetches.append(pltpu.make_async_copy(hid_hbm.at[s], hid.at[s], sems.at[s]))
        tiles = recv_hbm.at[:, 8 * s : 8 * s + 6]
        later.append(pltpu.make_async_copy(tiles, lat.at[s], sems.at[2 + s]))
        later.append(pltpu.make_async_copy(target_hbm.at[s], target.at[s], sems.at[4 + s]))
    for copy in (fetches[0], weights, fetches[1], *later):
        copy.start()
    part = part_ref[0]
    row = jnp.sum(sums_ref[...], axis=0, keepdims=True)
    low = lanes(PART) < 64
    even = part % 2 == 0

    def columns(s):
        total, square = (
            jnp.sum(jnp.where(members(C, 0, base), row, 0.0), axis=1, keepdims=True)
            for base in (32 * s, 64 + 32 * s)
        )
        affine(total, square, par_ref, 1, scale.at[s], offset.at[s])
        halo = silu_of_half(near_ref[...].astype(F32) * scale[s] + offset[s]).astype(BF16)
        sides[s] = jnp.dot(halo, pick_ref[s], preferred_element_type=F32).astype(BF16)
        fetches[s].wait()

    def prepare(s, b):
        at = b * PART if isinstance(b, int) else pl.multiple_of(b * PART, PART)
        rows = pl.ds(at, PART)
        a, o = scale[s, rows, :], offset[s, rows, :]

        def act(x):
            return silu_of_half(x * a + o)

        tiles = [act(hid[s, rows, 128 * q : 128 * (q + 1)]) for q in range(6)]
        below, above = one_ref[rows, :].astype(F32), other_ref[rows, :].astype(F32)
        above, below = jnp.where(even, above, below), jnp.where(even, below, above)
        if s == 0:
            edge = jnp.where(low, above, roll(below, 64))
        else:
            edge = jnp.where(low, roll(above, 64), below)
        spread_taps(xs.at[s], at, tiles, act(edge), sides.at[s], part)

    def finish(s, n, acc):
        keep, gain = coef_ref[2 * s], coef_ref[2 * s + 1]
        out = product(wv, xs.at[s], n)
        for h in range(2):
            q = n // 128 + h
            mine = lat[s, :, q].reshape(C, 128).astype(F32)
            noise = (out[:, 128 * h : 128 * h + 128] + added[...] + mine).astype(BF16)
            center = keep * mine + gain * noise.astype(F32)
            diff = target[s, q].astype(F32) - center
            acc += jnp.sum((diff * diff).reshape(C // 8, 8, 128), axis=0)
            plain = noise.T
            noise_out[s, q] = plain[0:64]
            noise_out[s, q + 6] = plain[64:128]
        return acc

    added[...] = jnp.broadcast_to(par_ref[:, 4:5], added.shape)
    columns(0)

    @pl.loop(0, SRC)
    def _(b):
        prepare(0, b)

    columns(1)
    weights.wait()
    for copy in later:
        copy.wait()
    result = jnp.zeros((1, 128), F32)
    stores = []
    for s in range(2):
        acc = jnp.zeros((8, 128), F32)
        for n, blocks in ((0, (0, 1, 2)), (256, (3, 4, 5)), (512, (6, 7))):
            acc = finish(s, n, acc)
            if s == 0:
                for b in blocks:
                    prepare(1, b)
        store = pltpu.make_async_copy(noise_out.at[s], noise_hbm.at[:, s], sems.at[7 + s])
        store.start()
        stores.append(store)
        value = jnp.sum(acc, axis=(0, 1), keepdims=True)
        result = jnp.where(lanes(1) == s, value, result)
    out_ref[...] = jnp.broadcast_to(result, out_ref.shape)
    for store in stores:
        store.wait()


def second_conv(part, coef, sums, params, pick, tiles, hidden, weights, recv, target):
    return pl.pallas_call(
        second_kernel,
        in_specs=[SMEM, SMEM] + [VMEM] * 6 + [ANY] * 4,
        out_specs=[ANY, VMEM],
        out_shape=[
            jax.ShapeDtypeStruct((ROWS, 2, COLS, C), BF16),
            jax.ShapeDtypeStruct((128, 128), F32),
        ],
        scratch_shapes=[
            pltpu.VMEM((2, 3 * C, 1024), BF16),
            pltpu.VMEM((C, TAPS * C), BF16),
            pltpu.VMEM((2, C, 768), F32),
            pltpu.VMEM((2, SRC, 6, PART, 128), BF16),
            pltpu.VMEM((2, 6, C, 128), BF16),
            pltpu.VMEM((2, ROWS, COLS, C), BF16),
            pltpu.VMEM((2, C, 128), BF16),
            pltpu.VMEM((2, C, 128), F32),
            pltpu.VMEM((2, C, 128), F32),
            pltpu.VMEM((C, 128), F32),
            pltpu.SemaphoreType.DMA((9,)),
        ],
        compiler_params=PARAMS,
        cost_estimate=pl.CostEstimate(
            flops=4 * 768 * C * C * 9, bytes_accessed=20_000_000, transcendentals=0
        ),
        name="second_conv",
    )(part, coef, sums, params, pick, *tiles, hidden, weights, recv, target)


def time_embed(timesteps, time_w1, time_w2):
    half = time_w1.shape[0] // 2
    freqs = jnp.exp(-math.log(10000.0) * jnp.arange(half, dtype=F32) / half)
    angles = timesteps.astype(F32)[:, None] * freqs[None, :]
    features = jnp.concatenate([jnp.cos(angles), jnp.sin(angles)], axis=1)
    hidden = jax.nn.silu(jnp.dot(features, time_w1, precision=lax.Precision.HIGHEST))
    return jnp.dot(hidden, time_w2, precision=lax.Precision.HIGHEST)


def plan(steps):
    frac = steps.astype(F32) / 1000.0
    return jnp.cos((frac + 0.008) / 1.008 * (math.pi / 2.0)) ** 2


def everywhere(rows, axes):
    got = lax.all_to_all(rows.reshape(-1, 1, 128), axes, 0, 0, tiled=True)
    return got.reshape(-1, 128)


def swap_neighbours(one, other, axis):
    size = lax.axis_size(axis)
    pairs = [(i, i ^ 1) for i in range(size)]
    rest = [(i, (i + 1 if i % 2 else i - 1) % size) for i in range(size)]
    return lax.ppermute(one, axis, pairs), lax.ppermute(other, axis, rest)


def swap(array, axis):
    return lax.all_to_all(array, axis, split_axis=0, concat_axis=0, tiled=True)


def after(value, *others):
    return lax.optimization_barrier((value,) + others)[0]


def body(
    latents, next_latents, timesteps, resume_steps, conv_weights, conv_bias,
    norm_gain, norm_shift, time_w1, time_w2,
):
    part = lax.axis_index("ch").astype(jnp.int32).reshape(1)
    first_pick = jnp.asarray(side_lanes(lambda r: 16 + r + 2, lambda r: 64 + r + 2))
    second_pick = jnp.asarray(
        np.stack(
            [
                side_lanes(lambda r: halo_lane(s, 0, r), lambda r: halo_lane(s, 1, r))
                for s in range(2)
            ]
        )
    )
    tap_pick = jnp.asarray(halo_taps())

    cells = latents.transpose(1, 2, 3, 0)
    place = lax.axis_index("lon").astype(jnp.int32).reshape(1)
    sums, *ours = local_sums(place, cells)
    sums = everywhere(sums, "lon")
    theirs = swap_neighbours(*ours, "lon")
    pay = pack(after(cells, ours[0]))
    pay = pack_halo(place, sums, ours, theirs, pay)
    recv = swap(pay, "ch")
    conv_weights, time_w1, following = after((conv_weights, time_w1, next_latents), pay)
    turned = [turn_weights(j, conv_weights) for j in range(2)]
    target = turn_target(following)

    temb = time_embed(timesteps, time_w1, time_w2)
    columns = [
        norm_gain[0], norm_shift[0], norm_gain[1], norm_shift[1], conv_bias[1],
        conv_bias[0] + temb[0], conv_bias[0] + temb[1],
    ]
    params = jnp.pad(jnp.stack(columns, axis=1), ((0, 0), (0, 128 - len(columns))))

    alpha = plan(timesteps)
    prior = plan(timesteps - resume_steps)
    variance = (1.0 - prior) / (1.0 - alpha) * (1.0 - alpha / prior)
    keep = (1.0 - prior) * jnp.sqrt(alpha / (prior * (1.0 - alpha)))
    ratio = jnp.sqrt(prior) / jnp.sqrt(alpha)
    coef = jnp.stack([ratio, keep - ratio * jnp.sqrt(1.0 - alpha)], axis=1).reshape(4)

    recv, turned, target = lax.optimization_barrier((recv, turned, target))
    hidden, sums, one, other, near = first_conv(
        part, params, first_pick, tap_pick, recv, turned[0]
    )
    one, other = swap_neighbours(one, other, "ch")
    sums = everywhere(sums, ("lon", "ch"))
    noise, terms = second_conv(
        part, coef, sums, params, second_pick, (near, one, other),
        hidden, turned[1], recv, target,
    )
    squares = jnp.sum(everywhere(terms, ("lon", "ch")), axis=0)[:2]
    logprob = (
        -squares / (2.0 * variance) / float(LAT * 1024 * C)
        - 0.5 * jnp.log(variance)
        - 0.5 * math.log(2.0 * math.pi)
    )
    return (noise, logprob)


def solution(mesh):
    return jax.shard_map(
        body,
        mesh=mesh,
        in_specs=(
            P(None, None, "lon", "ch"),
            P("ch", None, "lon", None),
            P(), P(), P(), P(), P(), P(), P(), P(),
        ),
        out_specs=(P("ch", None, "lon", None), P()),
        check_vma=False,
    )
```
